128 devices in a mesh: row: 16 (over x, y), col: 8 (over z, core).
Axes of the slice: x: 4, y: 4, z: 4, core: 2. Of those that a mesh axis runs over, the one named last changes fastest.
Arguments:
- atom_single: bfloat16 [16384, 128], P(('row', 'col')), may hold values from -6 to 6
- atom_token: int32 [16384], P(('row', 'col')), may hold values from 0 to 1023, as said below
- token_single: bfloat16 [1024, 768], replicated, may hold values from -6 to 6
- token_mask: int32 [1024], replicated, may hold values 0 or 1
- pair: bfloat16 [1024, 1024, 128], P('row', 'col'), may hold values from -6 to 6
- atom_proj: bfloat16 [128, 768], replicated, may hold values from -0.5 to 0.5
- pool_gain: float32 [768], replicated, may hold values from 0.25 to 1.75
- w_query: bfloat16 [768, 768], replicated, may hold values from -0.21875 to 0.21875
- w_key: bfloat16 [768, 768], replicated, may hold values from -0.21875 to 0.21875
- w_value: bfloat16 [768, 768], replicated, may hold values from -0.21875 to 0.21875
- w_gate: bfloat16 [768, 768], replicated, may hold values from -0.21875 to 0.21875
- w_out: bfloat16 [768, 768], replicated, may hold values from -0.21875 to 0.21875
- pair_proj: float32 [128, 16], replicated
- w_swiglu: bfloat16 [768, 3072], replicated, may hold values from -0.21875 to 0.21875
- w_down: bfloat16 [1536, 768], replicated, may hold values from -0.15625 to 0.15625
- cond_proj: bfloat16 [768, 128], replicated, may hold values from -0.21875 to 0.21875
- atom_swiglu: bfloat16 [128, 512], replicated, may hold values from -0.5 to 0.5
- atom_down: bfloat16 [256, 128], replicated, may hold values from -0.375 to 0.375
Outputs:
- tokens_out: bfloat16 [1024, 768], P('row')
- atoms_out: bfloat16 [16384, 128], P(('row', 'col'))
The draws below stay inside these ranges and needn't reach their ends.
Inputs may be any that keep to these rules, and one draw needn't show every extreme that they name: atom_token never falls along the atoms, every token has at least one atom, and the k-th aligned block of 64 tokens owns exactly the k-th aligned block of 1024 atoms.
All inputs are finite; a program needn't handle non-finite values.
Results may differ from the reference program's by a relative error of at most 0.018.
Values may be sent and summed in bfloat16 or wider, within the bound.
A program may use at most 768 MiB of HBM per device.

```python
import jax
import jax.numpy as jnp
from jax import lax

D = 768
HEADS = 16
C_ATOM = 128
C_PAIR = 128
FF_TOK = 1536
FF_ATOM = 256
TOK_ROW = 64
HEAD = 48
TOKENS = 1024
ATOMS = 16384


def draw_atom_token(key, part):
    key = jax.random.fold_in(key, 1)
    block_count = TOKENS // TOK_ROW
    per_block = ATOMS // block_count
    extra = jax.random.randint(key, (block_count, per_block - TOK_ROW), 0, TOK_ROW).astype(jnp.int32)
    every = jnp.broadcast_to(jnp.arange(TOK_ROW, dtype=jnp.int32)[None, :], (block_count, TOK_ROW))
    local = jnp.sort(jnp.concatenate([every, extra], axis=1), axis=1)
    offsets = (jnp.arange(block_count, dtype=jnp.int32) * TOK_ROW)[:, None]
    return (local + offsets).reshape(ATOMS).astype(jnp.int32)


def draw_pair_proj(key, part):
    key = jax.random.fold_in(key, 2)
    first = jax.random.fold_in(key, 0)
    base = jax.random.normal(first, (C_PAIR, HEADS), jnp.float32) * C_PAIR ** (-0.5)
    return base * 1.5


def touch_ends(drawn, stream_key, least, high):
    place = [jax.random.randint(jax.random.fold_in(stream_key, axis), (), 0, length) for axis, length in enumerate(drawn.shape)]
    main_axis = drawn.shape.index(max(drawn.shape))
    beside = place[:main_axis] + [(place[main_axis] + 1) % drawn.shape[main_axis]] + place[main_axis + 1:]
    return drawn.at[tuple(place)].set(least).at[tuple(beside)].set(high)


def steps_of(rng, shape, shards, smallest, high):
    gain, own = 1.0, jax.random.fold_in(rng, 6)
    for axis_at, shards_of in shards:
        draws = jnp.exp(jax.random.uniform(jax.random.fold_in(own, axis_at), (shards_of,), jnp.float32, smallest / len(shards), high / len(shards)))
        gain = gain * jnp.repeat(draws, shape[axis_at] // shards_of).reshape([-1 if axis == axis_at else 1 for axis in range(len(shape))])
    return gain


def scatter_about(stream_key, shape, scale, bound, cuts=(), kind=jnp.bfloat16):
    drawn = scale * jax.random.normal(stream_key, shape, jnp.float32)
    if cuts:
        drawn = drawn * steps_of(stream_key, shape, cuts, -0.22, 0.18)
    return jnp.clip(drawn, -bound, bound).astype(kind)


def setup_inputs(seed: int = 0) -> dict:
    keys = jax.random.split(jax.random.key(seed), 19)
    return {
        "atom_single": scatter_about(keys[0], (ATOMS, C_ATOM), 1.0, 6.0, ((0, 128),)),
        "atom_token": draw_atom_token(jax.random.fold_in(keys[18], 71), 0),
        "token_single": scatter_about(keys[2], (TOKENS, D), 1.0, 6.0),
        "token_mask": touch_ends((jax.random.randint(keys[3], (TOKENS,), 0, 8) < 7).astype(jnp.int32), jax.random.fold_in(keys[3], 1), 0, 1),
        "pair": scatter_about(keys[4], (TOKENS, TOKENS, C_PAIR), 1.0, 6.0, ((0, 16), (1, 8))),
        "atom_proj": scatter_about(keys[5], (C_ATOM, D), C_ATOM ** -0.5, 0.5),
        "pool_gain": jnp.clip(1.0 + 0.15 * jax.random.normal(keys[6], (D,), jnp.float32), 0.25, 1.75),
        "w_query": scatter_about(keys[7], (D, D), D ** -0.5, 0.21875),
        "w_key": scatter_about(keys[8], (D, D), D ** -0.5, 0.21875),
        "w_value": scatter_about(keys[9], (D, D), D ** -0.5, 0.21875),
        "w_gate": scatter_about(keys[10], (D, D), D ** -0.5, 0.21875),
        "w_out": scatter_about(keys[11], (D, D), D ** -0.5, 0.21875),
        "pair_proj": draw_pair_proj(jax.random.fold_in(keys[18], 71), 0),
        "w_swiglu": scatter_about(keys[13], (D, 2 * FF_TOK), D ** -0.5, 0.21875),
        "w_down": scatter_about(keys[14], (FF_TOK, D), FF_TOK ** -0.5, 0.15625),
        "cond_proj": scatter_about(keys[15], (D, C_ATOM), D ** -0.5, 0.21875),
        "atom_swiglu": scatter_about(keys[16], (C_ATOM, 2 * FF_ATOM), C_ATOM ** -0.5, 0.5),
        "atom_down": scatter_about(keys[17], (FF_ATOM, C_ATOM), FF_ATOM ** -0.5, 0.375),
    }


def layer_norm(values):
    mean = lax.optimization_barrier(jnp.mean(values, axis=-1, keepdims=True))
    centered = values - mean
    var = lax.optimization_barrier(jnp.mean(centered * centered, axis=-1, keepdims=True))
    return centered / jnp.sqrt(var + 1e-05)

def swiglu(inputs, w_both, w_back, width):
    both = jnp.dot(inputs, w_both, preferred_element_type=jnp.float32)
    mid = (jax.nn.silu(both[:, :width]) * both[:, width:]).astype(jnp.bfloat16)
    return jnp.dot(mid, w_back, preferred_element_type=jnp.float32)

def reference(atom_single, atom_token, token_single, token_mask, pair, atom_proj, pool_gain, w_query, w_key, w_value, w_gate, w_out, pair_proj, w_swiglu, w_down, cond_proj, atom_swiglu, atom_down):
    hidden = jax.nn.relu(jnp.dot(atom_single, atom_proj, preferred_element_type=jnp.float32)).astype(jnp.bfloat16)
    pooled = jax.ops.segment_sum(hidden.astype(jnp.float32), atom_token, num_segments=TOKENS)
    act = (layer_norm(pooled) * pool_gain + token_single.astype(jnp.float32)).astype(jnp.bfloat16)
    normed = layer_norm(act.astype(jnp.float32)).astype(jnp.bfloat16)
    query = jnp.dot(normed, w_query, preferred_element_type=jnp.float32).astype(jnp.bfloat16)
    key = jnp.dot(normed, w_key, preferred_element_type=jnp.float32).astype(jnp.bfloat16)
    value = jnp.dot(normed, w_value, preferred_element_type=jnp.float32).astype(jnp.bfloat16)
    gate = jax.nn.sigmoid(jnp.dot(normed, w_gate, preferred_element_type=jnp.float32))
    key_heads = key.reshape(TOKENS, HEADS, HEAD)
    value_heads = value.astype(jnp.float32).reshape(TOKENS, HEADS, HEAD)
    masking = jnp.where(token_mask == 1, 0.0, -1000000000.0).astype(jnp.float32)
    scale = 1.0 / HEAD ** 0.5

    def attend(blocks):
        pair_block, query_block = blocks
        bias = jnp.einsum('ijc,ch->hij', layer_norm(pair_block.astype(jnp.float32)), pair_proj, precision=lax.Precision.HIGHEST)
        query_heads = query_block.reshape(-1, HEADS, HEAD)
        scores = jnp.einsum('ihd,jhd->hij', query_heads, key_heads, preferred_element_type=jnp.float32) * scale + bias + masking[None, None, :]
        weights = jax.nn.softmax(scores, axis=-1)
        attended = jnp.einsum('hij,jhd->ihd', weights, value_heads, precision=lax.Precision.HIGHEST)
        return attended.reshape(-1, HEADS * HEAD)
    blocks_count = TOKENS // TOK_ROW
    attended = lax.map(attend, (pair.reshape(blocks_count, TOK_ROW, TOKENS, C_PAIR), query.reshape(blocks_count, TOK_ROW, D)))
    attended = attended.reshape(TOKENS, D)
    gated = (gate * attended).astype(jnp.bfloat16)
    updated = (act.astype(jnp.float32) + jnp.dot(gated, w_out, preferred_element_type=jnp.float32)).astype(jnp.bfloat16)
    updated_norm = layer_norm(updated.astype(jnp.float32)).astype(jnp.bfloat16)
    tokens_out = (updated.astype(jnp.float32) + swiglu(updated_norm, w_swiglu, w_down, FF_TOK)).astype(jnp.bfloat16)
    cond = jnp.dot(layer_norm(tokens_out.astype(jnp.float32)).astype(jnp.bfloat16), cond_proj, preferred_element_type=jnp.float32).astype(jnp.bfloat16)
    resid = atom_single.astype(jnp.float32) + jnp.take(cond, atom_token, axis=0).astype(jnp.float32)
    atom_norm = layer_norm(resid).astype(jnp.bfloat16)
    atoms_out = (resid + swiglu(atom_norm, atom_swiglu, atom_down, FF_ATOM)).astype(jnp.bfloat16)
    return (tokens_out, atoms_out)
```

```python
import jax
import jax.numpy as jnp
from jax import lax
from jax.experimental import pallas as pl
from jax.experimental.pallas import tpu as pltpu
from jax.sharding import PartitionSpec as P

MESH = pl.DeviceIdType.MESH
F32 = jnp.float32
BF16 = jnp.bfloat16

D = 768
HEADS = 16
HEAD = 48
FF_TOK = 1536
FF_ATOM = 256
ROWS = 64
KEYS = 128
COLS = 8
OWN = ROWS // COLS
PAIR_STEP = 8
PAIR_CHUNKS = 4

NT = (((1,), (1,)), ((), ()))


def norm(values):
    mean = jnp.mean(values, axis=-1, keepdims=True)
    centered = values - mean
    var = jnp.mean(centered * centered, axis=-1, keepdims=True)
    return centered * lax.rsqrt(var + 1e-05)


def dot(a, b):
    return jnp.dot(a, b, preferred_element_type=F32)


def kernel(
    atom_hbm,
    ids_hbm,
    single_hbm,
    mask_hbm,
    pair_hbm,
    aproj_hbm,
    gain_hbm,
    wq_hbm,
    wk_hbm,
    wv_hbm,
    wg_hbm,
    wo_hbm,
    pproj_hbm,
    wsw_hbm,
    wdn_hbm,
    cproj_hbm,
    asw_hbm,
    adn_hbm,
    out_tok,
    out_atom,
    packed,
    ids,
    single,
    mask,
    pair,
    aproj,
    gain,
    wq,
    wk,
    wv,
    wg,
    wo,
    pproj,
    wsw,
    wdn,
    cproj,
    asw,
    adn,
    bias,
    projs,
    expand,
    abuf,
    act_ref,
    normed_ref,
    nsend,
    kbuf,
    psend,
    rbuf,
    obuf,
    lsem,
    psem,
    send1,
    recv1,
    send2,
    recv2,
    send3,
    recv3,
    send4,
    recv4,
):
    r = lax.axis_index("row")
    c = lax.axis_index("col")
    x, y = lax.div(r, 4), lax.rem(r, 4)
    z, core = lax.div(c, 2), lax.rem(c, 2)
    turn = lax.rem(z - x + 4, 4)

    targets = []
    for step in range(2):
        dx = core + 2 * step
        tx = lax.rem(x + dx, 4)
        ty = lax.rem(y + dx + turn, 4)
        targets.append((tx * 4 + ty, lax.div(r, 2)))
    sources = []
    for block in range(2):
        sx = z
        sy = 2 * core + block
        dx = lax.rem(x - sx + 4, 4)
        sturn = lax.rem(y - sy - dx + 8, 4)
        sz = lax.rem(sx + sturn, 4)
        sources.append((sx * 4 + sy, sz * 2 + lax.rem(dx, 2)))
    own_keys = jnp.logical_and(targets[0][0] == r, targets[0][1] == c)

    barrier = pltpu.get_barrier_semaphore()
    peers = [lax.rem(c + k, COLS) for k in range(COLS)]
    for k in range(1, COLS):
        pl.semaphore_signal(barrier, inc=1, device_id=(r, peers[k]), device_id_type=MESH)
    for block in range(2):
        source_self = jnp.logical_and(sources[block][0] == r, sources[block][1] == c)

        @pl.when(jnp.logical_not(source_self))
        def _():
            pl.semaphore_signal(barrier, inc=1, device_id=sources[block], device_id_type=MESH)

    local = {}

    def fetch(name, index, src, dst):
        copy = pltpu.make_async_copy(src, dst, lsem.at[index])
        copy.start()
        local[name] = copy

    fetch("atom", 0, atom_hbm, packed.at[pl.ds(0, 128), :])
    fetch("ids", 1, ids_hbm, ids)
    fetch("aproj", 2, aproj_hbm, aproj)
    fetch("pproj", 3, pproj_hbm, pproj)
    pair_copies = []
    span = ROWS // PAIR_CHUNKS
    for chunk in range(PAIR_CHUNKS):
        part = pl.ds(chunk * span, span)
        copy = pltpu.make_async_copy(pair_hbm.at[part], pair.at[part], psem.at[chunk])
        copy.start()
        pair_copies.append(copy)
    fetch("single", 4, single_hbm.at[pl.ds(pl.multiple_of(r * ROWS, ROWS), ROWS), :], single)
    fetch("gain", 5, gain_hbm, gain)
    fetch("mask", 6, mask_hbm, mask)
    fetch("wq", 7, wq_hbm, wq)
    fetch("wk", 8, wk_hbm, wk)
    fetch("wv", 9, wv_hbm, wv)
    fetch("wg", 10, wg_hbm, wg)
    fetch("wo", 11, wo_hbm, wo)
    fetch("wsw", 12, wsw_hbm, wsw)
    fetch("wdn", 13, wdn_hbm, wdn)
    fetch("cproj", 14, cproj_hbm, cproj)
    fetch("asw", 15, asw_hbm, asw)
    fetch("adn", 16, adn_hbm, adn)

    local["ids"].wait()
    own_ids = (ids[...] - r * ROWS).astype(F32)
    packed[pl.ds(128, 16), :] = jnp.broadcast_to(own_ids, (16, 128)).astype(BF16)
    local["atom"].wait()
    pl.semaphore_wait(barrier, 9 - own_keys.astype(jnp.int32))

    sends1 = []
    for k in range(1, COLS):
        copy = pltpu.make_async_remote_copy(
            src_ref=packed,
            dst_ref=abuf.at[k],
            send_sem=send1.at[k],
            recv_sem=recv1.at[k],
            device_id=(r, peers[k]),
            device_id_type=MESH,
        )
        copy.start()
        sends1.append(copy)

    token_iota = lax.broadcasted_iota(jnp.int32, (ROWS, 128), 0).astype(F32)

    def pooled_of(atoms, id_row):
        hidden = jnp.maximum(dot(atoms, aproj[...]), 0.0).astype(BF16)
        onehot = jnp.where(token_iota == id_row, 1.0, 0.0).astype(BF16)
        return dot(onehot, hidden)

    local["pproj"].wait()
    proj_t = jnp.transpose(pproj[...])
    high = proj_t.astype(BF16)
    projs[pl.ds(0, 16), :] = high
    projs[pl.ds(16, 16), :] = (proj_t - high.astype(F32)).astype(BF16)
    lane = lax.broadcasted_iota(jnp.int32, (128, D), 1)
    line = lax.broadcasted_iota(jnp.int32, (128, D), 0)
    line = jnp.where(line >= HEADS, line - HEADS, line) * HEAD
    inside = jnp.logical_and(lane >= line, lane < line + HEAD)
    expand[...] = jnp.where(inside, 1.0, 0.0).astype(BF16)

    def pair_bias(group, carry):
        tile = pair[pl.ds(group * PAIR_STEP, PAIR_STEP)]
        rows = norm(tile.astype(F32).reshape(PAIR_STEP * KEYS, 128)).astype(BF16)
        both = lax.dot_general(projs[...], rows, NT, preferred_element_type=F32)
        summed = both[:HEADS] + both[HEADS:]
        for i in range(PAIR_STEP):
            bias[pl.ds(group * PAIR_STEP + i, HEADS, stride=ROWS), :] = summed[
                :, i * KEYS : (i + 1) * KEYS
            ]
        return carry

    groups = ROWS // PAIR_STEP
    first = groups // 2
    for copy in pair_copies[: PAIR_CHUNKS // 2]:
        copy.wait()
    lax.fori_loop(0, first, pair_bias, 0)

    local["aproj"].wait()
    pooled = pooled_of(packed[pl.ds(0, 128), :], own_ids)
    for k in range(1, COLS):
        sends1[k - 1].wait_recv()
        pooled += pooled_of(abuf[k, :128, :], abuf[k, 128:144, :].astype(F32)[:1, :])

    local["single"].wait()
    local["gain"].wait()
    act = (norm(pooled) * gain[...] + single[...].astype(F32)).astype(BF16).astype(F32)
    normed = norm(act).astype(BF16)
    nsend[...] = normed

    slot = lax.rem(r, 2)
    sends2 = []
    for step in range(2):
        copy = pltpu.make_async_remote_copy(
            src_ref=nsend,
            dst_ref=kbuf.at[slot],
            send_sem=send2.at[step],
            recv_sem=recv2.at[slot],
            device_id=targets[step],
            device_id_type=MESH,
        )
        sends2.append(copy)

    @pl.when(jnp.logical_not(own_keys))
    def _():
        sends2[0].start()

    sends2[1].start()

    @pl.when(own_keys)
    def _():
        kbuf[slot] = nsend[...]

    act_ref[...] = act
    normed_ref[...] = normed.astype(F32)
    local["wq"].wait()
    query = dot(normed, wq[...]).astype(BF16)
    own_rows = pl.ds(pl.multiple_of(c * OWN, OWN), OWN)
    local["wg"].wait()
    gate = jax.nn.sigmoid(dot(normed_ref[own_rows, :].astype(BF16), wg[...]))
    for copy in pair_copies[PAIR_CHUNKS // 2 :]:
        copy.wait()
    lax.fori_loop(first, groups, pair_bias, 0)
    local["mask"].wait()
    masking = jnp.where(mask[pl.ds(c, 1), :] == 1, 0.0, -1000000000.0).astype(F32)
    local["wk"].wait()
    local["wv"].wait()

    for block in range(2):
        own_block = jnp.logical_and(own_keys, slot == block)

        @pl.when(jnp.logical_not(own_block))
        def _():
            pltpu.make_async_remote_copy(
                src_ref=nsend,
                dst_ref=kbuf.at[block],
                send_sem=send2.at[0],
                recv_sem=recv2.at[block],
                device_id=targets[0],
                device_id_type=MESH,
            ).wait_recv()

    keys_in = kbuf[...].reshape(KEYS, D)
    key = dot(keys_in, wk[...]).astype(BF16)
    value = dot(keys_in, wv[...]).astype(BF16)

    lanes = lax.broadcasted_iota(jnp.int32, (1, 128), 1)
    stats = jnp.zeros((ROWS, 128), F32)
    parts = [None] * 6
    for h in range(HEADS):
        start, stop = h * HEAD, h * HEAD + HEAD
        tiles = range(start // 128, (stop - 1) // 128 + 1)
        score = None
        masks = {}
        for t in tiles:
            inside = jnp.logical_and(lanes >= start - t * 128, lanes < stop - t * 128)
            masks[t] = inside
            q_tile = jnp.where(inside, query[:, t * 128 : t * 128 + 128], 0.0).astype(BF16)
            term = lax.dot_general(
                q_tile, key[:, t * 128 : t * 128 + 128], NT, preferred_element_type=F32
            )
            score = term if score is None else score + term
        score = score * (1.0 / HEAD**0.5) + bias[pl.ds(h * ROWS, ROWS), :] + masking
        top = jnp.max(score, axis=-1, keepdims=True)
        expo = jnp.exp(score - top)
        total = jnp.sum(expo, axis=-1, keepdims=True)
        expo = expo.astype(BF16)
        for t in tiles:
            part = dot(expo, value[:, t * 128 : t * 128 + 128])
            part = jnp.where(masks[t], part, 0.0)
            parts[t] = part if parts[t] is None else parts[t] + part
        top_lanes = (lanes == h) | (lanes == h + 16) | (lanes == h + 32)
        total_lanes = (lanes == h + 48) | (lanes == h + 64)
        stats = jnp.where(top_lanes, top, stats)
        stats = jnp.where(total_lanes, total, stats)

    piece0 = stats.astype(BF16).astype(F32)
    rest = stats - piece0
    piece1 = rest.astype(BF16).astype(F32)
    piece2 = (rest - piece1).astype(BF16).astype(F32)
    use0 = (lanes < 16) | ((lanes >= 48) & (lanes < 64))
    use1 = ((lanes >= 16) & (lanes < 32)) | (lanes >= 64)
    coded = jnp.where(use0, piece0, jnp.where(use1, piece1, piece2))

    def chunked(top_half, bottom_half):
        both = jnp.concatenate(
            [top_half.reshape(COLS, OWN, 128), bottom_half.reshape(COLS, OWN, 128)], axis=1
        )
        return both.reshape(2 * ROWS, 128).astype(BF16)

    for t in range(3):
        psend[:, pl.ds(t * 128, 128)] = chunked(parts[t], parts[t + 3])
    psend[:, pl.ds(384, 128)] = chunked(coded, jnp.zeros_like(coded))

    sends3 = []
    for k in range(1, COLS):
        copy = pltpu.make_async_remote_copy(
            src_ref=psend.at[pl.ds(pl.multiple_of(peers[k] * 16, 16), 16), :],
            dst_ref=rbuf.at[k],
            send_sem=send3.at[k],
            recv_sem=recv3.at[k],
            device_id=(r, peers[k]),
            device_id_type=MESH,
        )
        copy.start()
        sends3.append(copy)
    own_act = act_ref[own_rows, :]
    for name in ("wo", "wsw", "wdn", "cproj", "asw", "adn"):
        local[name].wait()
    got = [psend[pl.ds(pl.multiple_of(c * 16, 16), 16), :].astype(F32)]
    for k in range(1, COLS):
        sends3[k - 1].wait_recv()
        got.append(rbuf[k].astype(F32))

    tops, totals = [], []
    for piece in got:
        line = piece[:OWN, 384:512]
        tops.append(line + pltpu.roll(line, 112, 1) + pltpu.roll(line, 96, 1))
        totals.append(pltpu.roll(line, 80, 1) + pltpu.roll(line, 64, 1))
    peak = tops[0]
    for top in tops[1:]:
        peak = jnp.maximum(peak, top)
    scales = [jnp.exp(top - peak) for top in tops]
    whole = scales[0] * totals[0]
    for scale, total in zip(scales[1:], totals[1:]):
        whole += scale * total
    coeffs = []
    for scale in scales:
        ratio = jnp.where(lanes < HEADS, scale / whole, 0.0)
        upper = ratio.astype(BF16).astype(F32)
        coeffs.append(upper + pltpu.roll(ratio - upper, 16, 1))
    spread = dot(jnp.concatenate(coeffs, axis=0).astype(BF16), expand[...])
    left = jnp.zeros((OWN, 384), F32)
    right = jnp.zeros((OWN, 384), F32)
    for s, piece in enumerate(got):
        left += spread[s * OWN : (s + 1) * OWN, :384] * piece[:OWN, :384]
        right += spread[s * OWN : (s + 1) * OWN, 384:] * piece[OWN:, :384]
    attended = jnp.concatenate([left, right], axis=1)

    gated = (gate * attended).astype(BF16)
    updated = (own_act + dot(gated, wo[...])).astype(BF16).astype(F32)
    updated_norm = norm(updated).astype(BF16)
    finished = updated
    width = 512
    down = jnp.zeros((OWN, D), F32)
    for step in range(FF_TOK // width):
        g = dot(updated_norm, wsw[:, step * width : (step + 1) * width])
        u = dot(updated_norm, wsw[:, FF_TOK + step * width : FF_TOK + (step + 1) * width])
        mid = (jax.nn.silu(g) * u).astype(BF16)
        down += dot(mid, wdn[step * width : (step + 1) * width, :])
    finished = (updated + down).astype(BF16).astype(F32)
    cond = dot(norm(finished).astype(BF16), cproj[...])
    block = jnp.concatenate(
        [
            jnp.concatenate([finished[:, :384], finished[:, 384:]], axis=0),
            jnp.concatenate([cond, jnp.zeros_like(cond)], axis=0),
        ],
        axis=1,
    ).astype(BF16)
    obuf[c] = block

    sends4 = []
    for k in range(1, COLS):
        copy = pltpu.make_async_remote_copy(
            src_ref=obuf.at[c],
            dst_ref=obuf.at[c],
            send_sem=send4.at[k],
            recv_sem=recv4.at[c],
            device_id=(r, peers[k]),
            device_id_type=MESH,
        )
        copy.start()
        sends4.append(copy)

    onehot_t = jnp.transpose(jnp.where(token_iota == own_ids, 1.0, 0.0)).astype(BF16)
    atoms = packed[pl.ds(0, 128), :].astype(F32)

    for k in range(1, COLS):
        pltpu.make_async_remote_copy(
            src_ref=obuf.at[peers[k]],
            dst_ref=obuf.at[peers[k]],
            send_sem=send4.at[k],
            recv_sem=recv4.at[peers[k]],
            device_id=(r, peers[k]),
            device_id_type=MESH,
        ).wait_recv()

    full = obuf[...].astype(F32)
    tokens = jnp.concatenate([full[:, :OWN, :384], full[:, OWN:, :384]], axis=2)
    out_tok[...] = tokens.reshape(ROWS, D).astype(BF16)
    conds = full[:, :OWN, 384:512].reshape(ROWS, 128).astype(BF16)
    resid = atoms + dot(onehot_t, conds)
    both = dot(norm(resid).astype(BF16), asw[...])
    mid = (jax.nn.silu(both[:, :FF_ATOM]) * both[:, FF_ATOM:]).astype(BF16)
    out_atom[...] = (resid + dot(mid, adn[...])).astype(BF16)

    for copy in sends1:
        copy.wait_send()

    @pl.when(jnp.logical_not(own_keys))
    def _():
        sends2[0].wait_send()

    sends2[1].wait_send()
    for copy in sends3:
        copy.wait_send()
    for copy in sends4:
        copy.wait_send()


def local_step(
    atom_single,
    atom_token,
    token_single,
    token_mask,
    pair,
    atom_proj,
    pool_gain,
    w_query,
    w_key,
    w_value,
    w_gate,
    w_out,
    pair_proj,
    w_swiglu,
    w_down,
    cond_proj,
    atom_swiglu,
    atom_down,
):
    args = (
        atom_single,
        atom_token.reshape(1, 128),
        token_single,
        token_mask.reshape(COLS, KEYS),
        pair,
        atom_proj,
        pool_gain.reshape(1, D),
        w_query,
        w_key,
        w_value,
        w_gate,
        w_out,
        pair_proj,
        w_swiglu,
        w_down,
        cond_proj,
        atom_swiglu,
        atom_down,
    )
    vmem = pltpu.VMEM
    dma = pltpu.SemaphoreType.DMA
    scratch = [
        vmem((144, 128), BF16),
        vmem((1, 128), jnp.int32),
        vmem((ROWS, D), BF16),
        vmem((COLS, KEYS), jnp.int32),
        vmem((ROWS, KEYS, 128), BF16),
        vmem((128, D), BF16),
        vmem((1, D), F32),
        vmem((D, D), BF16),
        vmem((D, D), BF16),
        vmem((D, D), BF16),
        vmem((D, D), BF16),
        vmem((D, D), BF16),
        vmem((128, HEADS), F32),
        vmem((D, 2 * FF_TOK), BF16),
        vmem((FF_TOK, D), BF16),
        vmem((D, 128), BF16),
        vmem((128, 2 * FF_ATOM), BF16),
        vmem((FF_ATOM, 128), BF16),
        vmem((HEADS * ROWS, KEYS), F32),
        vmem((2 * HEADS, 128), BF16),
        vmem((128, D), BF16),
        vmem((COLS, 144, 128), BF16),
        vmem((ROWS, D), F32),
        vmem((ROWS, D), F32),
        vmem((ROWS, D), BF16),
        vmem((2, ROWS, D), BF16),
        vmem((2 * ROWS, 512), BF16),
        vmem((COLS, 16, 512), BF16),
        vmem((COLS, 16, 512), BF16),
        dma((17,)),
        dma((PAIR_CHUNKS,)),
        dma((COLS,)),
        dma((COLS,)),
        dma((2,)),
        dma((2,)),
        dma((COLS,)),
        dma((COLS,)),
        dma((COLS,)),
        dma((COLS,)),
    ]
    return pl.pallas_call(
        kernel,
        out_shape=(
            jax.ShapeDtypeStruct((ROWS, D), BF16),
            jax.ShapeDtypeStruct((128, 128), BF16),
        ),
        in_specs=[pl.BlockSpec(memory_space=pl.ANY)] * len(args),
        out_specs=(
            pl.BlockSpec(memory_space=pltpu.VMEM),
            pl.BlockSpec(memory_space=pltpu.VMEM),
        ),
        scratch_shapes=scratch,
        compiler_params=pltpu.CompilerParams(
            collective_id=0, has_side_effects=True, vmem_limit_bytes=48 * 1024 * 1024
        ),
        name="step",
    )(*args)


def solution(mesh):
    split = P(("row", "col"), None)
    placed = (
        split,
        P(("row", "col")),
        P(),
        P(),
        P("row", "col", None),
    ) + (P(),) * 13
    return jax.shard_map(
        local_step,
        mesh=mesh,
        in_specs=placed,
        out_specs=(P("row", None), split),
        check_vma=False,
    )
```

```python
import jax
import jax.numpy as jnp
from jax import lax
from jax.experimental import pallas as pl
from jax.experimental.pallas import tpu as pltpu
from jax.sharding import PartitionSpec as P

MESH = pl.DeviceIdType.MESH
F32 = jnp.float32
BF16 = jnp.bfloat16

D = 768
HEADS = 16
HEAD = 48
FF_TOK = 1536
FF_ATOM = 256
ROWS = 64
KEYS = 128
COLS = 8
OWN = ROWS // COLS
PAIR_STEP = 8
PAIR_CHUNKS = 4

NT = (((1,), (1,)), ((), ()))


def norm(values):
    mean = jnp.mean(values, axis=-1, keepdims=True)
    centered = values - mean
    var = jnp.mean(centered * centered, axis=-1, keepdims=True)
    return centered * lax.rsqrt(var + 1e-05)


def dot(a, b):
    return jnp.dot(a, b, preferred_element_type=F32)


def kernel(
    atom_hbm,
    ids_hbm,
    single_hbm,
    mask_hbm,
    pair_hbm,
    aproj_hbm,
    gain_hbm,
    wq_hbm,
    wk_hbm,
    wv_hbm,
    wg_hbm,
    wo_hbm,
    pproj_hbm,
    wsw_hbm,
    wdn_hbm,
    cproj_hbm,
    asw_hbm,
    adn_hbm,
    out_tok,
    out_atom,
    packed,
    ids,
    single,
    mask,
    pair,
    aproj,
    gain,
    wq,
    wk,
    wv,
    wg,
    wo,
    pproj,
    wsw,
    wdn,
    cproj,
    asw,
    adn,
    bias,
    projs,
    expand,
    abuf,
    act_ref,
    normed_ref,
    nsend,
    kbuf,
    psend,
    rbuf,
    obuf,
    lsem,
    psem,
    send1,
    recv1,
    send2,
    recv2,
    send3,
    recv3,
    send4,
    recv4,
):
    r = lax.axis_index("row")
    c = lax.axis_index("col")
    x, y = lax.div(r, 4), lax.rem(r, 4)
    z, core = lax.div(c, 2), lax.rem(c, 2)
    turn = lax.rem(z - x + 4, 4)

    targets = []
    for step in range(2):
        dx = core + 2 * step
        tx = lax.rem(x + dx, 4)
        ty = lax.rem(y + dx + turn, 4)
        targets.append((tx * 4 + ty, lax.div(r, 2)))
    sources = []
    for block in range(2):
        sx = z
        sy = 2 * core + block
        dx = lax.rem(x - sx + 4, 4)
        sturn = lax.rem(y - sy - dx + 8, 4)
        sz = lax.rem(sx + sturn, 4)
        sources.append((sx * 4 + sy, sz * 2 + lax.rem(dx, 2)))
    own_keys = jnp.logical_and(targets[0][0] == r, targets[0][1] == c)

    barrier = pltpu.get_barrier_semaphore()
    peers = [lax.rem(c + k, COLS) for k in range(COLS)]
    for k in range(1, COLS):
        pl.semaphore_signal(barrier, inc=1, device_id=(r, peers[k]), device_id_type=MESH)
    for block in range(2):
        source_self = jnp.logical_and(sources[block][0] == r, sources[block][1] == c)

        @pl.when(jnp.logical_not(source_self))
        def _():
            pl.semaphore_signal(barrier, inc=1, device_id=sources[block], device_id_type=MESH)

    local = {}

    def fetch(name, index, src, dst):
        copy = pltpu.make_async_copy(src, dst, lsem.at[index])
        copy.start()
        local[name] = copy

    fetch("atom", 0, atom_hbm, packed.at[pl.ds(0, 128), :])
    fetch("ids", 1, ids_hbm, ids)
    fetch("aproj", 2, aproj_hbm, aproj)
    fetch("pproj", 3, pproj_hbm, pproj)
    pair_copies = []
    span = ROWS // PAIR_CHUNKS
    for chunk in range(PAIR_CHUNKS):
        part = pl.ds(chunk * span, span)
        copy = pltpu.make_async_copy(pair_hbm.at[part], pair.at[part], psem.at[chunk])
        copy.start()
        pair_copies.append(copy)
    fetch("single", 4, single_hbm.at[pl.ds(pl.multiple_of(r * ROWS, ROWS), ROWS), :], single)
    fetch("gain", 5, gain_hbm, gain)
    fetch("mask", 6, mask_hbm, mask)
    fetch("wq", 7, wq_hbm, wq)
    fetch("wk", 8, wk_hbm, wk)
    fetch("wv", 9, wv_hbm, wv)
    fetch("wg", 10, wg_hbm, wg)
    fetch("wo", 11, wo_hbm, wo)
    fetch("wsw", 12, wsw_hbm, wsw)
    fetch("wdn", 13, wdn_hbm, wdn)
    fetch("cproj", 14, cproj_hbm, cproj)
    fetch("asw", 15, asw_hbm, asw)
    fetch("adn", 16, adn_hbm, adn)

    local["ids"].wait()
    own_ids = (ids[...] - r * ROWS).astype(F32)
    packed[pl.ds(128, 16), :] = jnp.broadcast_to(own_ids, (16, 128)).astype(BF16)
    local["atom"].wait()
    pl.semaphore_wait(barrier, 9 - own_keys.astype(jnp.int32))

    sends1 = []
    for k in range(1, COLS):
        copy = pltpu.make_async_remote_copy(
            src_ref=packed,
            dst_ref=abuf.at[k],
            send_sem=send1.at[k],
            recv_sem=recv1.at[k],
            device_id=(r, peers[k]),
            device_id_type=MESH,
        )
        copy.start()
        sends1.append(copy)

    token_iota = lax.broadcasted_iota(jnp.int32, (ROWS, 128), 0).astype(F32)

    def pooled_of(atoms, id_row):
        hidden = jnp.maximum(dot(atoms, aproj[...]), 0.0).astype(BF16)
        onehot = jnp.where(token_iota == id_row, 1.0, 0.0).astype(BF16)
        return dot(onehot, hidden)

    local["pproj"].wait()
    proj_t = pproj[...]
    high = proj_t.astype(BF16)
    projs[pl.ds(0, 16), :] = high
    projs[pl.ds(16, 16), :] = (proj_t - high.astype(F32)).astype(BF16)
    lane = lax.broadcasted_iota(jnp.int32, (128, D), 1)
    line = lax.broadcasted_iota(jnp.int32, (128, D), 0)
    line = jnp.where(line >= HEADS, line - HEADS, line) * HEAD
    inside = jnp.logical_and(lane >= line, lane < line + HEAD)
    expand[...] = jnp.where(inside, 1.0, 0.0).astype(BF16)

    def pair_bias(group, carry):
        tile = pair[pl.ds(group * PAIR_STEP, PAIR_STEP)]
        rows = norm(tile.astype(F32).reshape(PAIR_STEP * KEYS, 128)).astype(BF16)
        both = lax.dot_general(projs[...], rows, NT, preferred_element_type=F32)
        summed = both[:HEADS] + both[HEADS:]
        for i in range(PAIR_STEP):
            bias[pl.ds(group * PAIR_STEP + i, HEADS, stride=ROWS), :] = summed[
                :, i * KEYS : (i + 1) * KEYS
            ]
        return carry

    groups = ROWS // PAIR_STEP
    first = groups // 2
    for copy in pair_copies[: PAIR_CHUNKS // 2]:
        copy.wait()
    lax.fori_loop(0, first, pair_bias, 0)

    local["aproj"].wait()
    pooled = pooled_of(packed[pl.ds(0, 128), :], own_ids)
    for k in range(1, COLS):
        sends1[k - 1].wait_recv()
        pooled += pooled_of(abuf[k, :128, :], abuf[k, 128:144, :].astype(F32)[:1, :])

    local["single"].wait()
    local["gain"].wait()
    gains = jnp.concatenate([gain[t : t + 1, :] for t in range(D // 128)], axis=1)
    act = (norm(pooled) * gains + single[...].astype(F32)).astype(BF16).astype(F32)
    normed = norm(act).astype(BF16)
    nsend[...] = normed

    slot = lax.rem(r, 2)
    sends2 = []
    for step in range(2):
        copy = pltpu.make_async_remote_copy(
            src_ref=nsend,
            dst_ref=kbuf.at[slot],
            send_sem=send2.at[step],
            recv_sem=recv2.at[slot],
            device_id=targets[step],
            device_id_type=MESH,
        )
        sends2.append(copy)

    @pl.when(jnp.logical_not(own_keys))
    def _():
        sends2[0].start()

    sends2[1].start()

    @pl.when(own_keys)
    def _():
        kbuf[slot] = nsend[...]

    act_ref[...] = act
    normed_ref[...] = normed.astype(F32)
    local["wq"].wait()
    query = dot(normed, wq[...]).astype(BF16)
    own_rows = pl.ds(pl.multiple_of(c * OWN, OWN), OWN)
    local["wg"].wait()
    gate = jax.nn.sigmoid(dot(normed_ref[own_rows, :].astype(BF16), wg[...]))
    for copy in pair_copies[PAIR_CHUNKS // 2 :]:
        copy.wait()
    lax.fori_loop(first, groups, pair_bias, 0)
    local["mask"].wait()
    masking = jnp.where(mask[pl.ds(c, 1), :] == 1, 0.0, -1000000000.0).astype(F32)
    local["wk"].wait()
    local["wv"].wait()

    for block in range(2):
        own_block = jnp.logical_and(own_keys, slot == block)

        @pl.when(jnp.logical_not(own_block))
        def _():
            pltpu.make_async_remote_copy(
                src_ref=nsend,
                dst_ref=kbuf.at[block],
                send_sem=send2.at[0],
                recv_sem=recv2.at[block],
                device_id=targets[0],
                device_id_type=MESH,
            ).wait_recv()

    keys_in = kbuf[...].reshape(KEYS, D)
    key = dot(keys_in, wk[...]).astype(BF16)
    value = dot(keys_in, wv[...]).astype(BF16)

    lanes = lax.broadcasted_iota(jnp.int32, (1, 128), 1)
    stats = jnp.zeros((ROWS, 128), F32)
    parts = [None] * 6
    for h in range(HEADS):
        start, stop = h * HEAD, h * HEAD + HEAD
        tiles = range(start // 128, (stop - 1) // 128 + 1)
        score = None
        masks = {}
        for t in tiles:
            inside = jnp.logical_and(lanes >= start - t * 128, lanes < stop - t * 128)
            masks[t] = inside
            q_tile = jnp.where(inside, query[:, t * 128 : t * 128 + 128], 0.0).astype(BF16)
            term = lax.dot_general(
                q_tile, key[:, t * 128 : t * 128 + 128], NT, preferred_element_type=F32
            )
            score = term if score is None else score + term
        score = score * (1.0 / HEAD**0.5) + bias[pl.ds(h * ROWS, ROWS), :] + masking
        top = jnp.max(score, axis=-1, keepdims=True)
        expo = jnp.exp(score - top)
        total = jnp.sum(expo, axis=-1, keepdims=True)
        expo = expo.astype(BF16)
        for t in tiles:
            part = dot(expo, value[:, t * 128 : t * 128 + 128])
            part = jnp.where(masks[t], part, 0.0)
            parts[t] = part if parts[t] is None else parts[t] + part
        top_lanes = (lanes == h) | (lanes == h + 16) | (lanes == h + 32)
        total_lanes = (lanes == h + 48) | (lanes == h + 64)
        stats = jnp.where(top_lanes, top, stats)
        stats = jnp.where(total_lanes, total, stats)

    piece0 = stats.astype(BF16).astype(F32)
    rest = stats - piece0
    piece1 = rest.astype(BF16).astype(F32)
    piece2 = (rest - piece1).astype(BF16).astype(F32)
    use0 = (lanes < 16) | ((lanes >= 48) & (lanes < 64))
    use1 = ((lanes >= 16) & (lanes < 32)) | (lanes >= 64)
    coded = jnp.where(use0, piece0, jnp.where(use1, piece1, piece2))

    def chunked(top_half, bottom_half):
        both = jnp.concatenate(
            [top_half.reshape(COLS, OWN, 128), bottom_half.reshape(COLS, OWN, 128)], axis=1
        )
        return both.reshape(2 * ROWS, 128).astype(BF16)

    for t in range(3):
        psend[:, pl.ds(t * 128, 128)] = chunked(parts[t], parts[t + 3])
    psend[:, pl.ds(384, 128)] = chunked(coded, jnp.zeros_like(coded))

    sends3 = []
    for k in range(1, COLS):
        copy = pltpu.make_async_remote_copy(
            src_ref=psend.at[pl.ds(pl.multiple_of(peers[k] * 16, 16), 16), :],
            dst_ref=rbuf.at[k],
            send_sem=send3.at[k],
            recv_sem=recv3.at[k],
            device_id=(r, peers[k]),
            device_id_type=MESH,
        )
        copy.start()
        sends3.append(copy)
    own_act = act_ref[own_rows, :]
    for name in ("wo", "wsw", "wdn", "cproj", "asw", "adn"):
        local[name].wait()
    got = [psend[pl.ds(pl.multiple_of(c * 16, 16), 16), :].astype(F32)]
    for k in range(1, COLS):
        sends3[k - 1].wait_recv()
        got.append(rbuf[k].astype(F32))

    tops, totals = [], []
    for piece in got:
        line = piece[:OWN, 384:512]
        tops.append(line + pltpu.roll(line, 112, 1) + pltpu.roll(line, 96, 1))
        totals.append(pltpu.roll(line, 80, 1) + pltpu.roll(line, 64, 1))
    peak = tops[0]
    for top in tops[1:]:
        peak = jnp.maximum(peak, top)
    scales = [jnp.exp(top - peak) for top in tops]
    whole = scales[0] * totals[0]
    for scale, total in zip(scales[1:], totals[1:]):
        whole += scale * total
    coeffs = []
    for scale in scales:
        ratio = jnp.where(lanes < HEADS, scale / whole, 0.0)
        upper = ratio.astype(BF16).astype(F32)
        coeffs.append(upper + pltpu.roll(ratio - upper, 16, 1))
    spread = dot(jnp.concatenate(coeffs, axis=0).astype(BF16), expand[...])
    left = jnp.zeros((OWN, 384), F32)
    right = jnp.zeros((OWN, 384), F32)
    for s, piece in enumerate(got):
        left += spread[s * OWN : (s + 1) * OWN, :384] * piece[:OWN, :384]
        right += spread[s * OWN : (s + 1) * OWN, 384:] * piece[OWN:, :384]
    attended = jnp.concatenate([left, right], axis=1)

    gated = (gate * attended).astype(BF16)
    updated = (own_act + dot(gated, wo[...])).astype(BF16).astype(F32)
    updated_norm = norm(updated).astype(BF16)
    finished = updated
    width = 512
    down = jnp.zeros((OWN, D), F32)
    for step in range(FF_TOK // width):
        g = dot(updated_norm, wsw[:, step * width : (step + 1) * width])
        u = dot(updated_norm, wsw[:, FF_TOK + step * width : FF_TOK + (step + 1) * width])
        mid = (jax.nn.silu(g) * u).astype(BF16)
        down += dot(mid, wdn[step * width : (step + 1) * width, :])
    finished = (updated + down).astype(BF16).astype(F32)
    cond = dot(norm(finished).astype(BF16), cproj[...])
    block = jnp.concatenate(
        [
            jnp.concatenate([finished[:, :384], finished[:, 384:]], axis=0),
            jnp.concatenate([cond, jnp.zeros_like(cond)], axis=0),
        ],
        axis=1,
    ).astype(BF16)
    obuf[c] = block

    sends4 = []
    for k in range(1, COLS):
        copy = pltpu.make_async_remote_copy(
            src_ref=obuf.at[c],
            dst_ref=obuf.at[c],
            send_sem=send4.at[k],
            recv_sem=recv4.at[c],
            device_id=(r, peers[k]),
            device_id_type=MESH,
        )
        copy.start()
        sends4.append(copy)

    onehot_t = jnp.transpose(jnp.where(token_iota == own_ids, 1.0, 0.0)).astype(BF16)
    atoms = packed[pl.ds(0, 128), :].astype(F32)

    for k in range(1, COLS):
        pltpu.make_async_remote_copy(
            src_ref=obuf.at[peers[k]],
            dst_ref=obuf.at[peers[k]],
            send_sem=send4.at[k],
            recv_sem=recv4.at[peers[k]],
            device_id=(r, peers[k]),
            device_id_type=MESH,
        ).wait_recv()

    full = obuf[...].astype(F32)
    tokens = jnp.concatenate([full[:, :OWN, :384], full[:, OWN:, :384]], axis=2)
    out_tok[...] = tokens.reshape(ROWS, D).astype(BF16)
    conds = full[:, :OWN, 384:512].reshape(ROWS, 128).astype(BF16)
    resid = atoms + dot(onehot_t, conds)
    both = dot(norm(resid).astype(BF16), asw[...])
    mid = (jax.nn.silu(both[:, :FF_ATOM]) * both[:, FF_ATOM:]).astype(BF16)
    out_atom[...] = (resid + dot(mid, adn[...])).astype(BF16)

    for copy in sends1:
        copy.wait_send()

    @pl.when(jnp.logical_not(own_keys))
    def _():
        sends2[0].wait_send()

    sends2[1].wait_send()
    for copy in sends3:
        copy.wait_send()
    for copy in sends4:
        copy.wait_send()


def local_step(
    atom_single,
    atom_token,
    token_single,
    token_mask,
    pair,
    atom_proj,
    pool_gain,
    w_query,
    w_key,
    w_value,
    w_gate,
    w_out,
    pair_proj,
    w_swiglu,
    w_down,
    cond_proj,
    atom_swiglu,
    atom_down,
):
    args = (
        atom_single,
        atom_token.reshape(1, 128),
        token_single,
        token_mask.reshape(COLS, KEYS),
        pair,
        atom_proj,
        pool_gain.reshape(D // 128, 128),
        w_query,
        w_key,
        w_value,
        w_gate,
        w_out,
        pair_proj.T,
        w_swiglu,
        w_down,
        cond_proj,
        atom_swiglu,
        atom_down,
    )
    vmem = pltpu.VMEM
    dma = pltpu.SemaphoreType.DMA
    scratch = [
        vmem((144, 128), BF16),
        vmem((1, 128), jnp.int32),
        vmem((ROWS, D), BF16),
        vmem((COLS, KEYS), jnp.int32),
        vmem((ROWS, KEYS, 128), BF16),
        vmem((128, D), BF16),
        vmem((D // 128, 128), F32),
        vmem((D, D), BF16),
        vmem((D, D), BF16),
        vmem((D, D), BF16),
        vmem((D, D), BF16),
        vmem((D, D), BF16),
        vmem((HEADS, 128), F32),
        vmem((D, 2 * FF_TOK), BF16),
        vmem((FF_TOK, D), BF16),
        vmem((D, 128), BF16),
        vmem((128, 2 * FF_ATOM), BF16),
        vmem((FF_ATOM, 128), BF16),
        vmem((HEADS * ROWS, KEYS), F32),
        vmem((2 * HEADS, 128), BF16),
        vmem((128, D), BF16),
        vmem((COLS, 144, 128), BF16),
        vmem((ROWS, D), F32),
        vmem((ROWS, D), F32),
        vmem((ROWS, D), BF16),
        vmem((2, ROWS, D), BF16),
        vmem((2 * ROWS, 512), BF16),
        vmem((COLS, 16, 512), BF16),
        vmem((COLS, 16, 512), BF16),
        dma((17,)),
        dma((PAIR_CHUNKS,)),
        dma((COLS,)),
        dma((COLS,)),
        dma((2,)),
        dma((2,)),
        dma((COLS,)),
        dma((COLS,)),
        dma((COLS,)),
        dma((COLS,)),
    ]
    return pl.pallas_call(
        kernel,
        out_shape=(
            jax.ShapeDtypeStruct((ROWS, D), BF16),
            jax.ShapeDtypeStruct((128, 128), BF16),
        ),
        in_specs=[pl.BlockSpec(memory_space=pl.ANY)] * len(args),
        out_specs=(
            pl.BlockSpec(memory_space=pltpu.VMEM),
            pl.BlockSpec(memory_space=pltpu.VMEM),
        ),
        scratch_shapes=scratch,
        compiler_params=pltpu.CompilerParams(
            collective_id=0, has_side_effects=True, vmem_limit_bytes=60 * 1024 * 1024
        ),
        name="step",
    )(*args)


def solution(mesh):
    split = P(("row", "col"), None)
    placed = (
        split,
        P(("row", "col")),
        P(),
        P(),
        P("row", "col", None),
    ) + (P(),) * 13
    return jax.shard_map(
        local_step,
        mesh=mesh,
        in_specs=placed,
        out_specs=(P("row", None), split),
        check_vma=False,
    )
```

```python
import jax
import jax.numpy as jnp
from jax import lax
from jax.experimental import pallas as pl
from jax.experimental.pallas import tpu as pltpu
from jax.sharding import PartitionSpec as P

MESH = pl.DeviceIdType.MESH
F32 = jnp.float32
BF16 = jnp.bfloat16

D = 768
HEADS = 16
HEAD = 48
FF_TOK = 1536
FF_ATOM = 256
ROWS = 64
KEYS = 128
COLS = 8
HALF = ROWS // 2
PAIR_STEP = 8
WIDE = D + 128
TILES = D // 128
PAIR_CHUNKS = 4

NT = (((1,), (1,)), ((), ()))


def norm(values):
    mean = jnp.mean(values, axis=-1, keepdims=True)
    centered = values - mean
    var = jnp.mean(centered * centered, axis=-1, keepdims=True)
    return centered * lax.rsqrt(var + 1e-05)


def dot(a, b):
    return jnp.dot(a, b, preferred_element_type=F32)


def heads_of(tile):
    return [
        h for h in range(HEADS) if h * HEAD < (tile + 1) * 128 and (h + 1) * HEAD > tile * 128
    ]


FIRST_OF = [sum(len(heads_of(before)) for before in range(tile)) for tile in range(TILES)]
PLACES = FIRST_OF[-1] + len(heads_of(TILES - 1))


def lane_ids():
    return lax.broadcasted_iota(jnp.int32, (1, 128), 1)


def in_head(tile, h):
    lanes = lane_ids()
    return (lanes >= h * HEAD - tile * 128) & (lanes < (h + 1) * HEAD - tile * 128)


def coded(stats):
    lanes = lane_ids()
    piece0 = stats.astype(BF16).astype(F32)
    rest = stats - piece0
    piece1 = rest.astype(BF16).astype(F32)
    piece2 = (rest - piece1).astype(BF16).astype(F32)
    use0 = (lanes < 16) | ((lanes >= 48) & (lanes < 64))
    use1 = ((lanes >= 16) & (lanes < 32)) | (lanes >= 64)
    return jnp.where(use0, piece0, jnp.where(use1, piece1, piece2)).astype(BF16)


def decoded(line):
    line = line.astype(F32)
    top = line + pltpu.roll(line, 112, 1) + pltpu.roll(line, 96, 1)
    total = pltpu.roll(line, 80, 1) + pltpu.roll(line, 64, 1)
    return top, total


def spread(scales, expand):
    lanes = lane_ids()
    pieces = []
    for scale in scales:
        scale = jnp.where(lanes < HEADS, scale, 0.0)
        upper = scale.astype(BF16).astype(F32)
        pieces.append(upper + pltpu.roll(scale - upper, 16, 1))
    wide = dot(jnp.concatenate(pieces, axis=0).astype(BF16), expand)
    rows = scales[0].shape[0]
    return [wide[i * rows : (i + 1) * rows] for i in range(len(scales))]


def kernel(
    atom_hbm,
    ids_hbm,
    single_hbm,
    mask_hbm,
    pair_hbm,
    aproj_hbm,
    gain_hbm,
    wq_hbm,
    wk_hbm,
    wv_hbm,
    wg_hbm,
    wo_hbm,
    pproj_hbm,
    wsw_hbm,
    wdn_hbm,
    cproj_hbm,
    asw_hbm,
    adn_hbm,
    out_tok,
    out_atom,
    packed,
    ids,
    single,
    mask,
    pair,
    aproj,
    gain,
    wq,
    wk,
    wv,
    wg,
    wo,
    pproj,
    wsw,
    wdn,
    cproj,
    asw,
    adn,
    bias,
    projs,
    expand,
    abuf,
    ones,
    act_ref,
    qmask,
    nsend,
    kbuf,
    psend,
    sbuf,
    zsend,
    zbuf,
    obuf,
    lsem,
    psem,
    send1,
    recv1,
    send2,
    recv2,
    sems3,
    send4,
    recv4,
):
    r = lax.axis_index("row")
    c = lax.axis_index("col")
    x, y = lax.div(r, 4), lax.rem(r, 4)
    z, core = lax.div(c, 2), lax.rem(c, 2)
    turn = lax.rem(z - x + 4, 4)

    targets = []
    for step in range(2):
        dx = core + 2 * step
        tx = lax.rem(x + dx, 4)
        ty = lax.rem(y + dx + turn, 4)
        targets.append((tx * 4 + ty, lax.div(r, 2)))
    sources = []
    for block in range(2):
        sx = z
        sy = 2 * core + block
        dx = lax.rem(x - sx + 4, 4)
        sturn = lax.rem(y - sy - dx + 8, 4)
        sz = lax.rem(sx + sturn, 4)
        sources.append((sx * 4 + sy, sz * 2 + lax.rem(dx, 2)))
    own_keys = jnp.logical_and(targets[0][0] == r, targets[0][1] == c)

    sibling = (r, c + 1 - 2 * core)
    around = [None] + [(r, lax.rem(c + 2 * k, COLS)) for k in range(1, 4)]

    barrier = pltpu.get_barrier_semaphore()
    for peer in around[1:] + [sibling]:
        pl.semaphore_signal(barrier, inc=1, device_id=peer, device_id_type=MESH)
    for block in range(2):
        source_self = jnp.logical_and(sources[block][0] == r, sources[block][1] == c)

        @pl.when(jnp.logical_not(source_self))
        def _():
            pl.semaphore_signal(barrier, inc=1, device_id=sources[block], device_id_type=MESH)

    local = {}

    def fetch(name, index, src, dst):
        copy = pltpu.make_async_copy(src, dst, lsem.at[index])
        copy.start()
        local[name] = copy

    fetch("atom", 0, atom_hbm, packed.at[pl.ds(0, 128), :])
    fetch("ids", 1, ids_hbm, ids)
    fetch("aproj", 2, aproj_hbm, aproj)
    fetch("pproj", 3, pproj_hbm, pproj)
    pair_copies = []
    span = ROWS // PAIR_CHUNKS
    for chunk in range(PAIR_CHUNKS):
        part = pl.ds(chunk * span, span)
        copy = pltpu.make_async_copy(pair_hbm.at[part], pair.at[part], psem.at[chunk])
        copy.start()
        pair_copies.append(copy)
    fetch("single", 4, single_hbm.at[pl.ds(pl.multiple_of(r * ROWS, ROWS), ROWS), :], single)
    fetch("gain", 5, gain_hbm, gain)
    fetch("mask", 6, mask_hbm, mask)
    fetch("wq", 7, wq_hbm, wq)
    fetch("wk", 8, wk_hbm, wk)
    fetch("wv", 9, wv_hbm, wv)
    fetch("wg", 10, wg_hbm, wg)
    fetch("wo", 11, wo_hbm, wo)
    fetch("wsw", 12, wsw_hbm, wsw)
    fetch("wdn", 13, wdn_hbm, wdn)
    fetch("cproj", 14, cproj_hbm, cproj)
    fetch("asw", 15, asw_hbm, asw)
    fetch("adn", 16, adn_hbm, adn)

    local["ids"].wait()
    own_ids = (ids[...] - r * ROWS).astype(F32)
    packed[pl.ds(128, 16), :] = jnp.broadcast_to(own_ids, (16, 128)).astype(BF16)
    local["atom"].wait()
    pl.semaphore_wait(barrier, 6 - own_keys.astype(jnp.int32))

    def remote(src, dst, send, recv, device):
        return pltpu.make_async_remote_copy(
            src_ref=src,
            dst_ref=dst,
            send_sem=send,
            recv_sem=recv,
            device_id=device,
            device_id_type=MESH,
        )

    sends1 = {}
    for k in (2, 1, 3):
        sends1[2 * k] = remote(packed, abuf.at[2 * k], send1.at[2 * k], recv1.at[2 * k], around[k])
    sends1[1] = remote(packed, abuf.at[1], send1.at[1], recv1.at[1], sibling)
    for copy in sends1.values():
        copy.start()

    token_iota = lax.broadcasted_iota(jnp.int32, (ROWS, 128), 0).astype(F32)

    def pooled_of(atoms, id_row):
        hidden = jnp.maximum(dot(atoms, aproj[...]), 0.0).astype(BF16)
        onehot = jnp.where(token_iota == id_row, 1.0, 0.0).astype(BF16)
        return dot(onehot, hidden)

    local["pproj"].wait()
    proj_t = pproj[...]
    high = proj_t.astype(BF16)
    projs[pl.ds(0, 16), :] = high
    projs[pl.ds(16, 16), :] = (proj_t - high.astype(F32)).astype(BF16)
    lane = lax.broadcasted_iota(jnp.int32, (128, D), 1)
    line = lax.broadcasted_iota(jnp.int32, (128, D), 0)
    line = jnp.where(line >= HEADS, line - HEADS, line) * HEAD
    inside = jnp.logical_and(lane >= line, lane < line + HEAD)
    expand[...] = jnp.where(inside, 1.0, 0.0).astype(BF16)
    lane = lax.broadcasted_iota(jnp.int32, (KEYS, 128), 1)
    for h in range(HEADS):
        ones[pl.ds(h * KEYS, KEYS), :] = jnp.where(
            (lane == h + 48) | (lane == h + 64), 1.0, 0.0
        ).astype(BF16)

    def pair_bias(group, carry):
        tile = pair[pl.ds(group * PAIR_STEP, PAIR_STEP)]
        rows = norm(tile.astype(F32).reshape(PAIR_STEP * KEYS, 128)).astype(BF16)
        both = lax.dot_general(projs[...], rows, NT, preferred_element_type=F32)
        summed = both[:HEADS] + both[HEADS:]
        for i in range(PAIR_STEP):
            bias[pl.ds(group * PAIR_STEP + i, HEADS, stride=ROWS), :] = summed[
                :, i * KEYS : (i + 1) * KEYS
            ]
        return carry

    groups = ROWS // PAIR_STEP
    first = groups // 2
    for copy in pair_copies[: PAIR_CHUNKS // 2]:
        copy.wait()
    lax.fori_loop(0, first, pair_bias, 0)

    local["aproj"].wait()
    pooled = pooled_of(packed[pl.ds(0, 128), :], own_ids)
    def pooled_slot(index):
        return pooled_of(abuf[index, :128, :], abuf[index, 128:144, :].astype(F32)[:1, :])

    sends1[1].wait_recv()
    pooled += pooled_slot(1)
    for k in (1, 3, 2):
        sends1[2 * k].wait_recv()
        index = 2 * k + 1
        sends1[index] = remote(
            abuf.at[2 * k], abuf.at[index], send1.at[index], recv1.at[index], sibling
        )
        sends1[index].start()
        pooled += pooled_slot(2 * k)
    for k in (1, 3, 2):
        sends1[2 * k + 1].wait_recv()
        pooled += pooled_slot(2 * k + 1)

    local["single"].wait()
    local["gain"].wait()
    gains = jnp.concatenate([gain[t : t + 1, :] for t in range(D // 128)], axis=1)
    act = (norm(pooled) * gains + single[...].astype(F32)).astype(BF16).astype(F32)
    normed = norm(act).astype(BF16)
    nsend[...] = normed

    slot = lax.rem(r, 2)
    sends2 = []
    for step in range(2):
        copy = pltpu.make_async_remote_copy(
            src_ref=nsend,
            dst_ref=kbuf.at[slot],
            send_sem=send2.at[step],
            recv_sem=recv2.at[slot],
            device_id=targets[step],
            device_id_type=MESH,
        )
        sends2.append(copy)

    @pl.when(jnp.logical_not(own_keys))
    def _():
        sends2[0].start()

    sends2[1].start()

    @pl.when(own_keys)
    def _():
        kbuf[slot] = nsend[...]

    act_ref[...] = act
    local["wq"].wait()
    query = dot(normed, wq[...]).astype(BF16)
    for t in range(TILES):
        for n, h in enumerate(heads_of(t)):
            qmask[pl.ds((FIRST_OF[t] + n) * ROWS, ROWS), :] = jnp.where(
                in_head(t, h), query[:, t * 128 : t * 128 + 128], 0.0
            ).astype(BF16)
    own_rows = pl.ds(pl.multiple_of(core * HALF, HALF), HALF)
    other_rows = pl.ds(pl.multiple_of(HALF - core * HALF, HALF), HALF)
    local["wg"].wait()
    gate = jax.nn.sigmoid(dot(nsend[own_rows, :], wg[...]))
    for copy in pair_copies[PAIR_CHUNKS // 2 :]:
        copy.wait()
    lax.fori_loop(first, groups, pair_bias, 0)
    local["mask"].wait()
    masking = jnp.where(mask[pl.ds(c, 1), :] == 1, 0.0, -1000000000.0).astype(F32)
    local["wk"].wait()
    local["wv"].wait()

    for block in range(2):
        own_block = jnp.logical_and(own_keys, slot == block)

        @pl.when(jnp.logical_not(own_block))
        def _():
            pltpu.make_async_remote_copy(
                src_ref=nsend,
                dst_ref=kbuf.at[block],
                send_sem=send2.at[0],
                recv_sem=recv2.at[block],
                device_id=targets[0],
                device_id_type=MESH,
            ).wait_recv()

    keys_in = kbuf[...].reshape(KEYS, D)
    key = dot(keys_in, wk[...]).astype(BF16)
    value = dot(keys_in, wv[...]).astype(BF16)

    scores = [None] * HEADS
    for t in range(TILES):
        heads = heads_of(t)
        terms = lax.dot_general(
            qmask[pl.ds(FIRST_OF[t] * ROWS, len(heads) * ROWS), :],
            key[:, t * 128 : t * 128 + 128],
            NT,
            preferred_element_type=F32,
        )
        for n, h in enumerate(heads):
            term = terms[n * ROWS : (n + 1) * ROWS]
            scores[h] = term if scores[h] is None else scores[h] + term
    scores = [
        score * (1.0 / HEAD**0.5) + bias[pl.ds(h * ROWS, ROWS), :] + masking
        for h, score in enumerate(scores)
    ]
    tops = [jnp.max(score, axis=-1, keepdims=True) for score in scores]
    expos = [jnp.exp(score - top).astype(BF16) for score, top in zip(scores, tops)]
    for t in range(TILES):
        heads = heads_of(t)
        v_tile = value[:, t * 128 : t * 128 + 128]
        part = dot(
            jnp.concatenate([expos[h] for h in heads], axis=1),
            jnp.concatenate(
                [jnp.where(in_head(t, h), v_tile, 0.0).astype(BF16) for h in heads], axis=0
            ),
        )
        psend[:, pl.ds(t * 128, 128)] = part.astype(BF16)
    stats = dot(jnp.concatenate(expos, axis=1), ones[...])
    lanes = lane_ids()
    for h, top in enumerate(tops):
        stats = jnp.where((lanes == h) | (lanes == h + 16) | (lanes == h + 32), top, stats)
    psend[:, pl.ds(D, 128)] = coded(stats)

    send3 = remote(psend.at[other_rows, :], sbuf, sems3.at[0], sems3.at[1], sibling)
    send3.start()
    own_act = act_ref[own_rows, :]
    for name in ("wo", "wsw", "wdn", "cproj", "asw", "adn"):
        local[name].wait()
    mine = psend[own_rows, :]
    send3.wait_recv()
    theirs = sbuf[...]
    top_a, total_a = decoded(mine[:, D:])
    top_b, total_b = decoded(theirs[:, D:])
    top = jnp.maximum(top_a, top_b)
    scale_a, scale_b = jnp.exp(top_a - top), jnp.exp(top_b - top)
    total = scale_a * total_a + scale_b * total_b
    wide_a, wide_b = spread([scale_a, scale_b], expand[...])
    merged = wide_a * mine[:, :D].astype(F32) + wide_b * theirs[:, :D].astype(F32)
    top = jnp.where(lanes < HEADS, top, 0.0)
    total = jnp.where(lanes < HEADS, total, 0.0)
    stats = (
        top
        + pltpu.roll(top, 16, 1)
        + pltpu.roll(top, 32, 1)
        + pltpu.roll(total, 48, 1)
        + pltpu.roll(total, 64, 1)
    )
    zsend[:, pl.ds(0, D)] = merged.astype(BF16)
    zsend[:, pl.ds(D, 128)] = coded(stats)
    sends4 = {}
    for k in (2, 1, 3):
        sends4[k] = remote(zsend, zbuf.at[k], send4.at[k], recv4.at[k], around[k])
        sends4[k].start()
    parts, tops, totals = [merged], [top], [total]
    for k in (1, 3, 2):
        sends4[k].wait_recv()
        got = zbuf[k]
        parts.append(got[:, :D].astype(F32))
        other_top, other_total = decoded(got[:, D:])
        tops.append(other_top)
        totals.append(other_total)
    peak = tops[0]
    for top in tops[1:]:
        peak = jnp.maximum(peak, top)
    scales = [jnp.exp(top - peak) for top in tops]
    whole = scales[0] * totals[0]
    for scale, total in zip(scales[1:], totals[1:]):
        whole += scale * total
    wides = spread([scale / whole for scale in scales], expand[...])
    attended = wides[0] * parts[0]
    for wide, part in zip(wides[1:], parts[1:]):
        attended += wide * part

    gated = (gate * attended).astype(BF16)
    updated = (own_act + dot(gated, wo[...])).astype(BF16).astype(F32)
    updated_norm = norm(updated).astype(BF16)
    finished = updated
    width = 512
    down = jnp.zeros((HALF, D), F32)
    for step in range(FF_TOK // width):
        g = dot(updated_norm, wsw[:, step * width : (step + 1) * width])
        u = dot(updated_norm, wsw[:, FF_TOK + step * width : FF_TOK + (step + 1) * width])
        mid = (jax.nn.silu(g) * u).astype(BF16)
        down += dot(mid, wdn[step * width : (step + 1) * width, :])
    finished = (updated + down).astype(BF16).astype(F32)
    cond = dot(norm(finished).astype(BF16), cproj[...])
    obuf[own_rows, pl.ds(0, D)] = finished.astype(BF16)
    obuf[own_rows, pl.ds(D, 128)] = cond.astype(BF16)

    send5 = remote(obuf.at[own_rows, :], obuf.at[own_rows, :], sems3.at[2], sems3.at[3], sibling)
    send5.start()

    onehot_t = jnp.transpose(jnp.where(token_iota == own_ids, 1.0, 0.0)).astype(BF16)
    atoms = packed[pl.ds(0, 128), :].astype(F32)

    remote(
        obuf.at[other_rows, :], obuf.at[other_rows, :], sems3.at[2], sems3.at[3], sibling
    ).wait_recv()
    out_tok[...] = obuf[:, pl.ds(0, D)]
    conds = obuf[:, pl.ds(D, 128)]
    resid = atoms + dot(onehot_t, conds)
    both = dot(norm(resid).astype(BF16), asw[...])
    mid = (jax.nn.silu(both[:, :FF_ATOM]) * both[:, FF_ATOM:]).astype(BF16)
    out_atom[...] = (resid + dot(mid, adn[...])).astype(BF16)

    for copy in sends1.values():
        copy.wait_send()

    @pl.when(jnp.logical_not(own_keys))
    def _():
        sends2[0].wait_send()

    sends2[1].wait_send()
    send3.wait_send()
    for copy in sends4.values():
        copy.wait_send()
    send5.wait_send()


def local_step(
    atom_single,
    atom_token,
    token_single,
    token_mask,
    pair,
    atom_proj,
    pool_gain,
    w_query,
    w_key,
    w_value,
    w_gate,
    w_out,
    pair_proj,
    w_swiglu,
    w_down,
    cond_proj,
    atom_swiglu,
    atom_down,
):
    args = (
        atom_single,
        atom_token.reshape(1, 128),
        token_single,
        token_mask.reshape(COLS, KEYS),
        pair,
        atom_proj,
        pool_gain.reshape(D // 128, 128),
        w_query,
        w_key,
        w_value,
        w_gate,
        w_out,
        pair_proj.T,
        w_swiglu,
        w_down,
        cond_proj,
        atom_swiglu,
        atom_down,
    )
    vmem = pltpu.VMEM
    dma = pltpu.SemaphoreType.DMA
    scratch = [
        vmem((144, 128), BF16),
        vmem((1, 128), jnp.int32),
        vmem((ROWS, D), BF16),
        vmem((COLS, KEYS), jnp.int32),
        vmem((ROWS, KEYS, 128), BF16),
        vmem((128, D), BF16),
        vmem((D // 128, 128), F32),
        vmem((D, D), BF16),
        vmem((D, D), BF16),
        vmem((D, D), BF16),
        vmem((D, D), BF16),
        vmem((D, D), BF16),
        vmem((HEADS, 128), F32),
        vmem((D, 2 * FF_TOK), BF16),
        vmem((FF_TOK, D), BF16),
        vmem((D, 128), BF16),
        vmem((128, 2 * FF_ATOM), BF16),
        vmem((FF_ATOM, 128), BF16),
        vmem((HEADS * ROWS, KEYS), F32),
        vmem((2 * HEADS, 128), BF16),
        vmem((128, D), BF16),
        vmem((COLS, 144, 128), BF16),
        vmem((HEADS * KEYS, 128), BF16),
        vmem((ROWS, D), F32),
        vmem((PLACES * ROWS, 128), BF16),
        vmem((ROWS, D), BF16),
        vmem((2, ROWS, D), BF16),
        vmem((ROWS, WIDE), BF16),
        vmem((HALF, WIDE), BF16),
        vmem((HALF, WIDE), BF16),
        vmem((4, HALF, WIDE), BF16),
        vmem((ROWS, WIDE), BF16),
        dma((17,)),
        dma((PAIR_CHUNKS,)),
        dma((COLS,)),
        dma((COLS,)),
        dma((2,)),
        dma((2,)),
        dma((4,)),
        dma((4,)),
        dma((4,)),
    ]
    return pl.pallas_call(
        kernel,
        out_shape=(
            jax.ShapeDtypeStruct((ROWS, D), BF16),
            jax.ShapeDtypeStruct((128, 128), BF16),
        ),
        in_specs=[pl.BlockSpec(memory_space=pl.ANY)] * len(args),
        out_specs=(
            pl.BlockSpec(memory_space=pltpu.VMEM),
            pl.BlockSpec(memory_space=pltpu.VMEM),
        ),
        scratch_shapes=scratch,
        compiler_params=pltpu.CompilerParams(
            collective_id=0, has_side_effects=True, vmem_limit_bytes=60 * 1024 * 1024
        ),
        name="step",
    )(*args)


def solution(mesh):
    split = P(("row", "col"), None)
    placed = (
        split,
        P(("row", "col")),
        P(),
        P(),
        P("row", "col", None),
    ) + (P(),) * 13
    return jax.shard_map(
        local_step,
        mesh=mesh,
        in_specs=placed,
        out_specs=(P("row", None), split),
        check_vma=False,
    )
```

```python
import jax
import jax.numpy as jnp
from jax import lax
from jax.experimental import pallas as pl
from jax.experimental.pallas import tpu as pltpu
from jax.sharding import PartitionSpec as P

MESH = pl.DeviceIdType.MESH
F32 = jnp.float32
BF16 = jnp.bfloat16

D = 768
HEADS = 16
HEAD = 48
FF_TOK = 1536
FF_ATOM = 256
ROWS = 64
KEYS = 128
COLS = 8
HALF = ROWS // 2
PAIR_STEP = 8
WIDE = D + 128
TILES = D // 128
PAIR_CHUNKS = 4

NT = (((1,), (1,)), ((), ()))


def norm(values):
    mean = jnp.mean(values, axis=-1, keepdims=True)
    centered = values - mean
    var = jnp.mean(centered * centered, axis=-1, keepdims=True)
    return centered * lax.rsqrt(var + 1e-05)


def dot(a, b):
    return jnp.dot(a, b, preferred_element_type=F32)


def heads_of(tile):
    return [
        h for h in range(HEADS) if h * HEAD < (tile + 1) * 128 and (h + 1) * HEAD > tile * 128
    ]


FIRST_OF = [sum(len(heads_of(before)) for before in range(tile)) for tile in range(TILES)]
PLACES = FIRST_OF[-1] + len(heads_of(TILES - 1))


def lane_ids():
    return lax.broadcasted_iota(jnp.int32, (1, 128), 1)


def in_head(tile, h):
    lanes = lane_ids()
    return (lanes >= h * HEAD - tile * 128) & (lanes < (h + 1) * HEAD - tile * 128)


def coded(stats):
    lanes = lane_ids()
    piece0 = stats.astype(BF16).astype(F32)
    rest = stats - piece0
    piece1 = rest.astype(BF16).astype(F32)
    piece2 = (rest - piece1).astype(BF16).astype(F32)
    use0 = (lanes < 16) | ((lanes >= 48) & (lanes < 64))
    use1 = ((lanes >= 16) & (lanes < 32)) | (lanes >= 64)
    return jnp.where(use0, piece0, jnp.where(use1, piece1, piece2)).astype(BF16)


def decoded(line):
    line = line.astype(F32)
    top = line + pltpu.roll(line, 112, 1) + pltpu.roll(line, 96, 1)
    total = pltpu.roll(line, 80, 1) + pltpu.roll(line, 64, 1)
    return top, total


def spread(scales, expand):
    lanes = lane_ids()
    pieces = []
    for scale in scales:
        scale = jnp.where(lanes < HEADS, scale, 0.0)
        upper = scale.astype(BF16).astype(F32)
        pieces.append(upper + pltpu.roll(scale - upper, 16, 1))
    wide = dot(jnp.concatenate(pieces, axis=0).astype(BF16), expand)
    rows = scales[0].shape[0]
    return [wide[i * rows : (i + 1) * rows] for i in range(len(scales))]


def kernel(
    atom_hbm,
    ids_hbm,
    single_hbm,
    mask_hbm,
    pair_hbm,
    aproj_hbm,
    gain_hbm,
    wq_hbm,
    wk_hbm,
    wv_hbm,
    wg_hbm,
    wo_hbm,
    pproj_hbm,
    wsw_hbm,
    wdn_hbm,
    cproj_hbm,
    done_hbm,
    packed,
    ids,
    single,
    mask,
    pair,
    aproj,
    gain,
    wq,
    wk,
    wv,
    wg,
    wo,
    pproj,
    wsw,
    wdn,
    cproj,
    bias,
    projs,
    expand,
    abuf,
    ones,
    act_ref,
    qmask,
    nsend,
    kbuf,
    psend,
    sbuf,
    zsend,
    zbuf,
    obuf,
    lsem,
    psem,
    send1,
    recv1,
    send2,
    recv2,
    sems3,
    send4,
    recv4,
):
    r = lax.axis_index("row")
    c = lax.axis_index("col")
    x, y = lax.div(r, 4), lax.rem(r, 4)
    z, core = lax.div(c, 2), lax.rem(c, 2)
    turn = lax.rem(z - x + 4, 4)

    targets = []
    for step in range(2):
        dx = core + 2 * step
        tx = lax.rem(x + dx, 4)
        ty = lax.rem(y + dx + turn, 4)
        targets.append((tx * 4 + ty, lax.div(r, 2)))
    sources = []
    for block in range(2):
        sx = z
        sy = 2 * core + block
        dx = lax.rem(x - sx + 4, 4)
        sturn = lax.rem(y - sy - dx + 8, 4)
        sz = lax.rem(sx + sturn, 4)
        sources.append((sx * 4 + sy, sz * 2 + lax.rem(dx, 2)))
    own_keys = jnp.logical_and(targets[0][0] == r, targets[0][1] == c)

    sibling = (r, c + 1 - 2 * core)
    around = [None] + [(r, lax.rem(c + 2 * k, COLS)) for k in range(1, 4)]

    barrier = pltpu.get_barrier_semaphore()
    for peer in around[1:] + [sibling]:
        pl.semaphore_signal(barrier, inc=1, device_id=peer, device_id_type=MESH)
    for block in range(2):
        source_self = jnp.logical_and(sources[block][0] == r, sources[block][1] == c)

        @pl.when(jnp.logical_not(source_self))
        def _():
            pl.semaphore_signal(barrier, inc=1, device_id=sources[block], device_id_type=MESH)

    local = {}

    def fetch(name, index, src, dst):
        copy = pltpu.make_async_copy(src, dst, lsem.at[index])
        copy.start()
        local[name] = copy

    fetch("atom", 0, atom_hbm, packed.at[pl.ds(0, 128), :])
    fetch("ids", 1, ids_hbm, ids)
    fetch("aproj", 2, aproj_hbm, aproj)
    fetch("pproj", 3, pproj_hbm, pproj)
    pair_copies = []
    span = ROWS // PAIR_CHUNKS
    for chunk in range(PAIR_CHUNKS):
        part = pl.ds(chunk * span, span)
        copy = pltpu.make_async_copy(pair_hbm.at[part], pair.at[part], psem.at[chunk])
        copy.start()
        pair_copies.append(copy)
    fetch("single", 4, single_hbm.at[pl.ds(pl.multiple_of(r * ROWS, ROWS), ROWS), :], single)
    fetch("gain", 5, gain_hbm, gain)
    fetch("mask", 6, mask_hbm, mask)
    fetch("wq", 7, wq_hbm, wq)
    fetch("wk", 8, wk_hbm, wk)
    fetch("wv", 9, wv_hbm, wv)
    fetch("wg", 10, wg_hbm, wg)
    fetch("wo", 11, wo_hbm, wo)
    fetch("wsw", 12, wsw_hbm, wsw)
    fetch("wdn", 13, wdn_hbm, wdn)
    fetch("cproj", 14, cproj_hbm, cproj)

    local["ids"].wait()
    own_ids = (ids[...] - r * ROWS).astype(F32)
    packed[pl.ds(128, 16), :] = jnp.broadcast_to(own_ids, (16, 128)).astype(BF16)
    local["atom"].wait()
    pl.semaphore_wait(barrier, 6 - own_keys.astype(jnp.int32))

    def remote(src, dst, send, recv, device):
        return pltpu.make_async_remote_copy(
            src_ref=src,
            dst_ref=dst,
            send_sem=send,
            recv_sem=recv,
            device_id=device,
            device_id_type=MESH,
        )

    sends1 = {}
    for k in (2, 1, 3):
        sends1[2 * k] = remote(packed, abuf.at[2 * k], send1.at[2 * k], recv1.at[2 * k], around[k])
    sends1[1] = remote(packed, abuf.at[1], send1.at[1], recv1.at[1], sibling)
    for copy in sends1.values():
        copy.start()

    token_iota = lax.broadcasted_iota(jnp.int32, (ROWS, 128), 0).astype(F32)

    def pooled_of(atoms, id_row):
        hidden = jnp.maximum(dot(atoms, aproj[...]), 0.0).astype(BF16)
        onehot = jnp.where(token_iota == id_row, 1.0, 0.0).astype(BF16)
        return dot(onehot, hidden)

    local["pproj"].wait()
    proj_t = pproj[...]
    high = proj_t.astype(BF16)
    projs[pl.ds(0, 16), :] = high
    projs[pl.ds(16, 16), :] = (proj_t - high.astype(F32)).astype(BF16)
    lane = lax.broadcasted_iota(jnp.int32, (128, D), 1)
    line = lax.broadcasted_iota(jnp.int32, (128, D), 0)
    line = jnp.where(line >= HEADS, line - HEADS, line) * HEAD
    inside = jnp.logical_and(lane >= line, lane < line + HEAD)
    expand[...] = jnp.where(inside, 1.0, 0.0).astype(BF16)
    lane = lax.broadcasted_iota(jnp.int32, (KEYS, 128), 1)
    for h in range(HEADS):
        ones[pl.ds(h * KEYS, KEYS), :] = jnp.where(
            (lane == h + 48) | (lane == h + 64), 1.0, 0.0
        ).astype(BF16)

    def pair_bias(group, carry):
        tile = pair[pl.ds(group * PAIR_STEP, PAIR_STEP)]
        rows = norm(tile.astype(F32).reshape(PAIR_STEP * KEYS, 128)).astype(BF16)
        both = lax.dot_general(projs[...], rows, NT, preferred_element_type=F32)
        summed = both[:HEADS] + both[HEADS:]
        for i in range(PAIR_STEP):
            bias[pl.ds(group * PAIR_STEP + i, HEADS, stride=ROWS), :] = summed[
                :, i * KEYS : (i + 1) * KEYS
            ]
        return carry

    groups = ROWS // PAIR_STEP
    first = groups // 2
    for copy in pair_copies[: PAIR_CHUNKS // 2]:
        copy.wait()
    lax.fori_loop(0, first, pair_bias, 0)

    local["aproj"].wait()
    pooled = pooled_of(packed[pl.ds(0, 128), :], own_ids)
    def pooled_slot(index):
        return pooled_of(abuf[index, :128, :], abuf[index, 128:144, :].astype(F32)[:1, :])

    sends1[1].wait_recv()
    pooled += pooled_slot(1)
    for k in (1, 3, 2):
        sends1[2 * k].wait_recv()
        index = 2 * k + 1
        sends1[index] = remote(
            abuf.at[2 * k], abuf.at[index], send1.at[index], recv1.at[index], sibling
        )
        sends1[index].start()
        pooled += pooled_slot(2 * k)
    for k in (1, 3, 2):
        sends1[2 * k + 1].wait_recv()
        pooled += pooled_slot(2 * k + 1)

    local["single"].wait()
    local["gain"].wait()
    gains = jnp.concatenate([gain[t : t + 1, :] for t in range(D // 128)], axis=1)
    act = (norm(pooled) * gains + single[...].astype(F32)).astype(BF16).astype(F32)
    normed = norm(act).astype(BF16)
    nsend[...] = normed

    slot = lax.rem(r, 2)
    sends2 = []
    for step in range(2):
        copy = pltpu.make_async_remote_copy(
            src_ref=nsend,
            dst_ref=kbuf.at[slot],
            send_sem=send2.at[step],
            recv_sem=recv2.at[slot],
            device_id=targets[step],
            device_id_type=MESH,
        )
        sends2.append(copy)

    @pl.when(jnp.logical_not(own_keys))
    def _():
        sends2[0].start()

    sends2[1].start()

    @pl.when(own_keys)
    def _():
        kbuf[slot] = nsend[...]

    act_ref[...] = act
    local["wq"].wait()
    query = dot(normed, wq[...]).astype(BF16)
    for t in range(TILES):
        for n, h in enumerate(heads_of(t)):
            qmask[pl.ds((FIRST_OF[t] + n) * ROWS, ROWS), :] = jnp.where(
                in_head(t, h), query[:, t * 128 : t * 128 + 128], 0.0
            ).astype(BF16)
    own_rows = pl.ds(pl.multiple_of(core * HALF, HALF), HALF)
    other_rows = pl.ds(pl.multiple_of(HALF - core * HALF, HALF), HALF)
    local["wg"].wait()
    gate = jax.nn.sigmoid(dot(nsend[own_rows, :], wg[...]))
    for copy in pair_copies[PAIR_CHUNKS // 2 :]:
        copy.wait()
    lax.fori_loop(first, groups, pair_bias, 0)
    local["mask"].wait()
    masking = jnp.where(mask[pl.ds(c, 1), :] == 1, 0.0, -1000000000.0).astype(F32)
    local["wk"].wait()
    local["wv"].wait()

    for block in range(2):
        own_block = jnp.logical_and(own_keys, slot == block)

        @pl.when(jnp.logical_not(own_block))
        def _():
            pltpu.make_async_remote_copy(
                src_ref=nsend,
                dst_ref=kbuf.at[block],
                send_sem=send2.at[0],
                recv_sem=recv2.at[block],
                device_id=targets[0],
                device_id_type=MESH,
            ).wait_recv()

    keys_in = kbuf[...].reshape(KEYS, D)
    key = dot(keys_in, wk[...]).astype(BF16)
    value = dot(keys_in, wv[...]).astype(BF16)

    scores = [None] * HEADS
    for t in range(TILES):
        heads = heads_of(t)
        terms = lax.dot_general(
            qmask[pl.ds(FIRST_OF[t] * ROWS, len(heads) * ROWS), :],
            key[:, t * 128 : t * 128 + 128],
            NT,
            preferred_element_type=F32,
        )
        for n, h in enumerate(heads):
            term = terms[n * ROWS : (n + 1) * ROWS]
            scores[h] = term if scores[h] is None else scores[h] + term
    scores = [
        score * (1.0 / HEAD**0.5) + bias[pl.ds(h * ROWS, ROWS), :] + masking
        for h, score in enumerate(scores)
    ]
    tops = [jnp.max(score, axis=-1, keepdims=True) for score in scores]
    expos = [jnp.exp(score - top).astype(BF16) for score, top in zip(scores, tops)]
    for t in range(TILES):
        heads = heads_of(t)
        v_tile = value[:, t * 128 : t * 128 + 128]
        part = dot(
            jnp.concatenate([expos[h] for h in heads], axis=1),
            jnp.concatenate(
                [jnp.where(in_head(t, h), v_tile, 0.0).astype(BF16) for h in heads], axis=0
            ),
        )
        psend[:, pl.ds(t * 128, 128)] = part.astype(BF16)
    stats = dot(jnp.concatenate(expos, axis=1), ones[...])
    lanes = lane_ids()
    for h, top in enumerate(tops):
        stats = jnp.where((lanes == h) | (lanes == h + 16) | (lanes == h + 32), top, stats)
    psend[:, pl.ds(D, 128)] = coded(stats)

    send3 = remote(psend.at[other_rows, :], sbuf, sems3.at[0], sems3.at[1], sibling)
    send3.start()
    own_act = act_ref[own_rows, :]
    for name in ("wo", "wsw", "wdn", "cproj"):
        local[name].wait()
    mine = psend[own_rows, :]
    send3.wait_recv()
    theirs = sbuf[...]
    top_a, total_a = decoded(mine[:, D:])
    top_b, total_b = decoded(theirs[:, D:])
    top = jnp.maximum(top_a, top_b)
    scale_a, scale_b = jnp.exp(top_a - top), jnp.exp(top_b - top)
    total = scale_a * total_a + scale_b * total_b
    wide_a, wide_b = spread([scale_a, scale_b], expand[...])
    merged = wide_a * mine[:, :D].astype(F32) + wide_b * theirs[:, :D].astype(F32)
    top = jnp.where(lanes < HEADS, top, 0.0)
    total = jnp.where(lanes < HEADS, total, 0.0)
    stats = (
        top
        + pltpu.roll(top, 16, 1)
        + pltpu.roll(top, 32, 1)
        + pltpu.roll(total, 48, 1)
        + pltpu.roll(total, 64, 1)
    )
    zsend[:, pl.ds(0, D)] = merged.astype(BF16)
    zsend[:, pl.ds(D, 128)] = coded(stats)
    sends4 = {}
    for k in (2, 1, 3):
        sends4[k] = remote(zsend, zbuf.at[k], send4.at[k], recv4.at[k], around[k])
        sends4[k].start()
    parts, tops, totals = [merged], [top], [total]
    for k in (1, 3, 2):
        sends4[k].wait_recv()
        got = zbuf[k]
        parts.append(got[:, :D].astype(F32))
        other_top, other_total = decoded(got[:, D:])
        tops.append(other_top)
        totals.append(other_total)
    peak = tops[0]
    for top in tops[1:]:
        peak = jnp.maximum(peak, top)
    scales = [jnp.exp(top - peak) for top in tops]
    whole = scales[0] * totals[0]
    for scale, total in zip(scales[1:], totals[1:]):
        whole += scale * total
    wides = spread([scale / whole for scale in scales], expand[...])
    attended = wides[0] * parts[0]
    for wide, part in zip(wides[1:], parts[1:]):
        attended += wide * part

    gated = (gate * attended).astype(BF16)
    updated = (own_act + dot(gated, wo[...])).astype(BF16).astype(F32)
    updated_norm = norm(updated).astype(BF16)
    finished = updated
    width = 512
    down = jnp.zeros((HALF, D), F32)
    for step in range(FF_TOK // width):
        g = dot(updated_norm, wsw[:, step * width : (step + 1) * width])
        u = dot(updated_norm, wsw[:, FF_TOK + step * width : FF_TOK + (step + 1) * width])
        mid = (jax.nn.silu(g) * u).astype(BF16)
        down += dot(mid, wdn[step * width : (step + 1) * width, :])
    finished = (updated + down).astype(BF16).astype(F32)
    cond = dot(norm(finished).astype(BF16), cproj[...])
    obuf[own_rows, pl.ds(0, D)] = finished.astype(BF16)
    obuf[own_rows, pl.ds(D, 128)] = cond.astype(BF16)

    send5 = remote(obuf.at[own_rows, :], obuf.at[own_rows, :], sems3.at[2], sems3.at[3], sibling)
    send5.start()
    store_own = pltpu.make_async_copy(
        obuf.at[own_rows, :], done_hbm.at[own_rows, :], lsem.at[15]
    )
    store_own.start()
    remote(
        obuf.at[other_rows, :], obuf.at[other_rows, :], sems3.at[2], sems3.at[3], sibling
    ).wait_recv()
    store_other = pltpu.make_async_copy(
        obuf.at[other_rows, :], done_hbm.at[other_rows, :], lsem.at[16]
    )
    store_other.start()

    for copy in sends1.values():
        copy.wait_send()

    @pl.when(jnp.logical_not(own_keys))
    def _():
        sends2[0].wait_send()

    sends2[1].wait_send()
    send3.wait_send()
    for copy in sends4.values():
        copy.wait_send()
    send5.wait_send()
    store_own.wait()
    store_other.wait()


def atoms_kernel(
    done_hbm,
    atom_hbm,
    ids_hbm,
    asw_hbm,
    adn_hbm,
    out_tok,
    out_atom,
    done,
    atom,
    ids,
    asw,
    adn,
    result,
    sems,
):
    pairs = ((ids_hbm, ids), (done_hbm, done), (atom_hbm, atom), (asw_hbm, asw), (adn_hbm, adn))
    copies = [
        pltpu.make_async_copy(src, dst, sems.at[n]) for n, (src, dst) in enumerate(pairs)
    ]
    for copy in copies:
        copy.start()
    row_start = lax.axis_index("row") * ROWS
    copies[0].wait()
    token_iota = lax.broadcasted_iota(jnp.int32, (ROWS, 128), 0) + row_start
    onehot_t = jnp.transpose(jnp.where(token_iota == ids[...], 1.0, 0.0)).astype(BF16)
    copies[1].wait()
    store_tok = pltpu.make_async_copy(done.at[:, pl.ds(0, D)], out_tok, sems.at[5])
    store_tok.start()
    for copy in copies[2:]:
        copy.wait()
    resid = atom[...].astype(F32) + dot(onehot_t, done[:, pl.ds(D, 128)])
    both = dot(norm(resid).astype(BF16), asw[...])
    mid = (jax.nn.silu(both[:, :FF_ATOM]) * both[:, FF_ATOM:]).astype(BF16)
    result[...] = (resid + dot(mid, adn[...])).astype(BF16)
    store_atom = pltpu.make_async_copy(result, out_atom, sems.at[6])
    store_atom.start()
    store_tok.wait()
    store_atom.wait()


def local_step(
    atom_single,
    atom_token,
    token_single,
    token_mask,
    pair,
    atom_proj,
    pool_gain,
    w_query,
    w_key,
    w_value,
    w_gate,
    w_out,
    pair_proj,
    w_swiglu,
    w_down,
    cond_proj,
    atom_swiglu,
    atom_down,
):
    ids = atom_token.reshape(1, 128)
    args = (
        atom_single,
        ids,
        token_single,
        token_mask.reshape(COLS, KEYS),
        pair,
        atom_proj,
        pool_gain.reshape(D // 128, 128),
        w_query,
        w_key,
        w_value,
        w_gate,
        w_out,
        pair_proj.T,
        w_swiglu,
        w_down,
        cond_proj,
    )
    vmem = pltpu.VMEM
    dma = pltpu.SemaphoreType.DMA
    scratch = [
        vmem((144, 128), BF16),
        vmem((1, 128), jnp.int32),
        vmem((ROWS, D), BF16),
        vmem((COLS, KEYS), jnp.int32),
        vmem((ROWS, KEYS, 128), BF16),
        vmem((128, D), BF16),
        vmem((D // 128, 128), F32),
        vmem((D, D), BF16),
        vmem((D, D), BF16),
        vmem((D, D), BF16),
        vmem((D, D), BF16),
        vmem((D, D), BF16),
        vmem((HEADS, 128), F32),
        vmem((D, 2 * FF_TOK), BF16),
        vmem((FF_TOK, D), BF16),
        vmem((D, 128), BF16),
        vmem((HEADS * ROWS, KEYS), F32),
        vmem((2 * HEADS, 128), BF16),
        vmem((128, D), BF16),
        vmem((COLS, 144, 128), BF16),
        vmem((HEADS * KEYS, 128), BF16),
        vmem((ROWS, D), F32),
        vmem((PLACES * ROWS, 128), BF16),
        vmem((ROWS, D), BF16),
        vmem((2, ROWS, D), BF16),
        vmem((ROWS, WIDE), BF16),
        vmem((HALF, WIDE), BF16),
        vmem((HALF, WIDE), BF16),
        vmem((4, HALF, WIDE), BF16),
        vmem((ROWS, WIDE), BF16),
        dma((17,)),
        dma((PAIR_CHUNKS,)),
        dma((COLS,)),
        dma((COLS,)),
        dma((2,)),
        dma((2,)),
        dma((4,)),
        dma((4,)),
        dma((4,)),
    ]
    anywhere = pl.BlockSpec(memory_space=pl.ANY)
    limit = 60 * 1024 * 1024
    done = pl.pallas_call(
        kernel,
        out_shape=jax.ShapeDtypeStruct((ROWS, WIDE), BF16),
        in_specs=[anywhere] * len(args),
        out_specs=anywhere,
        scratch_shapes=scratch,
        compiler_params=pltpu.CompilerParams(
            collective_id=0, has_side_effects=True, vmem_limit_bytes=limit
        ),
        name="step",
    )(*args)
    return pl.pallas_call(
        atoms_kernel,
        out_shape=(
            jax.ShapeDtypeStruct((ROWS, D), BF16),
            jax.ShapeDtypeStruct((128, 128), BF16),
        ),
        in_specs=[anywhere] * 5,
        out_specs=(anywhere, anywhere),
        scratch_shapes=[
            vmem((ROWS, WIDE), BF16),
            vmem((128, 128), BF16),
            vmem((1, 128), jnp.int32),
            vmem((128, 2 * FF_ATOM), BF16),
            vmem((FF_ATOM, 128), BF16),
            vmem((128, 128), BF16),
            dma((7,)),
        ],
        compiler_params=pltpu.CompilerParams(vmem_limit_bytes=limit),
        name="atoms",
    )(done, atom_single, ids, atom_swiglu, atom_down)


def solution(mesh):
    split = P(("row", "col"), None)
    placed = (
        split,
        P(("row", "col")),
        P(),
        P(),
        P("row", "col", None),
    ) + (P(),) * 13
    return jax.shard_map(
        local_step,
        mesh=mesh,
        in_specs=placed,
        out_specs=(P("row", None), split),
        check_vma=False,
    )
```

```python
import jax
import jax.numpy as jnp
from jax import lax
from jax.experimental import pallas as pl
from jax.experimental.pallas import tpu as pltpu
from jax.sharding import PartitionSpec as P

MESH = pl.DeviceIdType.MESH
F32 = jnp.float32
BF16 = jnp.bfloat16

D = 768
HEADS = 16
HEAD = 48
FF_TOK = 1536
FF_ATOM = 256
ROWS = 64
KEYS = 128
COLS = 8
HALF = ROWS // 2
PAIR_STEP = 8
WIDE = D + 128
TILES = D // 128
PAIR_CHUNKS = 4

NT = (((1,), (1,)), ((), ()))


def norm(values):
    mean = jnp.mean(values, axis=-1, keepdims=True)
    centered = values - mean
    var = jnp.mean(centered * centered, axis=-1, keepdims=True)
    return centered * lax.rsqrt(var + 1e-05)


def dot(a, b):
    return jnp.dot(a, b, preferred_element_type=F32)


def heads_of(tile):
    return [
        h for h in range(HEADS) if h * HEAD < (tile + 1) * 128 and (h + 1) * HEAD > tile * 128
    ]


FIRST_OF = [sum(len(heads_of(before)) for before in range(tile)) for tile in range(TILES)]
PLACES = FIRST_OF[-1] + len(heads_of(TILES - 1))


def lane_ids():
    return lax.broadcasted_iota(jnp.int32, (1, 128), 1)


def in_head(tile, h):
    lanes = lane_ids()
    return (lanes >= h * HEAD - tile * 128) & (lanes < (h + 1) * HEAD - tile * 128)


def coded(stats):
    lanes = lane_ids()
    piece0 = stats.astype(BF16).astype(F32)
    rest = stats - piece0
    piece1 = rest.astype(BF16).astype(F32)
    piece2 = (rest - piece1).astype(BF16).astype(F32)
    use0 = (lanes < 16) | ((lanes >= 48) & (lanes < 64))
    use1 = ((lanes >= 16) & (lanes < 32)) | (lanes >= 64)
    return jnp.where(use0, piece0, jnp.where(use1, piece1, piece2)).astype(BF16)


def decoded(line):
    line = line.astype(F32)
    top = line + pltpu.roll(line, 112, 1) + pltpu.roll(line, 96, 1)
    total = pltpu.roll(line, 80, 1) + pltpu.roll(line, 64, 1)
    return top, total


def spread(scales, expand):
    lanes = lane_ids()
    pieces = []
    for scale in scales:
        scale = jnp.where(lanes < HEADS, scale, 0.0)
        upper = scale.astype(BF16).astype(F32)
        pieces.append(upper + pltpu.roll(scale - upper, 16, 1))
    wide = dot(jnp.concatenate(pieces, axis=0).astype(BF16), expand)
    rows = scales[0].shape[0]
    return [wide[i * rows : (i + 1) * rows] for i in range(len(scales))]


def kernel(
    atom_hbm,
    ids_hbm,
    single_hbm,
    mask_hbm,
    pair_hbm,
    aproj_hbm,
    gain_hbm,
    wq_hbm,
    wk_hbm,
    wv_hbm,
    wg_hbm,
    wo_hbm,
    pproj_hbm,
    wsw_hbm,
    wdn_hbm,
    cproj_hbm,
    done_hbm,
    packed,
    ids,
    single,
    mask,
    pair,
    aproj,
    gain,
    wq,
    wk,
    wv,
    wg,
    wo,
    pproj,
    wsw,
    wdn,
    cproj,
    bias,
    projs,
    expand,
    abuf,
    ones,
    act_ref,
    qmask,
    nsend,
    kbuf,
    psend,
    sbuf,
    zsend,
    zbuf,
    obuf,
    lsem,
    psem,
    send1,
    recv1,
    relay,
    send2,
    recv2,
    sems3,
    send4,
    recv4,
):
    r = lax.axis_index("row")
    c = lax.axis_index("col")
    x, y = lax.div(r, 4), lax.rem(r, 4)
    z, core = lax.div(c, 2), lax.rem(c, 2)
    turn = lax.rem(z - x + 4, 4)

    home = lax.div(y, 2)
    sender = core == home
    targets = []
    for dx in range(4):
        tx, ty = lax.rem(x + dx, 4), lax.rem(y + dx + turn, 4)
        targets.append((tx * 4 + ty, lax.div(r, 2)))
    own_keys = jnp.logical_and(sender, turn == 0)

    sibling = (r, c + 1 - 2 * core)
    around = [None] + [(r, lax.rem(c + 2 * k, COLS)) for k in range(1, 4)]
    along_x = [(lax.rem(x + k, 4) * 4 + y, c) for k in range(1, 4)]
    along_y = [(x * 4 + lax.rem(y + k, 4), c) for k in range(1, 4)]

    barrier = pltpu.get_barrier_semaphore()
    for peer in around[1:] + [sibling] + along_x + along_y:
        pl.semaphore_signal(barrier, inc=1, device_id=peer, device_id_type=MESH)

    local = {}

    def fetch(name, index, src, dst):
        copy = pltpu.make_async_copy(src, dst, lsem.at[index])
        copy.start()
        local[name] = copy

    fetch("atom", 0, atom_hbm, packed.at[pl.ds(0, 128), :])
    fetch("ids", 1, ids_hbm, ids)
    fetch("aproj", 2, aproj_hbm, aproj)
    fetch("pproj", 3, pproj_hbm, pproj)
    pair_copies = []
    span = ROWS // PAIR_CHUNKS
    for chunk in range(PAIR_CHUNKS):
        part = pl.ds(chunk * span, span)
        copy = pltpu.make_async_copy(pair_hbm.at[part], pair.at[part], psem.at[chunk])
        copy.start()
        pair_copies.append(copy)
    fetch("single", 4, single_hbm.at[pl.ds(pl.multiple_of(r * ROWS, ROWS), ROWS), :], single)
    fetch("gain", 5, gain_hbm, gain)
    fetch("mask", 6, mask_hbm, mask)
    fetch("wq", 7, wq_hbm, wq)
    fetch("wk", 8, wk_hbm, wk)
    fetch("wv", 9, wv_hbm, wv)
    fetch("wg", 10, wg_hbm, wg)
    fetch("wo", 11, wo_hbm, wo)
    fetch("wsw", 12, wsw_hbm, wsw)
    fetch("wdn", 13, wdn_hbm, wdn)
    fetch("cproj", 14, cproj_hbm, cproj)

    local["ids"].wait()
    own_ids = (ids[...] - r * ROWS).astype(F32)
    packed[pl.ds(128, 16), :] = jnp.broadcast_to(own_ids, (16, 128)).astype(BF16)
    local["atom"].wait()
    pl.semaphore_wait(barrier, 10)

    def remote(src, dst, send, recv, device):
        return pltpu.make_async_remote_copy(
            src_ref=src,
            dst_ref=dst,
            send_sem=send,
            recv_sem=recv,
            device_id=device,
            device_id_type=MESH,
        )

    sends1 = {}
    for k in (2, 1, 3):
        sends1[2 * k] = remote(packed, abuf.at[2 * k], send1.at[2 * k], recv1.at[2 * k], around[k])
    sends1[1] = remote(packed, abuf.at[1], send1.at[1], recv1.at[1], sibling)
    for copy in sends1.values():
        copy.start()
    for peer in along_x:
        pl.semaphore_signal(relay.at[0], inc=1, device_id=peer, device_id_type=MESH)

    token_iota = lax.broadcasted_iota(jnp.int32, (ROWS, 128), 0).astype(F32)

    def pooled_of(atoms, id_row):
        hidden = jnp.maximum(dot(atoms, aproj[...]), 0.0).astype(BF16)
        onehot = jnp.where(token_iota == id_row, 1.0, 0.0).astype(BF16)
        return dot(onehot, hidden)

    local["pproj"].wait()
    proj_t = pproj[...]
    high = proj_t.astype(BF16)
    projs[pl.ds(0, 16), :] = high
    projs[pl.ds(16, 16), :] = (proj_t - high.astype(F32)).astype(BF16)
    lane = lax.broadcasted_iota(jnp.int32, (128, D), 1)
    line = lax.broadcasted_iota(jnp.int32, (128, D), 0)
    line = jnp.where(line >= HEADS, line - HEADS, line) * HEAD
    inside = jnp.logical_and(lane >= line, lane < line + HEAD)
    expand[...] = jnp.where(inside, 1.0, 0.0).astype(BF16)
    lane = lax.broadcasted_iota(jnp.int32, (KEYS, 128), 1)
    for h in range(HEADS):
        ones[pl.ds(h * KEYS, KEYS), :] = jnp.where(
            (lane == h + 48) | (lane == h + 64), 1.0, 0.0
        ).astype(BF16)

    def pair_bias(group, carry):
        tile = pair[pl.ds(group * PAIR_STEP, PAIR_STEP)]
        rows = norm(tile.astype(F32).reshape(PAIR_STEP * KEYS, 128)).astype(BF16)
        both = lax.dot_general(projs[...], rows, NT, preferred_element_type=F32)
        summed = both[:HEADS] + both[HEADS:]
        for i in range(PAIR_STEP):
            bias[pl.ds(group * PAIR_STEP + i, HEADS, stride=ROWS), :] = summed[
                :, i * KEYS : (i + 1) * KEYS
            ]
        return carry

    groups = ROWS // PAIR_STEP
    first = groups // 2
    for copy in pair_copies[: PAIR_CHUNKS // 2]:
        copy.wait()
    lax.fori_loop(0, first, pair_bias, 0)
    pl.semaphore_wait(relay.at[0], 3)
    for peer in around[1:]:
        pl.semaphore_signal(relay.at[1], inc=1, device_id=peer, device_id_type=MESH)

    local["aproj"].wait()
    pooled = pooled_of(packed[pl.ds(0, 128), :], own_ids)
    def pooled_slot(index):
        return pooled_of(abuf[index, :128, :], abuf[index, 128:144, :].astype(F32)[:1, :])

    sends1[1].wait_recv()
    pooled += pooled_slot(1)
    for k in (1, 3, 2):
        sends1[2 * k].wait_recv()
        index = 2 * k + 1
        sends1[index] = remote(
            abuf.at[2 * k], abuf.at[index], send1.at[index], recv1.at[index], sibling
        )
        sends1[index].start()
        pooled += pooled_slot(2 * k)
    for k in (1, 3, 2):
        sends1[2 * k + 1].wait_recv()
        pooled += pooled_slot(2 * k + 1)

    local["single"].wait()
    local["gain"].wait()
    gains = jnp.concatenate([gain[t : t + 1, :] for t in range(D // 128)], axis=1)
    act = (norm(pooled) * gains + single[...].astype(F32)).astype(BF16).astype(F32)
    normed = norm(act).astype(BF16)
    nsend[...] = normed

    slot = lax.rem(r, 2)
    sends2 = [
        remote(nsend, kbuf.at[slot], send2.at[dx], recv2.at[slot], targets[dx])
        for dx in range(4)
    ]
    pl.semaphore_wait(relay.at[1], 3)

    @pl.when(sender)
    def _():
        for copy in (sends2[2], sends2[1], sends2[3]):
            copy.start()

    @pl.when(jnp.logical_and(sender, turn != 0))
    def _():
        sends2[0].start()

    @pl.when(own_keys)
    def _():
        kbuf[slot] = nsend[...]

    act_ref[...] = act
    local["wq"].wait()
    query = dot(normed, wq[...]).astype(BF16)
    for t in range(TILES):
        for n, h in enumerate(heads_of(t)):
            qmask[pl.ds((FIRST_OF[t] + n) * ROWS, ROWS), :] = jnp.where(
                in_head(t, h), query[:, t * 128 : t * 128 + 128], 0.0
            ).astype(BF16)
    own_rows = pl.ds(pl.multiple_of(core * HALF, HALF), HALF)
    other_rows = pl.ds(pl.multiple_of(HALF - core * HALF, HALF), HALF)
    local["wg"].wait()
    gate = jax.nn.sigmoid(dot(nsend[own_rows, :], wg[...]))
    for copy in pair_copies[PAIR_CHUNKS // 2 :]:
        copy.wait()
    lax.fori_loop(first, groups, pair_bias, 0)
    local["mask"].wait()
    masking = jnp.where(mask[pl.ds(c, 1), :] == 1, 0.0, -1000000000.0).astype(F32)
    local["wk"].wait()
    local["wv"].wait()

    for block in range(2):
        own_block = jnp.logical_and(own_keys, slot == block)

        @pl.when(jnp.logical_not(own_block))
        def _():
            remote(
                nsend, kbuf.at[block], send2.at[0], recv2.at[block], targets[1]
            ).wait_recv()

    keys_in = kbuf[...].reshape(KEYS, D)
    key = dot(keys_in, wk[...]).astype(BF16)
    value = dot(keys_in, wv[...]).astype(BF16)

    scores = [None] * HEADS
    for t in range(TILES):
        heads = heads_of(t)
        terms = lax.dot_general(
            qmask[pl.ds(FIRST_OF[t] * ROWS, len(heads) * ROWS), :],
            key[:, t * 128 : t * 128 + 128],
            NT,
            preferred_element_type=F32,
        )
        for n, h in enumerate(heads):
            term = terms[n * ROWS : (n + 1) * ROWS]
            scores[h] = term if scores[h] is None else scores[h] + term
    scores = [
        score * (1.0 / HEAD**0.5) + bias[pl.ds(h * ROWS, ROWS), :] + masking
        for h, score in enumerate(scores)
    ]
    tops = [jnp.max(score, axis=-1, keepdims=True) for score in scores]
    expos = [jnp.exp(score - top).astype(BF16) for score, top in zip(scores, tops)]
    for t in range(TILES):
        heads = heads_of(t)
        v_tile = value[:, t * 128 : t * 128 + 128]
        part = dot(
            jnp.concatenate([expos[h] for h in heads], axis=1),
            jnp.concatenate(
                [jnp.where(in_head(t, h), v_tile, 0.0).astype(BF16) for h in heads], axis=0
            ),
        )
        psend[:, pl.ds(t * 128, 128)] = part.astype(BF16)
    stats = dot(jnp.concatenate(expos, axis=1), ones[...])
    lanes = lane_ids()
    for h, top in enumerate(tops):
        stats = jnp.where((lanes == h) | (lanes == h + 16) | (lanes == h + 32), top, stats)
    psend[:, pl.ds(D, 128)] = coded(stats)

    send3 = remote(psend.at[other_rows, :], sbuf, sems3.at[0], sems3.at[1], sibling)
    send3.start()
    own_act = act_ref[own_rows, :]
    for name in ("wo", "wsw", "wdn", "cproj"):
        local[name].wait()
    mine = psend[own_rows, :]
    send3.wait_recv()
    theirs = sbuf[...]
    top_a, total_a = decoded(mine[:, D:])
    top_b, total_b = decoded(theirs[:, D:])
    top = jnp.maximum(top_a, top_b)
    scale_a, scale_b = jnp.exp(top_a - top), jnp.exp(top_b - top)
    total = scale_a * total_a + scale_b * total_b
    wide_a, wide_b = spread([scale_a, scale_b], expand[...])
    merged = wide_a * mine[:, :D].astype(F32) + wide_b * theirs[:, :D].astype(F32)
    top = jnp.where(lanes < HEADS, top, 0.0)
    total = jnp.where(lanes < HEADS, total, 0.0)
    stats = (
        top
        + pltpu.roll(top, 16, 1)
        + pltpu.roll(top, 32, 1)
        + pltpu.roll(total, 48, 1)
        + pltpu.roll(total, 64, 1)
    )
    zsend[:, pl.ds(0, D)] = merged.astype(BF16)
    zsend[:, pl.ds(D, 128)] = coded(stats)
    sends4 = {}
    for k in (2, 1, 3):
        sends4[k] = remote(zsend, zbuf.at[k], send4.at[k], recv4.at[k], around[k])
        sends4[k].start()
    parts, tops, totals = [merged], [top], [total]
    for k in (1, 3, 2):
        sends4[k].wait_recv()
        got = zbuf[k]
        parts.append(got[:, :D].astype(F32))
        other_top, other_total = decoded(got[:, D:])
        tops.append(other_top)
        totals.append(other_total)
    peak = tops[0]
    for top in tops[1:]:
        peak = jnp.maximum(peak, top)
    scales = [jnp.exp(top - peak) for top in tops]
    whole = scales[0] * totals[0]
    for scale, total in zip(scales[1:], totals[1:]):
        whole += scale * total
    wides = spread([scale / whole for scale in scales], expand[...])
    attended = wides[0] * parts[0]
    for wide, part in zip(wides[1:], parts[1:]):
        attended += wide * part

    gated = (gate * attended).astype(BF16)
    updated = (own_act + dot(gated, wo[...])).astype(BF16).astype(F32)
    updated_norm = norm(updated).astype(BF16)
    finished = updated
    width = 512
    down = jnp.zeros((HALF, D), F32)
    for step in range(FF_TOK // width):
        g = dot(updated_norm, wsw[:, step * width : (step + 1) * width])
        u = dot(updated_norm, wsw[:, FF_TOK + step * width : FF_TOK + (step + 1) * width])
        mid = (jax.nn.silu(g) * u).astype(BF16)
        down += dot(mid, wdn[step * width : (step + 1) * width, :])
    finished = (updated + down).astype(BF16).astype(F32)
    cond = dot(norm(finished).astype(BF16), cproj[...])
    obuf[own_rows, pl.ds(0, D)] = finished.astype(BF16)
    obuf[own_rows, pl.ds(D, 128)] = cond.astype(BF16)

    send5 = remote(
        obuf.at[own_rows, :], done_hbm.at[own_rows, :], sems3.at[2], sems3.at[3], sibling
    )
    send5.start()
    store_own = pltpu.make_async_copy(
        obuf.at[own_rows, :], done_hbm.at[own_rows, :], lsem.at[15]
    )
    store_own.start()
    remote(
        obuf.at[other_rows, :], done_hbm.at[other_rows, :], sems3.at[2], sems3.at[3], sibling
    ).wait_recv()

    for copy in sends1.values():
        copy.wait_send()

    @pl.when(sender)
    def _():
        for copy in sends2[1:]:
            copy.wait_send()

    @pl.when(jnp.logical_and(sender, turn != 0))
    def _():
        sends2[0].wait_send()

    send3.wait_send()
    for copy in sends4.values():
        copy.wait_send()
    send5.wait_send()
    store_own.wait()


def atoms_kernel(
    done_hbm,
    atom_hbm,
    ids_hbm,
    asw_hbm,
    adn_hbm,
    out_tok,
    out_atom,
    done,
    atom,
    ids,
    asw,
    adn,
    result,
    sems,
):
    pairs = ((ids_hbm, ids), (done_hbm, done), (atom_hbm, atom), (asw_hbm, asw), (adn_hbm, adn))
    copies = [
        pltpu.make_async_copy(src, dst, sems.at[n]) for n, (src, dst) in enumerate(pairs)
    ]
    for copy in copies:
        copy.start()
    row_start = lax.axis_index("row") * ROWS
    copies[0].wait()
    token_iota = lax.broadcasted_iota(jnp.int32, (ROWS, 128), 0) + row_start
    onehot_t = jnp.transpose(jnp.where(token_iota == ids[...], 1.0, 0.0)).astype(BF16)
    copies[1].wait()
    store_tok = pltpu.make_async_copy(done.at[:, pl.ds(0, D)], out_tok, sems.at[5])
    store_tok.start()
    for copy in copies[2:]:
        copy.wait()
    resid = atom[...].astype(F32) + dot(onehot_t, done[:, pl.ds(D, 128)])
    both = dot(norm(resid).astype(BF16), asw[...])
    mid = (jax.nn.silu(both[:, :FF_ATOM]) * both[:, FF_ATOM:]).astype(BF16)
    result[...] = (resid + dot(mid, adn[...])).astype(BF16)
    store_atom = pltpu.make_async_copy(result, out_atom, sems.at[6])
    store_atom.start()
    store_tok.wait()
    store_atom.wait()


def local_step(
    atom_single,
    atom_token,
    token_single,
    token_mask,
    pair,
    atom_proj,
    pool_gain,
    w_query,
    w_key,
    w_value,
    w_gate,
    w_out,
    pair_proj,
    w_swiglu,
    w_down,
    cond_proj,
    atom_swiglu,
    atom_down,
):
    ids = atom_token.reshape(1, 128)
    args = (
        atom_single,
        ids,
        token_single,
        token_mask.reshape(COLS, KEYS),
        pair,
        atom_proj,
        pool_gain.reshape(D // 128, 128),
        w_query,
        w_key,
        w_value,
        w_gate,
        w_out,
        pair_proj.T,
        w_swiglu,
        w_down,
        cond_proj,
    )
    vmem = pltpu.VMEM
    dma = pltpu.SemaphoreType.DMA
    scratch = [
        vmem((144, 128), BF16),
        vmem((1, 128), jnp.int32),
        vmem((ROWS, D), BF16),
        vmem((COLS, KEYS), jnp.int32),
        vmem((ROWS, KEYS, 128), BF16),
        vmem((128, D), BF16),
        vmem((D // 128, 128), F32),
        vmem((D, D), BF16),
        vmem((D, D), BF16),
        vmem((D, D), BF16),
        vmem((D, D), BF16),
        vmem((D, D), BF16),
        vmem((HEADS, 128), F32),
        vmem((D, 2 * FF_TOK), BF16),
        vmem((FF_TOK, D), BF16),
        vmem((D, 128), BF16),
        vmem((HEADS * ROWS, KEYS), F32),
        vmem((2 * HEADS, 128), BF16),
        vmem((128, D), BF16),
        vmem((COLS, 144, 128), BF16),
        vmem((HEADS * KEYS, 128), BF16),
        vmem((ROWS, D), F32),
        vmem((PLACES * ROWS, 128), BF16),
        vmem((ROWS, D), BF16),
        vmem((2, ROWS, D), BF16),
        vmem((ROWS, WIDE), BF16),
        vmem((HALF, WIDE), BF16),
        vmem((HALF, WIDE), BF16),
        vmem((4, HALF, WIDE), BF16),
        vmem((ROWS, WIDE), BF16),
        dma((17,)),
        dma((PAIR_CHUNKS,)),
        dma((COLS,)),
        dma((COLS,)),
        pltpu.SemaphoreType.REGULAR((2,)),
        dma((4,)),
        dma((2,)),
        dma((4,)),
        dma((4,)),
        dma((4,)),
    ]
    anywhere = pl.BlockSpec(memory_space=pl.ANY)
    limit = 60 * 1024 * 1024
    done = pl.pallas_call(
        kernel,
        out_shape=jax.ShapeDtypeStruct((ROWS, WIDE), BF16),
        in_specs=[anywhere] * len(args),
        out_specs=anywhere,
        scratch_shapes=scratch,
        compiler_params=pltpu.CompilerParams(
            collective_id=0, has_side_effects=True, vmem_limit_bytes=limit
        ),
        name="step",
    )(*args)
    return pl.pallas_call(
        atoms_kernel,
        out_shape=(
            jax.ShapeDtypeStruct((ROWS, D), BF16),
            jax.ShapeDtypeStruct((128, 128), BF16),
        ),
        in_specs=[anywhere] * 5,
        out_specs=(anywhere, anywhere),
        scratch_shapes=[
            vmem((ROWS, WIDE), BF16),
            vmem((128, 128), BF16),
            vmem((1, 128), jnp.int32),
            vmem((128, 2 * FF_ATOM), BF16),
            vmem((FF_ATOM, 128), BF16),
            vmem((128, 128), BF16),
            dma((7,)),
        ],
        compiler_params=pltpu.CompilerParams(vmem_limit_bytes=limit),
        name="atoms",
    )(done, atom_single, ids, atom_swiglu, atom_down)


def solution(mesh):
    split = P(("row", "col"), None)
    placed = (
        split,
        P(("row", "col")),
        P(),
        P(),
        P("row", "col", None),
    ) + (P(),) * 13
    return jax.shard_map(
        local_step,
        mesh=mesh,
        in_specs=placed,
        out_specs=(P("row", None), split),
        check_vma=False,
    )
```

```python
import jax
import jax.numpy as jnp
from jax import lax
from jax.experimental import pallas as pl
from jax.experimental.pallas import tpu as pltpu
from jax.sharding import PartitionSpec as P

MESH = pl.DeviceIdType.MESH
F32 = jnp.float32
BF16 = jnp.bfloat16

D = 768
HEADS = 16
HEAD = 48
FF_TOK = 1536
FF_ATOM = 256
ROWS = 64
KEYS = 128
COLS = 8
HALF = ROWS // 2
PAIR_STEP = 8
WIDE = D + 128
TILES = D // 128
PAIR_CHUNKS = 4

NT = (((1,), (1,)), ((), ()))


def norm(values):
    mean = jnp.mean(values, axis=-1, keepdims=True)
    centered = values - mean
    var = jnp.mean(centered * centered, axis=-1, keepdims=True)
    return centered * lax.rsqrt(var + 1e-05)


def dot(a, b):
    return jnp.dot(a, b, preferred_element_type=F32)


def heads_of(tile):
    return [
        h for h in range(HEADS) if h * HEAD < (tile + 1) * 128 and (h + 1) * HEAD > tile * 128
    ]


FIRST_OF = [sum(len(heads_of(before)) for before in range(tile)) for tile in range(TILES)]
PLACES = FIRST_OF[-1] + len(heads_of(TILES - 1))


def lane_ids():
    return lax.broadcasted_iota(jnp.int32, (1, 128), 1)


def in_head(tile, h):
    lanes = lane_ids()
    return (lanes >= h * HEAD - tile * 128) & (lanes < (h + 1) * HEAD - tile * 128)


def coded(stats):
    lanes = lane_ids()
    piece0 = stats.astype(BF16).astype(F32)
    rest = stats - piece0
    piece1 = rest.astype(BF16).astype(F32)
    piece2 = (rest - piece1).astype(BF16).astype(F32)
    use0 = (lanes < 16) | ((lanes >= 48) & (lanes < 64))
    use1 = ((lanes >= 16) & (lanes < 32)) | (lanes >= 64)
    return jnp.where(use0, piece0, jnp.where(use1, piece1, piece2)).astype(BF16)


def decoded(line):
    line = line.astype(F32)
    top = line + pltpu.roll(line, 112, 1) + pltpu.roll(line, 96, 1)
    total = pltpu.roll(line, 80, 1) + pltpu.roll(line, 64, 1)
    return top, total


def spread(scales, expand):
    lanes = lane_ids()
    pieces = []
    for scale in scales:
        scale = jnp.where(lanes < HEADS, scale, 0.0)
        upper = scale.astype(BF16).astype(F32)
        pieces.append(upper + pltpu.roll(scale - upper, 16, 1))
    wide = dot(jnp.concatenate(pieces, axis=0).astype(BF16), expand)
    rows = scales[0].shape[0]
    return [wide[i * rows : (i + 1) * rows] for i in range(len(scales))]


def kernel(
    atom_hbm,
    ids_hbm,
    single_hbm,
    mask_hbm,
    pair_hbm,
    aproj_hbm,
    gain_hbm,
    wq_hbm,
    wk_hbm,
    wv_hbm,
    wg_hbm,
    wo_hbm,
    pproj_hbm,
    wsw_hbm,
    wdn_hbm,
    cproj_hbm,
    tok_hbm,
    cond_hbm,
    packed,
    ids,
    single,
    mask,
    pair,
    aproj,
    gain,
    wq,
    wk,
    wv,
    wg,
    wo,
    pproj,
    wsw,
    wdn,
    cproj,
    bias,
    projs,
    expand,
    abuf,
    ones,
    act_ref,
    qmask,
    nsend,
    kbuf,
    psend,
    sbuf,
    zsend,
    zbuf,
    obuf,
    cbuf,
    lsem,
    psem,
    send1,
    recv1,
    relay,
    send2,
    recv2,
    sems3,
    send4,
    recv4,
):
    r = lax.axis_index("row")
    c = lax.axis_index("col")
    x, y = lax.div(r, 4), lax.rem(r, 4)
    z, core = lax.div(c, 2), lax.rem(c, 2)
    turn = lax.rem(z - x + 4, 4)

    home = lax.div(y, 2)
    sender = core == home
    targets = []
    for dx in range(4):
        tx, ty = lax.rem(x + dx, 4), lax.rem(y + dx + turn, 4)
        targets.append((tx * 4 + ty, lax.div(r, 2)))
    own_keys = jnp.logical_and(sender, turn == 0)

    sibling = (r, c + 1 - 2 * core)
    around = [None] + [(r, lax.rem(c + 2 * k, COLS)) for k in range(1, 4)]
    along_x = [(lax.rem(x + k, 4) * 4 + y, c) for k in range(1, 4)]
    along_y = [(x * 4 + lax.rem(y + k, 4), c) for k in range(1, 4)]

    barrier = pltpu.get_barrier_semaphore()
    for peer in around[1:] + [sibling] + along_x + along_y:
        pl.semaphore_signal(barrier, inc=1, device_id=peer, device_id_type=MESH)

    local = {}

    def fetch(name, index, src, dst):
        copy = pltpu.make_async_copy(src, dst, lsem.at[index])
        copy.start()
        local[name] = copy

    fetch("atom", 0, atom_hbm, packed.at[pl.ds(0, 128), :])
    fetch("ids", 1, ids_hbm, ids)
    fetch("aproj", 2, aproj_hbm, aproj)
    fetch("pproj", 3, pproj_hbm, pproj)
    pair_copies = []
    span = ROWS // PAIR_CHUNKS
    for chunk in range(PAIR_CHUNKS):
        part = pl.ds(chunk * span, span)
        copy = pltpu.make_async_copy(pair_hbm.at[part], pair.at[part], psem.at[chunk])
        copy.start()
        pair_copies.append(copy)
    fetch("single", 4, single_hbm.at[pl.ds(pl.multiple_of(r * ROWS, ROWS), ROWS), :], single)
    fetch("gain", 5, gain_hbm, gain)
    fetch("mask", 6, mask_hbm, mask)
    fetch("wq", 7, wq_hbm, wq)
    fetch("wk", 8, wk_hbm, wk)
    fetch("wv", 9, wv_hbm, wv)
    fetch("wg", 10, wg_hbm, wg)
    fetch("wo", 11, wo_hbm, wo)
    fetch("wsw", 12, wsw_hbm, wsw)
    fetch("wdn", 13, wdn_hbm, wdn)
    fetch("cproj", 14, cproj_hbm, cproj)

    local["ids"].wait()
    own_ids = (ids[...] - r * ROWS).astype(F32)
    packed[pl.ds(128, 16), :] = jnp.broadcast_to(own_ids, (16, 128)).astype(BF16)
    local["atom"].wait()
    pl.semaphore_wait(barrier, 10)

    def remote(src, dst, send, recv, device):
        return pltpu.make_async_remote_copy(
            src_ref=src,
            dst_ref=dst,
            send_sem=send,
            recv_sem=recv,
            device_id=device,
            device_id_type=MESH,
        )

    sends1 = {}
    for k in (2, 1, 3):
        sends1[2 * k] = remote(packed, abuf.at[2 * k], send1.at[2 * k], recv1.at[2 * k], around[k])
    sends1[1] = remote(packed, abuf.at[1], send1.at[1], recv1.at[1], sibling)
    for copy in sends1.values():
        copy.start()
    for peer in along_x:
        pl.semaphore_signal(relay.at[0], inc=1, device_id=peer, device_id_type=MESH)

    token_iota = lax.broadcasted_iota(jnp.int32, (ROWS, 128), 0).astype(F32)

    def pooled_of(atoms, id_row):
        hidden = jnp.maximum(dot(atoms, aproj[...]), 0.0).astype(BF16)
        onehot = jnp.where(token_iota == id_row, 1.0, 0.0).astype(BF16)
        return dot(onehot, hidden)

    local["pproj"].wait()
    proj_t = pproj[...]
    high = proj_t.astype(BF16)
    projs[pl.ds(0, 16), :] = high
    projs[pl.ds(16, 16), :] = (proj_t - high.astype(F32)).astype(BF16)
    lane = lax.broadcasted_iota(jnp.int32, (128, D), 1)
    line = lax.broadcasted_iota(jnp.int32, (128, D), 0)
    line = jnp.where(line >= HEADS, line - HEADS, line) * HEAD
    inside = jnp.logical_and(lane >= line, lane < line + HEAD)
    expand[...] = jnp.where(inside, 1.0, 0.0).astype(BF16)
    lane = lax.broadcasted_iota(jnp.int32, (KEYS, 128), 1)
    for h in range(HEADS):
        ones[pl.ds(h * KEYS, KEYS), :] = jnp.where(
            (lane == h + 48) | (lane == h + 64), 1.0, 0.0
        ).astype(BF16)

    def pair_bias(group, carry):
        tile = pair[pl.ds(group * PAIR_STEP, PAIR_STEP)]
        rows = norm(tile.astype(F32).reshape(PAIR_STEP * KEYS, 128)).astype(BF16)
        both = lax.dot_general(projs[...], rows, NT, preferred_element_type=F32)
        summed = both[:HEADS] + both[HEADS:]
        for i in range(PAIR_STEP):
            bias[pl.ds(group * PAIR_STEP + i, HEADS, stride=ROWS), :] = summed[
                :, i * KEYS : (i + 1) * KEYS
            ]
        return carry

    groups = ROWS // PAIR_STEP
    first = 3
    for copy in pair_copies[:2]:
        copy.wait()
    lax.fori_loop(0, first, pair_bias, 0)
    pl.semaphore_wait(relay.at[0], 3)
    for peer in around[1:]:
        pl.semaphore_signal(relay.at[1], inc=1, device_id=peer, device_id_type=MESH)

    local["aproj"].wait()
    pooled = pooled_of(packed[pl.ds(0, 128), :], own_ids)
    def pooled_slot(index):
        return pooled_of(abuf[index, :128, :], abuf[index, 128:144, :].astype(F32)[:1, :])

    sends1[1].wait_recv()
    pooled += pooled_slot(1)
    for k in (1, 3, 2):
        sends1[2 * k].wait_recv()
        index = 2 * k + 1
        sends1[index] = remote(
            abuf.at[2 * k], abuf.at[index], send1.at[index], recv1.at[index], sibling
        )
        sends1[index].start()
        pooled += pooled_slot(2 * k)
    for k in (1, 3, 2):
        sends1[2 * k + 1].wait_recv()
        pooled += pooled_slot(2 * k + 1)

    local["single"].wait()
    local["gain"].wait()
    gains = jnp.concatenate([gain[t : t + 1, :] for t in range(D // 128)], axis=1)
    act = (norm(pooled) * gains + single[...].astype(F32)).astype(BF16).astype(F32)
    normed = norm(act).astype(BF16)
    nsend[...] = normed

    slot = lax.rem(r, 2)
    sends2 = [
        remote(nsend, kbuf.at[slot], send2.at[dx], recv2.at[slot], targets[dx])
        for dx in range(4)
    ]
    pl.semaphore_wait(relay.at[1], 3)

    @pl.when(sender)
    def _():
        for copy in (sends2[2], sends2[1], sends2[3]):
            copy.start()

    @pl.when(jnp.logical_and(sender, turn != 0))
    def _():
        sends2[0].start()

    @pl.when(own_keys)
    def _():
        kbuf[slot] = nsend[...]

    act_ref[...] = act
    local["wq"].wait()
    query = dot(normed, wq[...]).astype(BF16)
    for t in range(TILES):
        for n, h in enumerate(heads_of(t)):
            qmask[pl.ds((FIRST_OF[t] + n) * ROWS, ROWS), :] = jnp.where(
                in_head(t, h), query[:, t * 128 : t * 128 + 128], 0.0
            ).astype(BF16)
    own_rows = pl.ds(pl.multiple_of(core * HALF, HALF), HALF)
    other_rows = pl.ds(pl.multiple_of(HALF - core * HALF, HALF), HALF)
    local["wg"].wait()
    gate = jax.nn.sigmoid(dot(nsend[own_rows, :], wg[...]))
    for copy in pair_copies[2:]:
        copy.wait()
    lax.fori_loop(first, groups, pair_bias, 0)
    local["mask"].wait()
    masking = jnp.where(mask[pl.ds(c, 1), :] == 1, 0.0, -1000000000.0).astype(F32)
    local["wk"].wait()
    local["wv"].wait()

    for block in range(2):
        own_block = jnp.logical_and(own_keys, slot == block)

        @pl.when(jnp.logical_not(own_block))
        def _():
            remote(
                nsend, kbuf.at[block], send2.at[0], recv2.at[block], targets[1]
            ).wait_recv()

    keys_in = kbuf[...].reshape(KEYS, D)
    key = dot(keys_in, wk[...]).astype(BF16)
    value = dot(keys_in, wv[...]).astype(BF16)

    scores = [None] * HEADS
    for t in range(TILES):
        heads = heads_of(t)
        terms = lax.dot_general(
            qmask[pl.ds(FIRST_OF[t] * ROWS, len(heads) * ROWS), :],
            key[:, t * 128 : t * 128 + 128],
            NT,
            preferred_element_type=F32,
        )
        for n, h in enumerate(heads):
            term = terms[n * ROWS : (n + 1) * ROWS]
            scores[h] = term if scores[h] is None else scores[h] + term
    scores = [
        score * (1.0 / HEAD**0.5) + bias[pl.ds(h * ROWS, ROWS), :] + masking
        for h, score in enumerate(scores)
    ]
    tops = [jnp.max(score, axis=-1, keepdims=True) for score in scores]
    expos = [jnp.exp(score - top).astype(BF16) for score, top in zip(scores, tops)]
    for t in range(TILES):
        heads = heads_of(t)
        v_tile = value[:, t * 128 : t * 128 + 128]
        part = dot(
            jnp.concatenate([expos[h] for h in heads], axis=1),
            jnp.concatenate(
                [jnp.where(in_head(t, h), v_tile, 0.0).astype(BF16) for h in heads], axis=0
            ),
        )
        psend[:, pl.ds(t * 128, 128)] = part.astype(BF16)
    stats = dot(jnp.concatenate(expos, axis=1), ones[...])
    lanes = lane_ids()
    for h, top in enumerate(tops):
        stats = jnp.where((lanes == h) | (lanes == h + 16) | (lanes == h + 32), top, stats)
    psend[:, pl.ds(D, 128)] = coded(stats)

    send3 = remote(psend.at[other_rows, :], sbuf, sems3.at[0], sems3.at[1], sibling)
    send3.start()
    own_act = act_ref[own_rows, :]
    for name in ("wo", "wsw", "wdn", "cproj"):
        local[name].wait()
    mine = psend[own_rows, :]
    send3.wait_recv()
    theirs = sbuf[...]
    top_a, total_a = decoded(mine[:, D:])
    top_b, total_b = decoded(theirs[:, D:])
    top = jnp.maximum(top_a, top_b)
    scale_a, scale_b = jnp.exp(top_a - top), jnp.exp(top_b - top)
    total = scale_a * total_a + scale_b * total_b
    wide_a, wide_b = spread([scale_a, scale_b], expand[...])
    merged = wide_a * mine[:, :D].astype(F32) + wide_b * theirs[:, :D].astype(F32)
    top = jnp.where(lanes < HEADS, top, 0.0)
    total = jnp.where(lanes < HEADS, total, 0.0)
    stats = (
        top
        + pltpu.roll(top, 16, 1)
        + pltpu.roll(top, 32, 1)
        + pltpu.roll(total, 48, 1)
        + pltpu.roll(total, 64, 1)
    )
    zsend[:, pl.ds(0, D)] = merged.astype(BF16)
    zsend[:, pl.ds(D, 128)] = coded(stats)
    sends4 = {}
    for k in (2, 1, 3):
        sends4[k] = remote(zsend, zbuf.at[k], send4.at[k], recv4.at[k], around[k])
        sends4[k].start()
    parts, tops, totals = [merged], [top], [total]
    for k in (1, 3, 2):
        sends4[k].wait_recv()
        got = zbuf[k]
        parts.append(got[:, :D].astype(F32))
        other_top, other_total = decoded(got[:, D:])
        tops.append(other_top)
        totals.append(other_total)
    peak = tops[0]
    for top in tops[1:]:
        peak = jnp.maximum(peak, top)
    scales = [jnp.exp(top - peak) for top in tops]
    whole = scales[0] * totals[0]
    for scale, total in zip(scales[1:], totals[1:]):
        whole += scale * total
    wides = spread([scale / whole for scale in scales], expand[...])
    attended = wides[0] * parts[0]
    for wide, part in zip(wides[1:], parts[1:]):
        attended += wide * part

    gated = (gate * attended).astype(BF16)
    updated = (own_act + dot(gated, wo[...])).astype(BF16).astype(F32)
    updated_norm = norm(updated).astype(BF16)
    finished = updated
    width = 512
    down = jnp.zeros((HALF, D), F32)
    for step in range(FF_TOK // width):
        g = dot(updated_norm, wsw[:, step * width : (step + 1) * width])
        u = dot(updated_norm, wsw[:, FF_TOK + step * width : FF_TOK + (step + 1) * width])
        mid = (jax.nn.silu(g) * u).astype(BF16)
        down += dot(mid, wdn[step * width : (step + 1) * width, :])
    finished = (updated + down).astype(BF16).astype(F32)
    obuf[own_rows, :] = finished.astype(BF16)

    send5 = remote(
        obuf.at[own_rows, :], tok_hbm.at[own_rows, :], sems3.at[2], sems3.at[3], sibling
    )
    send5.start()
    cond = dot(norm(finished).astype(BF16), cproj[...])
    cbuf[own_rows, :] = cond.astype(BF16)
    send6 = remote(
        cbuf.at[own_rows, :], cond_hbm.at[own_rows, :], sems3.at[4], sems3.at[5], sibling
    )
    send6.start()
    store_tok = pltpu.make_async_copy(
        obuf.at[own_rows, :], tok_hbm.at[own_rows, :], lsem.at[15]
    )
    store_tok.start()
    store_cond = pltpu.make_async_copy(
        cbuf.at[own_rows, :], cond_hbm.at[own_rows, :], lsem.at[16]
    )
    store_cond.start()
    remote(
        obuf.at[other_rows, :], tok_hbm.at[other_rows, :], sems3.at[2], sems3.at[3], sibling
    ).wait_recv()
    remote(
        cbuf.at[other_rows, :], cond_hbm.at[other_rows, :], sems3.at[4], sems3.at[5], sibling
    ).wait_recv()

    for copy in sends1.values():
        copy.wait_send()

    @pl.when(sender)
    def _():
        for copy in sends2[1:]:
            copy.wait_send()

    @pl.when(jnp.logical_and(sender, turn != 0))
    def _():
        sends2[0].wait_send()

    send3.wait_send()
    for copy in sends4.values():
        copy.wait_send()
    send5.wait_send()
    send6.wait_send()
    store_tok.wait()
    store_cond.wait()


def atoms_kernel(
    tok_hbm,
    cond_hbm,
    atom_hbm,
    ids_hbm,
    asw_hbm,
    adn_hbm,
    out_tok,
    out_atom,
    tok,
    cond,
    atom,
    ids,
    asw,
    adn,
    result,
    sems,
):
    pairs = (
        (ids_hbm, ids),
        (tok_hbm, tok),
        (cond_hbm, cond),
        (atom_hbm, atom),
        (asw_hbm, asw),
        (adn_hbm, adn),
    )
    copies = [
        pltpu.make_async_copy(src, dst, sems.at[n]) for n, (src, dst) in enumerate(pairs)
    ]
    for copy in copies:
        copy.start()
    row_start = lax.axis_index("row") * ROWS
    copies[0].wait()
    token_iota = lax.broadcasted_iota(jnp.int32, (ROWS, 128), 0) + row_start
    onehot_t = jnp.transpose(jnp.where(token_iota == ids[...], 1.0, 0.0)).astype(BF16)
    copies[1].wait()
    store_tok = pltpu.make_async_copy(tok, out_tok, sems.at[6])
    store_tok.start()
    for copy in copies[2:]:
        copy.wait()
    resid = atom[...].astype(F32) + dot(onehot_t, cond[...])
    both = dot(norm(resid).astype(BF16), asw[...])
    mid = (jax.nn.silu(both[:, :FF_ATOM]) * both[:, FF_ATOM:]).astype(BF16)
    result[...] = (resid + dot(mid, adn[...])).astype(BF16)
    store_atom = pltpu.make_async_copy(result, out_atom, sems.at[7])
    store_atom.start()
    store_tok.wait()
    store_atom.wait()


def local_step(
    atom_single,
    atom_token,
    token_single,
    token_mask,
    pair,
    atom_proj,
    pool_gain,
    w_query,
    w_key,
    w_value,
    w_gate,
    w_out,
    pair_proj,
    w_swiglu,
    w_down,
    cond_proj,
    atom_swiglu,
    atom_down,
):
    ids = atom_token.reshape(1, 128)
    args = (
        atom_single,
        ids,
        token_single,
        token_mask.reshape(COLS, KEYS),
        pair,
        atom_proj,
        pool_gain.reshape(D // 128, 128),
        w_query,
        w_key,
        w_value,
        w_gate,
        w_out,
        pair_proj.T,
        w_swiglu,
        w_down,
        cond_proj,
    )
    vmem = pltpu.VMEM
    dma = pltpu.SemaphoreType.DMA
    scratch = [
        vmem((144, 128), BF16),
        vmem((1, 128), jnp.int32),
        vmem((ROWS, D), BF16),
        vmem((COLS, KEYS), jnp.int32),
        vmem((ROWS, KEYS, 128), BF16),
        vmem((128, D), BF16),
        vmem((D // 128, 128), F32),
        vmem((D, D), BF16),
        vmem((D, D), BF16),
        vmem((D, D), BF16),
        vmem((D, D), BF16),
        vmem((D, D), BF16),
        vmem((HEADS, 128), F32),
        vmem((D, 2 * FF_TOK), BF16),
        vmem((FF_TOK, D), BF16),
        vmem((D, 128), BF16),
        vmem((HEADS * ROWS, KEYS), F32),
        vmem((2 * HEADS, 128), BF16),
        vmem((128, D), BF16),
        vmem((COLS, 144, 128), BF16),
        vmem((HEADS * KEYS, 128), BF16),
        vmem((ROWS, D), F32),
        vmem((PLACES * ROWS, 128), BF16),
        vmem((ROWS, D), BF16),
        vmem((2, ROWS, D), BF16),
        vmem((ROWS, WIDE), BF16),
        vmem((HALF, WIDE), BF16),
        vmem((HALF, WIDE), BF16),
        vmem((4, HALF, WIDE), BF16),
        vmem((ROWS, D), BF16),
        vmem((ROWS, 128), BF16),
        dma((17,)),
        dma((PAIR_CHUNKS,)),
        dma((COLS,)),
        dma((COLS,)),
        pltpu.SemaphoreType.REGULAR((2,)),
        dma((4,)),
        dma((2,)),
        dma((6,)),
        dma((4,)),
        dma((4,)),
    ]
    anywhere = pl.BlockSpec(memory_space=pl.ANY)
    limit = 60 * 1024 * 1024
    tok, cond = pl.pallas_call(
        kernel,
        out_shape=(
            jax.ShapeDtypeStruct((ROWS, D), BF16),
            jax.ShapeDtypeStruct((ROWS, 128), BF16),
        ),
        in_specs=[anywhere] * len(args),
        out_specs=(anywhere, anywhere),
        scratch_shapes=scratch,
        compiler_params=pltpu.CompilerParams(
            collective_id=0, has_side_effects=True, vmem_limit_bytes=limit
        ),
        name="step",
    )(*args)
    return pl.pallas_call(
        atoms_kernel,
        out_shape=(
            jax.ShapeDtypeStruct((ROWS, D), BF16),
            jax.ShapeDtypeStruct((128, 128), BF16),
        ),
        in_specs=[anywhere] * 6,
        out_specs=(anywhere, anywhere),
        scratch_shapes=[
            vmem((ROWS, D), BF16),
            vmem((ROWS, 128), BF16),
            vmem((128, 128), BF16),
            vmem((1, 128), jnp.int32),
            vmem((128, 2 * FF_ATOM), BF16),
            vmem((FF_ATOM, 128), BF16),
            vmem((128, 128), BF16),
            dma((8,)),
        ],
        compiler_params=pltpu.CompilerParams(vmem_limit_bytes=limit),
        name="atoms",
    )(tok, cond, atom_single, ids, atom_swiglu, atom_down)


def solution(mesh):
    split = P(("row", "col"), None)
    placed = (
        split,
        P(("row", "col")),
        P(),
        P(),
        P("row", "col", None),
    ) + (P(),) * 13
    return jax.shard_map(
        local_step,
        mesh=mesh,
        in_specs=placed,
        out_specs=(P("row", None), split),
        check_vma=False,
    )
```

```python
import jax
import jax.numpy as jnp
from jax import lax
from jax.experimental import pallas as pl
from jax.experimental.pallas import tpu as pltpu
from jax.sharding import PartitionSpec as P

MESH = pl.DeviceIdType.MESH
F32 = jnp.float32
BF16 = jnp.bfloat16

D = 768
HEADS = 16
HEAD = 48
FF_TOK = 1536
FF_ATOM = 256
ROWS = 64
KEYS = 128
COLS = 8
HALF = ROWS // 2
PAIR_STEP = 8
WIDE = D + 128
TILES = D // 128
PAIR_CHUNKS = 4

NT = (((1,), (1,)), ((), ()))


def norm(values):
    mean = jnp.mean(values, axis=-1, keepdims=True)
    centered = values - mean
    var = jnp.mean(centered * centered, axis=-1, keepdims=True)
    return centered * lax.rsqrt(var + 1e-05)


def dot(a, b):
    return jnp.dot(a, b, preferred_element_type=F32)


def heads_of(tile):
    return [
        h for h in range(HEADS) if h * HEAD < (tile + 1) * 128 and (h + 1) * HEAD > tile * 128
    ]


FIRST_OF = [sum(len(heads_of(before)) for before in range(tile)) for tile in range(TILES)]
PLACES = FIRST_OF[-1] + len(heads_of(TILES - 1))


def lane_ids():
    return lax.broadcasted_iota(jnp.int32, (1, 128), 1)


def in_head(tile, h):
    lanes = lane_ids()
    return (lanes >= h * HEAD - tile * 128) & (lanes < (h + 1) * HEAD - tile * 128)


def coded(stats):
    lanes = lane_ids()
    piece0 = stats.astype(BF16).astype(F32)
    rest = stats - piece0
    piece1 = rest.astype(BF16).astype(F32)
    piece2 = (rest - piece1).astype(BF16).astype(F32)
    use0 = (lanes < 16) | ((lanes >= 48) & (lanes < 64))
    use1 = ((lanes >= 16) & (lanes < 32)) | (lanes >= 64)
    return jnp.where(use0, piece0, jnp.where(use1, piece1, piece2)).astype(BF16)


def decoded(line):
    line = line.astype(F32)
    top = line + pltpu.roll(line, 112, 1) + pltpu.roll(line, 96, 1)
    total = pltpu.roll(line, 80, 1) + pltpu.roll(line, 64, 1)
    return top, total


def spread(scales, expand):
    lanes = lane_ids()
    pieces = []
    for scale in scales:
        scale = jnp.where(lanes < HEADS, scale, 0.0)
        upper = scale.astype(BF16).astype(F32)
        pieces.append(upper + pltpu.roll(scale - upper, 16, 1))
    wide = dot(jnp.concatenate(pieces, axis=0).astype(BF16), expand)
    rows = scales[0].shape[0]
    return [wide[i * rows : (i + 1) * rows] for i in range(len(scales))]


def kernel(
    atom_hbm,
    ids_hbm,
    single_hbm,
    mask_hbm,
    pair_hbm,
    aproj_hbm,
    gain_hbm,
    wq_hbm,
    wk_hbm,
    wv_hbm,
    wg_hbm,
    wo_hbm,
    pproj_hbm,
    wsw_hbm,
    wdn_hbm,
    cproj_hbm,
    done_hbm,
    packed,
    ids,
    single,
    mask,
    pair,
    aproj,
    gain,
    wq,
    wk,
    wv,
    wg,
    wo,
    pproj,
    wsw,
    wdn,
    cproj,
    bias,
    projs,
    expand,
    abuf,
    ones,
    act_ref,
    qmask,
    nsend,
    kbuf,
    psend,
    sbuf,
    zsend,
    zbuf,
    obuf,
    lsem,
    psem,
    send1,
    recv1,
    relay,
    send2,
    recv2,
    sems3,
    send4,
    recv4,
):
    r = lax.axis_index("row")
    c = lax.axis_index("col")
    x, y = lax.div(r, 4), lax.rem(r, 4)
    z, core = lax.div(c, 2), lax.rem(c, 2)
    turn = lax.rem(z - x + 4, 4)

    home = lax.div(y, 2)
    sender = core == home
    targets = []
    for dx in range(4):
        tx, ty = lax.rem(x + dx, 4), lax.rem(y + dx + turn, 4)
        targets.append((tx * 4 + ty, lax.div(r, 2)))
    own_keys = jnp.logical_and(sender, turn == 0)

    sibling = (r, c + 1 - 2 * core)
    around = [None] + [(r, lax.rem(c + 2 * k, COLS)) for k in range(1, 4)]
    along_x = [(lax.rem(x + k, 4) * 4 + y, c) for k in range(1, 4)]
    along_y = [(x * 4 + lax.rem(y + k, 4), c) for k in range(1, 4)]

    barrier = pltpu.get_barrier_semaphore()
    for peer in around[1:] + [sibling] + along_x + along_y:
        pl.semaphore_signal(barrier, inc=1, device_id=peer, device_id_type=MESH)

    local = {}

    def fetch(name, index, src, dst):
        copy = pltpu.make_async_copy(src, dst, lsem.at[index])
        copy.start()
        local[name] = copy

    fetch("atom", 0, atom_hbm, packed.at[pl.ds(0, 128), :])
    fetch("ids", 1, ids_hbm, ids)
    fetch("aproj", 2, aproj_hbm, aproj)
    fetch("pproj", 3, pproj_hbm, pproj)
    pair_copies = []
    span = ROWS // PAIR_CHUNKS
    for chunk in range(PAIR_CHUNKS):
        part = pl.ds(chunk * span, span)
        copy = pltpu.make_async_copy(pair_hbm.at[part], pair.at[part], psem.at[chunk])
        copy.start()
        pair_copies.append(copy)
    fetch("single", 4, single_hbm.at[pl.ds(pl.multiple_of(r * ROWS, ROWS), ROWS), :], single)
    fetch("gain", 5, gain_hbm, gain)
    fetch("mask", 6, mask_hbm, mask)
    fetch("wq", 7, wq_hbm, wq)
    fetch("wk", 8, wk_hbm, wk)
    fetch("wv", 9, wv_hbm, wv)
    fetch("wg", 10, wg_hbm, wg)
    fetch("wo", 11, wo_hbm, wo)
    fetch("wsw", 12, wsw_hbm, wsw)
    fetch("wdn", 13, wdn_hbm, wdn)
    fetch("cproj", 14, cproj_hbm, cproj)

    local["ids"].wait()
    own_ids = (ids[...] - r * ROWS).astype(F32)
    packed[pl.ds(128, 16), :] = jnp.broadcast_to(own_ids, (16, 128)).astype(BF16)
    local["atom"].wait()
    pl.semaphore_wait(barrier, 10)

    def remote(src, dst, send, recv, device):
        return pltpu.make_async_remote_copy(
            src_ref=src,
            dst_ref=dst,
            send_sem=send,
            recv_sem=recv,
            device_id=device,
            device_id_type=MESH,
        )

    sends1 = {}
    for k in (2, 1, 3):
        sends1[2 * k] = remote(packed, abuf.at[2 * k], send1.at[2 * k], recv1.at[2 * k], around[k])
    sends1[1] = remote(packed, abuf.at[1], send1.at[1], recv1.at[1], sibling)
    for copy in sends1.values():
        copy.start()
    for peer in along_x:
        pl.semaphore_signal(relay.at[0], inc=1, device_id=peer, device_id_type=MESH)

    token_iota = lax.broadcasted_iota(jnp.int32, (ROWS, 128), 0).astype(F32)

    def pooled_of(atoms, id_row):
        hidden = jnp.maximum(dot(atoms, aproj[...]), 0.0).astype(BF16)
        onehot = jnp.where(token_iota == id_row, 1.0, 0.0).astype(BF16)
        return dot(onehot, hidden)

    local["pproj"].wait()
    proj_t = pproj[...]
    high = proj_t.astype(BF16)
    projs[pl.ds(0, 16), :] = high
    projs[pl.ds(16, 16), :] = (proj_t - high.astype(F32)).astype(BF16)
    lane = lax.broadcasted_iota(jnp.int32, (128, D), 1)
    line = lax.broadcasted_iota(jnp.int32, (128, D), 0)
    line = jnp.where(line >= HEADS, line - HEADS, line) * HEAD
    inside = jnp.logical_and(lane >= line, lane < line + HEAD)
    expand[...] = jnp.where(inside, 1.0, 0.0).astype(BF16)
    lane = lax.broadcasted_iota(jnp.int32, (KEYS, 128), 1)
    for h in range(HEADS):
        ones[pl.ds(h * KEYS, KEYS), :] = jnp.where(
            (lane == h + 48) | (lane == h + 64), 1.0, 0.0
        ).astype(BF16)

    def pair_bias(group, carry):
        tile = pair[pl.ds(group * PAIR_STEP, PAIR_STEP)]
        rows = norm(tile.astype(F32).reshape(PAIR_STEP * KEYS, 128)).astype(BF16)
        both = lax.dot_general(projs[...], rows, NT, preferred_element_type=F32)
        summed = both[:HEADS] + both[HEADS:]
        for i in range(PAIR_STEP):
            bias[pl.ds(group * PAIR_STEP + i, HEADS, stride=ROWS), :] = summed[
                :, i * KEYS : (i + 1) * KEYS
            ]
        return carry

    groups = ROWS // PAIR_STEP
    first = groups // 2
    for copy in pair_copies[: PAIR_CHUNKS // 2]:
        copy.wait()
    lax.fori_loop(0, first, pair_bias, 0)
    pl.semaphore_wait(relay.at[0], 3)
    for peer in around[1:]:
        pl.semaphore_signal(relay.at[1], inc=1, device_id=peer, device_id_type=MESH)

    local["aproj"].wait()
    pooled = pooled_of(packed[pl.ds(0, 128), :], own_ids)
    def pooled_slot(index):
        return pooled_of(abuf[index, :128, :], abuf[index, 128:144, :].astype(F32)[:1, :])

    sends1[1].wait_recv()
    pooled += pooled_slot(1)
    for k in (1, 3, 2):
        sends1[2 * k].wait_recv()
        index = 2 * k + 1
        sends1[index] = remote(
            abuf.at[2 * k], abuf.at[index], send1.at[index], recv1.at[index], sibling
        )
        sends1[index].start()
        pooled += pooled_slot(2 * k)
    for k in (1, 3, 2):
        sends1[2 * k + 1].wait_recv()
        pooled += pooled_slot(2 * k + 1)

    local["single"].wait()
    local["gain"].wait()
    gains = jnp.concatenate([gain[t : t + 1, :] for t in range(D // 128)], axis=1)
    act = (norm(pooled) * gains + single[...].astype(F32)).astype(BF16).astype(F32)
    normed = norm(act).astype(BF16)
    nsend[...] = normed

    slot = lax.rem(r, 2)
    sends2 = [
        remote(nsend, kbuf.at[slot], send2.at[dx], recv2.at[slot], targets[dx])
        for dx in range(4)
    ]
    pl.semaphore_wait(relay.at[1], 3)

    @pl.when(sender)
    def _():
        for copy in (sends2[2], sends2[1], sends2[3]):
            copy.start()

    @pl.when(jnp.logical_and(sender, turn != 0))
    def _():
        sends2[0].start()

    @pl.when(own_keys)
    def _():
        kbuf[slot] = nsend[...]

    act_ref[...] = act
    local["wq"].wait()
    query = dot(normed, wq[...]).astype(BF16)
    for t in range(TILES):
        for n, h in enumerate(heads_of(t)):
            qmask[pl.ds((FIRST_OF[t] + n) * ROWS, ROWS), :] = jnp.where(
                in_head(t, h), query[:, t * 128 : t * 128 + 128], 0.0
            ).astype(BF16)
    own_rows = pl.ds(pl.multiple_of(core * HALF, HALF), HALF)
    other_rows = pl.ds(pl.multiple_of(HALF - core * HALF, HALF), HALF)
    local["wg"].wait()
    gate = jax.nn.sigmoid(dot(nsend[own_rows, :], wg[...]))
    for copy in pair_copies[PAIR_CHUNKS // 2 :]:
        copy.wait()
    lax.fori_loop(first, groups, pair_bias, 0)
    local["mask"].wait()
    masking = jnp.where(mask[pl.ds(c, 1), :] == 1, 0.0, -1000000000.0).astype(F32)
    local["wk"].wait()
    local["wv"].wait()

    for block in range(2):
        own_block = jnp.logical_and(own_keys, slot == block)

        @pl.when(jnp.logical_not(own_block))
        def _():
            remote(
                nsend, kbuf.at[block], send2.at[0], recv2.at[block], targets[1]
            ).wait_recv()

    keys_in = kbuf[...].reshape(KEYS, D)
    key = dot(keys_in, wk[...]).astype(BF16)
    value = dot(keys_in, wv[...]).astype(BF16)

    scores = [None] * HEADS
    for t in range(TILES):
        heads = heads_of(t)
        terms = lax.dot_general(
            qmask[pl.ds(FIRST_OF[t] * ROWS, len(heads) * ROWS), :],
            key[:, t * 128 : t * 128 + 128],
            NT,
            preferred_element_type=F32,
        )
        for n, h in enumerate(heads):
            term = terms[n * ROWS : (n + 1) * ROWS]
            scores[h] = term if scores[h] is None else scores[h] + term
    scores = [
        score * (1.0 / HEAD**0.5) + bias[pl.ds(h * ROWS, ROWS), :] + masking
        for h, score in enumerate(scores)
    ]
    tops = [jnp.max(score, axis=-1, keepdims=True) for score in scores]
    expos = [jnp.exp(score - top).astype(BF16) for score, top in zip(scores, tops)]
    for t in range(TILES):
        heads = heads_of(t)
        v_tile = value[:, t * 128 : t * 128 + 128]
        part = dot(
            jnp.concatenate([expos[h] for h in heads], axis=1),
            jnp.concatenate(
                [jnp.where(in_head(t, h), v_tile, 0.0).astype(BF16) for h in heads], axis=0
            ),
        )
        psend[:, pl.ds(t * 128, 128)] = part.astype(BF16)
    stats = dot(jnp.concatenate(expos, axis=1), ones[...])
    lanes = lane_ids()
    for h, top in enumerate(tops):
        stats = jnp.where((lanes == h) | (lanes == h + 16) | (lanes == h + 32), top, stats)
    psend[:, pl.ds(D, 128)] = coded(stats)

    send3 = remote(psend.at[other_rows, :], sbuf, sems3.at[0], sems3.at[1], sibling)
    send3.start()
    own_act = act_ref[own_rows, :]
    for name in ("wo", "wsw", "wdn", "cproj"):
        local[name].wait()
    mine = psend[own_rows, :]
    send3.wait_recv()
    theirs = sbuf[...]
    top_a, total_a = decoded(mine[:, D:])
    top_b, total_b = decoded(theirs[:, D:])
    top = jnp.maximum(top_a, top_b)
    scale_a, scale_b = jnp.exp(top_a - top), jnp.exp(top_b - top)
    total = scale_a * total_a + scale_b * total_b
    wide_a, wide_b = spread([scale_a, scale_b], expand[...])
    merged = wide_a * mine[:, :D].astype(F32) + wide_b * theirs[:, :D].astype(F32)
    top = jnp.where(lanes < HEADS, top, 0.0)
    total = jnp.where(lanes < HEADS, total, 0.0)
    stats = (
        top
        + pltpu.roll(top, 16, 1)
        + pltpu.roll(top, 32, 1)
        + pltpu.roll(total, 48, 1)
        + pltpu.roll(total, 64, 1)
    )
    zsend[:, pl.ds(0, D)] = merged.astype(BF16)
    zsend[:, pl.ds(D, 128)] = coded(stats)
    sends4 = {}
    for k in (2, 1, 3):
        sends4[k] = remote(zsend, zbuf.at[k], send4.at[k], recv4.at[k], around[k])
        sends4[k].start()
    parts, tops, totals = [merged], [top], [total]
    for k in (1, 3, 2):
        sends4[k].wait_recv()
        got = zbuf[k]
        parts.append(got[:, :D].astype(F32))
        other_top, other_total = decoded(got[:, D:])
        tops.append(other_top)
        totals.append(other_total)
    peak = tops[0]
    for top in tops[1:]:
        peak = jnp.maximum(peak, top)
    scales = [jnp.exp(top - peak) for top in tops]
    whole = scales[0] * totals[0]
    for scale, total in zip(scales[1:], totals[1:]):
        whole += scale * total
    wides = spread([scale / whole for scale in scales], expand[...])
    attended = wides[0] * parts[0]
    for wide, part in zip(wides[1:], parts[1:]):
        attended += wide * part

    gated = (gate * attended).astype(BF16)
    updated = (own_act + dot(gated, wo[...])).astype(BF16).astype(F32)
    updated_norm = norm(updated).astype(BF16)
    finished = updated
    width = 512
    down = jnp.zeros((HALF, D), F32)
    for step in range(FF_TOK // width):
        g = dot(updated_norm, wsw[:, step * width : (step + 1) * width])
        u = dot(updated_norm, wsw[:, FF_TOK + step * width : FF_TOK + (step + 1) * width])
        mid = (jax.nn.silu(g) * u).astype(BF16)
        down += dot(mid, wdn[step * width : (step + 1) * width, :])
    finished = (updated + down).astype(BF16).astype(F32)
    cond = dot(norm(finished).astype(BF16), cproj[...])
    obuf[own_rows, pl.ds(0, D)] = finished.astype(BF16)
    obuf[own_rows, pl.ds(D, 128)] = cond.astype(BF16)

    send5 = remote(
        obuf.at[own_rows, :], done_hbm.at[own_rows, :], sems3.at[2], sems3.at[3], sibling
    )
    send5.start()
    store_own = pltpu.make_async_copy(
        obuf.at[own_rows, :], done_hbm.at[own_rows, :], lsem.at[15]
    )
    store_own.start()
    remote(
        obuf.at[other_rows, :], done_hbm.at[other_rows, :], sems3.at[2], sems3.at[3], sibling
    ).wait_recv()

    for copy in sends1.values():
        copy.wait_send()

    @pl.when(sender)
    def _():
        for copy in sends2[1:]:
            copy.wait_send()

    @pl.when(jnp.logical_and(sender, turn != 0))
    def _():
        sends2[0].wait_send()

    send3.wait_send()
    for copy in sends4.values():
        copy.wait_send()
    send5.wait_send()
    store_own.wait()


def atoms_kernel(
    done_hbm,
    atom_hbm,
    ids_hbm,
    asw_hbm,
    adn_hbm,
    out_tok,
    out_atom,
    done,
    atom,
    ids,
    asw,
    adn,
    result,
    sems,
):
    pairs = ((ids_hbm, ids), (done_hbm, done), (atom_hbm, atom), (asw_hbm, asw), (adn_hbm, adn))
    copies = [
        pltpu.make_async_copy(src, dst, sems.at[n]) for n, (src, dst) in enumerate(pairs)
    ]
    for copy in copies:
        copy.start()
    row_start = lax.axis_index("row") * ROWS
    copies[0].wait()
    token_iota = lax.broadcasted_iota(jnp.int32, (ROWS, 128), 0) + row_start
    onehot_t = jnp.transpose(jnp.where(token_iota == ids[...], 1.0, 0.0)).astype(BF16)
    copies[1].wait()
    store_tok = pltpu.make_async_copy(done.at[:, pl.ds(0, D)], out_tok, sems.at[5])
    store_tok.start()
    for copy in copies[2:]:
        copy.wait()
    resid = atom[...].astype(F32) + dot(onehot_t, done[:, pl.ds(D, 128)])
    both = dot(norm(resid).astype(BF16), asw[...])
    mid = (jax.nn.silu(both[:, :FF_ATOM]) * both[:, FF_ATOM:]).astype(BF16)
    result[...] = (resid + dot(mid, adn[...])).astype(BF16)
    store_atom = pltpu.make_async_copy(result, out_atom, sems.at[6])
    store_atom.start()
    store_tok.wait()
    store_atom.wait()


def local_step(
    atom_single,
    atom_token,
    token_single,
    token_mask,
    pair,
    atom_proj,
    pool_gain,
    w_query,
    w_key,
    w_value,
    w_gate,
    w_out,
    pair_proj,
    w_swiglu,
    w_down,
    cond_proj,
    atom_swiglu,
    atom_down,
):
    ids = atom_token.reshape(1, 128)
    args = (
        atom_single,
        ids,
        token_single,
        token_mask.reshape(COLS, KEYS),
        pair,
        atom_proj,
        pool_gain.reshape(D // 128, 128),
        w_query,
        w_key,
        w_value,
        w_gate,
        w_out,
        pair_proj.T,
        w_swiglu,
        w_down,
        cond_proj,
    )
    vmem = pltpu.VMEM
    dma = pltpu.SemaphoreType.DMA
    scratch = [
        vmem((144, 128), BF16),
        vmem((1, 128), jnp.int32),
        vmem((ROWS, D), BF16),
        vmem((COLS, KEYS), jnp.int32),
        vmem((ROWS, KEYS, 128), BF16),
        vmem((128, D), BF16),
        vmem((D // 128, 128), F32),
        vmem((D, D), BF16),
        vmem((D, D), BF16),
        vmem((D, D), BF16),
        vmem((D, D), BF16),
        vmem((D, D), BF16),
        vmem((HEADS, 128), F32),
        vmem((D, 2 * FF_TOK), BF16),
        vmem((FF_TOK, D), BF16),
        vmem((D, 128), BF16),
        vmem((HEADS * ROWS + ROWS, KEYS), F32),
        vmem((2 * HEADS, 128), BF16),
        vmem((128, D), BF16),
        vmem((COLS, 144, 128), BF16),
        vmem((HEADS * KEYS, 128), BF16),
        vmem((ROWS, D), F32),
        vmem((PLACES * ROWS, 128), BF16),
        vmem((ROWS, D), BF16),
        vmem((2, ROWS, D), BF16),
        vmem((ROWS, WIDE), BF16),
        vmem((HALF, WIDE), BF16),
        vmem((HALF, WIDE), BF16),
        vmem((4, HALF, WIDE), BF16),
        vmem((ROWS, WIDE), BF16),
        dma((17,)),
        dma((PAIR_CHUNKS,)),
        dma((COLS,)),
        dma((COLS,)),
        pltpu.SemaphoreType.REGULAR((2,)),
        dma((4,)),
        dma((2,)),
        dma((4,)),
        dma((4,)),
        dma((4,)),
    ]
    anywhere = pl.BlockSpec(memory_space=pl.ANY)
    limit = 60 * 1024 * 1024
    done = pl.pallas_call(
        kernel,
        out_shape=jax.ShapeDtypeStruct((ROWS, WIDE), BF16),
        in_specs=[anywhere] * len(args),
        out_specs=anywhere,
        scratch_shapes=scratch,
        compiler_params=pltpu.CompilerParams(
            collective_id=0, has_side_effects=True, vmem_limit_bytes=limit
        ),
        name="step",
    )(*args)
    return pl.pallas_call(
        atoms_kernel,
        out_shape=(
            jax.ShapeDtypeStruct((ROWS, D), BF16),
            jax.ShapeDtypeStruct((128, 128), BF16),
        ),
        in_specs=[anywhere] * 5,
        out_specs=(anywhere, anywhere),
        scratch_shapes=[
            vmem((ROWS, WIDE), BF16),
            vmem((128, 128), BF16),
            vmem((1, 128), jnp.int32),
            vmem((128, 2 * FF_ATOM), BF16),
            vmem((FF_ATOM, 128), BF16),
            vmem((128, 128), BF16),
            dma((7,)),
        ],
        compiler_params=pltpu.CompilerParams(vmem_limit_bytes=limit),
        name="atoms",
    )(done, atom_single, ids, atom_swiglu, atom_down)


def solution(mesh):
    split = P(("row", "col"), None)
    placed = (
        split,
        P(("row", "col")),
        P(),
        P(),
        P("row", "col", None),
    ) + (P(),) * 13
    return jax.shard_map(
        local_step,
        mesh=mesh,
        in_specs=placed,
        out_specs=(P("row", None), split),
        check_vma=False,
    )
```

```python
import jax
import jax.numpy as jnp
from jax import lax
from jax.experimental import pallas as pl
from jax.experimental.pallas import tpu as pltpu
from jax.sharding import PartitionSpec as P

MESH = pl.DeviceIdType.MESH
F32 = jnp.float32
BF16 = jnp.bfloat16

D = 768
HEADS = 16
HEAD = 48
FF_TOK = 1536
FF_ATOM = 256
ROWS = 64
KEYS = 128
COLS = 8
HALF = ROWS // 2
PAIR_STEP = 8
WIDE = D + 128
TILES = D // 128
PAIR_CHUNKS = 4

NT = (((1,), (1,)), ((), ()))


def norm(values):
    mean = jnp.mean(values, axis=-1, keepdims=True)
    centered = values - mean
    var = jnp.mean(centered * centered, axis=-1, keepdims=True)
    return centered * lax.rsqrt(var + 1e-05)


def row_mean(values):
    return jnp.mean(values, axis=-1, keepdims=True)


def norm_about(values, shift):
    moved = values - shift
    mean = row_mean(moved)
    var = jnp.maximum(row_mean(moved * moved) - mean * mean, 0.0)
    return (moved - mean) * lax.rsqrt(var + 1e-05)


def dot(a, b):
    return jnp.dot(a, b, preferred_element_type=F32)


def heads_of(tile):
    return [
        h for h in range(HEADS) if h * HEAD < (tile + 1) * 128 and (h + 1) * HEAD > tile * 128
    ]


FIRST_OF = [sum(len(heads_of(before)) for before in range(tile)) for tile in range(TILES)]
PLACES = FIRST_OF[-1] + len(heads_of(TILES - 1))


def lane_ids():
    return lax.broadcasted_iota(jnp.int32, (1, 128), 1)


def in_head(tile, h):
    lanes = lane_ids()
    return (lanes >= h * HEAD - tile * 128) & (lanes < (h + 1) * HEAD - tile * 128)


def coded(stats):
    lanes = lane_ids()
    piece0 = stats.astype(BF16).astype(F32)
    rest = stats - piece0
    piece1 = rest.astype(BF16).astype(F32)
    piece2 = (rest - piece1).astype(BF16).astype(F32)
    use0 = (lanes < 16) | ((lanes >= 48) & (lanes < 64))
    use1 = ((lanes >= 16) & (lanes < 32)) | (lanes >= 64)
    return jnp.where(use0, piece0, jnp.where(use1, piece1, piece2)).astype(BF16)


def decoded(line):
    line = line.astype(F32)
    top = line + pltpu.roll(line, 112, 1) + pltpu.roll(line, 96, 1)
    total = pltpu.roll(line, 80, 1) + pltpu.roll(line, 64, 1)
    return top, total


def spread(scales, expand):
    lanes = lane_ids()
    pieces = []
    for scale in scales:
        scale = jnp.where(lanes < HEADS, scale, 0.0)
        upper = scale.astype(BF16).astype(F32)
        pieces.append(upper + pltpu.roll(scale - upper, 16, 1))
    wide = dot(jnp.concatenate(pieces, axis=0).astype(BF16), expand)
    rows = scales[0].shape[0]
    return [wide[i * rows : (i + 1) * rows] for i in range(len(scales))]


def kernel(
    atom_hbm,
    ids_hbm,
    single_hbm,
    mask_hbm,
    pair_hbm,
    aproj_hbm,
    gain_hbm,
    wq_hbm,
    wk_hbm,
    wv_hbm,
    wg_hbm,
    wo_hbm,
    pproj_hbm,
    wsw_hbm,
    wdn_hbm,
    cproj_hbm,
    done_hbm,
    packed,
    ids,
    single,
    mask,
    pair,
    aproj,
    gain,
    wq,
    wk,
    wv,
    wg,
    wo,
    pproj,
    wsw,
    wdn,
    cproj,
    bias,
    projs,
    expand,
    abuf,
    ones,
    act_ref,
    qmask,
    nsend,
    kbuf,
    psend,
    sbuf,
    zsend,
    zbuf,
    obuf,
    lsem,
    psem,
    send1,
    recv1,
    relay,
    send2,
    recv2,
    sems3,
    send4,
    recv4,
):
    r = lax.axis_index("row")
    c = lax.axis_index("col")
    x, y = lax.div(r, 4), lax.rem(r, 4)
    z, core = lax.div(c, 2), lax.rem(c, 2)
    turn = lax.rem(z - x + 4, 4)

    home = lax.div(y, 2)
    sender = core == home
    targets = []
    for dx in range(4):
        tx, ty = lax.rem(x + dx, 4), lax.rem(y + dx + turn, 4)
        targets.append((tx * 4 + ty, lax.div(r, 2)))
    own_keys = jnp.logical_and(sender, turn == 0)

    sibling = (r, c + 1 - 2 * core)
    around = [None] + [(r, lax.rem(c + 2 * k, COLS)) for k in range(1, 4)]
    along_x = [(lax.rem(x + k, 4) * 4 + y, c) for k in range(1, 4)]
    along_y = [(x * 4 + lax.rem(y + k, 4), c) for k in range(1, 4)]

    barrier = pltpu.get_barrier_semaphore()
    for peer in around[1:] + [sibling] + along_x + along_y:
        pl.semaphore_signal(barrier, inc=1, device_id=peer, device_id_type=MESH)

    local = {}

    def fetch(name, index, src, dst):
        copy = pltpu.make_async_copy(src, dst, lsem.at[index])
        copy.start()
        local[name] = copy

    fetch("atom", 0, atom_hbm, packed.at[pl.ds(0, 128), :])
    fetch("ids", 1, ids_hbm, ids)
    fetch("aproj", 2, aproj_hbm, aproj)
    fetch("pproj", 3, pproj_hbm, pproj)
    pair_copies = []
    span = ROWS // PAIR_CHUNKS
    for chunk in range(PAIR_CHUNKS):
        part = pl.ds(chunk * span, span)
        copy = pltpu.make_async_copy(pair_hbm.at[part], pair.at[part], psem.at[chunk])
        copy.start()
        pair_copies.append(copy)
    fetch("single", 4, single_hbm.at[pl.ds(pl.multiple_of(r * ROWS, ROWS), ROWS), :], single)
    fetch("gain", 5, gain_hbm, gain)
    fetch("mask", 6, mask_hbm, mask)
    fetch("wq", 7, wq_hbm, wq)
    fetch("wk", 8, wk_hbm, wk)
    fetch("wv", 9, wv_hbm, wv)
    fetch("wg", 10, wg_hbm, wg)
    fetch("wo", 11, wo_hbm, wo)
    fetch("wsw", 12, wsw_hbm, wsw)
    fetch("wdn", 13, wdn_hbm, wdn)
    fetch("cproj", 14, cproj_hbm, cproj)

    local["ids"].wait()
    own_ids = (ids[...] - r * ROWS).astype(F32)
    packed[pl.ds(128, 16), :] = jnp.broadcast_to(own_ids, (16, 128)).astype(BF16)
    local["atom"].wait()
    pl.semaphore_wait(barrier, 10)

    def remote(src, dst, send, recv, device):
        return pltpu.make_async_remote_copy(
            src_ref=src,
            dst_ref=dst,
            send_sem=send,
            recv_sem=recv,
            device_id=device,
            device_id_type=MESH,
        )

    sends1 = {}
    for k in (2, 1, 3):
        sends1[2 * k] = remote(packed, abuf.at[2 * k], send1.at[2 * k], recv1.at[2 * k], around[k])
    sends1[1] = remote(packed, abuf.at[1], send1.at[1], recv1.at[1], sibling)
    for copy in sends1.values():
        copy.start()
    for peer in along_x:
        pl.semaphore_signal(relay.at[0], inc=1, device_id=peer, device_id_type=MESH)

    token_iota = lax.broadcasted_iota(jnp.int32, (ROWS, 128), 0).astype(F32)

    def pooled_of(atoms, id_row):
        hidden = jnp.maximum(dot(atoms, aproj[...]), 0.0).astype(BF16)
        onehot = jnp.where(token_iota == id_row, 1.0, 0.0).astype(BF16)
        return dot(onehot, hidden)

    local["pproj"].wait()
    proj_t = pproj[...]
    high = proj_t.astype(BF16)
    projs[pl.ds(0, 16), :] = high
    projs[pl.ds(16, 16), :] = (proj_t - high.astype(F32)).astype(BF16)
    lane = lax.broadcasted_iota(jnp.int32, (128, D), 1)
    line = lax.broadcasted_iota(jnp.int32, (128, D), 0)
    line = jnp.where(line >= HEADS, line - HEADS, line) * HEAD
    inside = jnp.logical_and(lane >= line, lane < line + HEAD)
    expand[...] = jnp.where(inside, 1.0, 0.0).astype(BF16)
    lane = lax.broadcasted_iota(jnp.int32, (KEYS, 128), 1)
    for h in range(HEADS):
        ones[pl.ds(h * KEYS, KEYS), :] = jnp.where(
            (lane == h + 48) | (lane == h + 64), 1.0, 0.0
        ).astype(BF16)

    def pair_bias(group, carry):
        tile = pair[pl.ds(group * PAIR_STEP, PAIR_STEP)]
        rows = norm(tile.astype(F32).reshape(PAIR_STEP * KEYS, 128)).astype(BF16)
        both = lax.dot_general(projs[...], rows, NT, preferred_element_type=F32)
        summed = both[:HEADS] + both[HEADS:]
        for i in range(PAIR_STEP):
            bias[pl.ds(group * PAIR_STEP + i, HEADS, stride=ROWS), :] = summed[
                :, i * KEYS : (i + 1) * KEYS
            ]
        return carry

    groups = ROWS // PAIR_STEP
    first = groups // 2
    for copy in pair_copies[: PAIR_CHUNKS // 2]:
        copy.wait()
    lax.fori_loop(0, first, pair_bias, 0)
    pl.semaphore_wait(relay.at[0], 3)
    for peer in around[1:]:
        pl.semaphore_signal(relay.at[1], inc=1, device_id=peer, device_id_type=MESH)

    local["single"].wait()
    local["gain"].wait()
    given = single[...].astype(F32)
    gains = jnp.concatenate([gain[t : t + 1, :] for t in range(D // 128)], axis=1)
    local["aproj"].wait()
    pooled = pooled_of(packed[pl.ds(0, 128), :], own_ids)
    def pooled_slot(index):
        return pooled_of(abuf[index, :128, :], abuf[index, 128:144, :].astype(F32)[:1, :])

    sends1[1].wait_recv()
    pooled += pooled_slot(1)
    for k in (1, 3, 2):
        sends1[2 * k].wait_recv()
        index = 2 * k + 1
        sends1[index] = remote(
            abuf.at[2 * k], abuf.at[index], send1.at[index], recv1.at[index], sibling
        )
        sends1[index].start()
        pooled += pooled_slot(2 * k)
    for k in (1, 3, 2):
        sends1[2 * k + 1].wait_recv()
        pooled += pooled_slot(2 * k + 1)

    act = (norm(pooled) * gains + given).astype(BF16).astype(F32)
    normed = norm_about(act, row_mean(given)).astype(BF16)
    nsend[...] = normed

    slot = lax.rem(r, 2)
    sends2 = [
        remote(nsend, kbuf.at[slot], send2.at[dx], recv2.at[slot], targets[dx])
        for dx in range(4)
    ]
    pl.semaphore_wait(relay.at[1], 3)

    @pl.when(sender)
    def _():
        for copy in (sends2[2], sends2[1], sends2[3]):
            copy.start()

    @pl.when(jnp.logical_and(sender, turn != 0))
    def _():
        sends2[0].start()

    @pl.when(own_keys)
    def _():
        kbuf[slot] = nsend[...]

    act_ref[...] = act
    local["wq"].wait()
    query = dot(normed, wq[...]).astype(BF16)
    for t in range(TILES):
        for n, h in enumerate(heads_of(t)):
            qmask[pl.ds((FIRST_OF[t] + n) * ROWS, ROWS), :] = jnp.where(
                in_head(t, h), query[:, t * 128 : t * 128 + 128], 0.0
            ).astype(BF16)
    own_rows = pl.ds(pl.multiple_of(core * HALF, HALF), HALF)
    other_rows = pl.ds(pl.multiple_of(HALF - core * HALF, HALF), HALF)
    local["wg"].wait()
    gate = jax.nn.sigmoid(dot(nsend[own_rows, :], wg[...]))
    for copy in pair_copies[PAIR_CHUNKS // 2 :]:
        copy.wait()
    lax.fori_loop(first, groups, pair_bias, 0)
    local["mask"].wait()
    masking = jnp.where(mask[pl.ds(c, 1), :] == 1, 0.0, -1000000000.0).astype(F32)
    local["wk"].wait()
    local["wv"].wait()

    for block in range(2):
        own_block = jnp.logical_and(own_keys, slot == block)

        @pl.when(jnp.logical_not(own_block))
        def _():
            remote(
                nsend, kbuf.at[block], send2.at[0], recv2.at[block], targets[1]
            ).wait_recv()

    keys_in = kbuf[...].reshape(KEYS, D)
    key = dot(keys_in, wk[...]).astype(BF16)
    value = dot(keys_in, wv[...]).astype(BF16)

    scores = [None] * HEADS
    for t in range(TILES):
        heads = heads_of(t)
        terms = lax.dot_general(
            qmask[pl.ds(FIRST_OF[t] * ROWS, len(heads) * ROWS), :],
            key[:, t * 128 : t * 128 + 128],
            NT,
            preferred_element_type=F32,
        )
        for n, h in enumerate(heads):
            term = terms[n * ROWS : (n + 1) * ROWS]
            scores[h] = term if scores[h] is None else scores[h] + term
    scores = [
        score * (1.0 / HEAD**0.5) + bias[pl.ds(h * ROWS, ROWS), :] + masking
        for h, score in enumerate(scores)
    ]
    tops = [jnp.max(score, axis=-1, keepdims=True) for score in scores]
    expos = [jnp.exp(score - top).astype(BF16) for score, top in zip(scores, tops)]
    for t in range(TILES):
        heads = heads_of(t)
        v_tile = value[:, t * 128 : t * 128 + 128]
        part = dot(
            jnp.concatenate([expos[h] for h in heads], axis=1),
            jnp.concatenate(
                [jnp.where(in_head(t, h), v_tile, 0.0).astype(BF16) for h in heads], axis=0
            ),
        )
        psend[:, pl.ds(t * 128, 128)] = part.astype(BF16)
    stats = dot(jnp.concatenate(expos, axis=1), ones[...])
    lanes = lane_ids()
    for h, top in enumerate(tops):
        stats = jnp.where((lanes == h) | (lanes == h + 16) | (lanes == h + 32), top, stats)
    psend[:, pl.ds(D, 128)] = coded(stats)

    send3 = remote(psend.at[other_rows, :], sbuf, sems3.at[0], sems3.at[1], sibling)
    send3.start()
    own_act = act_ref[own_rows, :]
    own_mean = row_mean(own_act)
    for name in ("wo", "wsw", "wdn", "cproj"):
        local[name].wait()
    mine = psend[own_rows, :]
    send3.wait_recv()
    theirs = sbuf[...]
    top_a, total_a = decoded(mine[:, D:])
    top_b, total_b = decoded(theirs[:, D:])
    top = jnp.maximum(top_a, top_b)
    scale_a, scale_b = jnp.exp(top_a - top), jnp.exp(top_b - top)
    total = scale_a * total_a + scale_b * total_b
    wide_a, wide_b = spread([scale_a, scale_b], expand[...])
    merged = wide_a * mine[:, :D].astype(F32) + wide_b * theirs[:, :D].astype(F32)
    top = jnp.where(lanes < HEADS, top, 0.0)
    total = jnp.where(lanes < HEADS, total, 0.0)
    stats = (
        top
        + pltpu.roll(top, 16, 1)
        + pltpu.roll(top, 32, 1)
        + pltpu.roll(total, 48, 1)
        + pltpu.roll(total, 64, 1)
    )
    zsend[:, pl.ds(0, D)] = merged.astype(BF16)
    zsend[:, pl.ds(D, 128)] = coded(stats)
    sends4 = {}
    for k in (2, 1, 3):
        sends4[k] = remote(zsend, zbuf.at[k], send4.at[k], recv4.at[k], around[k])
        sends4[k].start()
    parts, tops, totals = [merged], [top], [total]
    for k in (1, 3, 2):
        sends4[k].wait_recv()
        got = zbuf[k]
        parts.append(got[:, :D].astype(F32))
        other_top, other_total = decoded(got[:, D:])
        tops.append(other_top)
        totals.append(other_total)
    peak = tops[0]
    for top in tops[1:]:
        peak = jnp.maximum(peak, top)
    scales = [jnp.exp(top - peak) for top in tops]
    whole = scales[0] * totals[0]
    for scale, total in zip(scales[1:], totals[1:]):
        whole += scale * total
    wides = spread([scale / whole for scale in scales], expand[...])
    attended = wides[0] * parts[0]
    for wide, part in zip(wides[1:], parts[1:]):
        attended += wide * part

    gated = (gate * attended).astype(BF16)
    updated = (own_act + dot(gated, wo[...])).astype(BF16).astype(F32)
    updated_norm = norm_about(updated, own_mean).astype(BF16)
    updated_mean = row_mean(updated)
    finished = updated
    width = 512
    down = jnp.zeros((HALF, D), F32)
    for step in range(FF_TOK // width):
        g = dot(updated_norm, wsw[:, step * width : (step + 1) * width])
        u = dot(updated_norm, wsw[:, FF_TOK + step * width : FF_TOK + (step + 1) * width])
        mid = (jax.nn.silu(g) * u).astype(BF16)
        down += dot(mid, wdn[step * width : (step + 1) * width, :])
    finished = (updated + down).astype(BF16).astype(F32)
    cond = dot(norm_about(finished, updated_mean).astype(BF16), cproj[...])
    obuf[own_rows, pl.ds(0, D)] = finished.astype(BF16)
    obuf[own_rows, pl.ds(D, 128)] = cond.astype(BF16)

    send5 = remote(
        obuf.at[own_rows, :], done_hbm.at[own_rows, :], sems3.at[2], sems3.at[3], sibling
    )
    send5.start()
    store_own = pltpu.make_async_copy(
        obuf.at[own_rows, :], done_hbm.at[own_rows, :], lsem.at[15]
    )
    store_own.start()
    remote(
        obuf.at[other_rows, :], done_hbm.at[other_rows, :], sems3.at[2], sems3.at[3], sibling
    ).wait_recv()

    for copy in sends1.values():
        copy.wait_send()

    @pl.when(sender)
    def _():
        for copy in sends2[1:]:
            copy.wait_send()

    @pl.when(jnp.logical_and(sender, turn != 0))
    def _():
        sends2[0].wait_send()

    send3.wait_send()
    for copy in sends4.values():
        copy.wait_send()
    send5.wait_send()
    store_own.wait()


def atoms_kernel(
    done_hbm,
    atom_hbm,
    ids_hbm,
    asw_hbm,
    adn_hbm,
    out_tok,
    out_atom,
    done,
    atom,
    ids,
    asw,
    adn,
    result,
    sems,
):
    pairs = ((ids_hbm, ids), (done_hbm, done), (atom_hbm, atom), (asw_hbm, asw), (adn_hbm, adn))
    copies = [
        pltpu.make_async_copy(src, dst, sems.at[n]) for n, (src, dst) in enumerate(pairs)
    ]
    for copy in copies:
        copy.start()
    row_start = lax.axis_index("row") * ROWS
    copies[0].wait()
    token_iota = lax.broadcasted_iota(jnp.int32, (ROWS, 128), 0) + row_start
    onehot_t = jnp.transpose(jnp.where(token_iota == ids[...], 1.0, 0.0)).astype(BF16)
    copies[1].wait()
    store_tok = pltpu.make_async_copy(done.at[:, pl.ds(0, D)], out_tok, sems.at[5])
    store_tok.start()
    for copy in copies[2:]:
        copy.wait()
    atoms = atom[...].astype(F32)
    resid = atoms + dot(onehot_t, done[:, pl.ds(D, 128)])
    both = dot(norm_about(resid, row_mean(atoms)).astype(BF16), asw[...])
    mid = (jax.nn.silu(both[:, :FF_ATOM]) * both[:, FF_ATOM:]).astype(BF16)
    result[...] = (resid + dot(mid, adn[...])).astype(BF16)
    store_atom = pltpu.make_async_copy(result, out_atom, sems.at[6])
    store_atom.start()
    store_tok.wait()
    store_atom.wait()


def local_step(
    atom_single,
    atom_token,
    token_single,
    token_mask,
    pair,
    atom_proj,
    pool_gain,
    w_query,
    w_key,
    w_value,
    w_gate,
    w_out,
    pair_proj,
    w_swiglu,
    w_down,
    cond_proj,
    atom_swiglu,
    atom_down,
):
    ids = atom_token.reshape(1, 128)
    args = (
        atom_single,
        ids,
        token_single,
        token_mask.reshape(COLS, KEYS),
        pair,
        atom_proj,
        pool_gain.reshape(D // 128, 128),
        w_query,
        w_key,
        w_value,
        w_gate,
        w_out,
        pair_proj.T,
        w_swiglu,
        w_down,
        cond_proj,
    )
    vmem = pltpu.VMEM
    dma = pltpu.SemaphoreType.DMA
    scratch = [
        vmem((144, 128), BF16),
        vmem((1, 128), jnp.int32),
        vmem((ROWS, D), BF16),
        vmem((COLS, KEYS), jnp.int32),
        vmem((ROWS, KEYS, 128), BF16),
        vmem((128, D), BF16),
        vmem((D // 128, 128), F32),
        vmem((D, D), BF16),
        vmem((D, D), BF16),
        vmem((D, D), BF16),
        vmem((D, D), BF16),
        vmem((D, D), BF16),
        vmem((HEADS, 128), F32),
        vmem((D, 2 * FF_TOK), BF16),
        vmem((FF_TOK, D), BF16),
        vmem((D, 128), BF16),
        vmem((HEADS * ROWS + ROWS, KEYS), F32),
        vmem((2 * HEADS, 128), BF16),
        vmem((128, D), BF16),
        vmem((COLS, 144, 128), BF16),
        vmem((HEADS * KEYS, 128), BF16),
        vmem((ROWS, D), F32),
        vmem((PLACES * ROWS, 128), BF16),
        vmem((ROWS, D), BF16),
        vmem((2, ROWS, D), BF16),
        vmem((ROWS, WIDE), BF16),
        vmem((HALF, WIDE), BF16),
        vmem((HALF, WIDE), BF16),
        vmem((4, HALF, WIDE), BF16),
        vmem((ROWS, WIDE), BF16),
        dma((17,)),
        dma((PAIR_CHUNKS,)),
        dma((COLS,)),
        dma((COLS,)),
        pltpu.SemaphoreType.REGULAR((2,)),
        dma((4,)),
        dma((2,)),
        dma((4,)),
        dma((4,)),
        dma((4,)),
    ]
    anywhere = pl.BlockSpec(memory_space=pl.ANY)
    limit = 60 * 1024 * 1024
    done = pl.pallas_call(
        kernel,
        out_shape=jax.ShapeDtypeStruct((ROWS, WIDE), BF16),
        in_specs=[anywhere] * len(args),
        out_specs=anywhere,
        scratch_shapes=scratch,
        compiler_params=pltpu.CompilerParams(
            collective_id=0, has_side_effects=True, vmem_limit_bytes=limit
        ),
        name="step",
    )(*args)
    return pl.pallas_call(
        atoms_kernel,
        out_shape=(
            jax.ShapeDtypeStruct((ROWS, D), BF16),
            jax.ShapeDtypeStruct((128, 128), BF16),
        ),
        in_specs=[anywhere] * 5,
        out_specs=(anywhere, anywhere),
        scratch_shapes=[
            vmem((ROWS, WIDE), BF16),
            vmem((128, 128), BF16),
            vmem((1, 128), jnp.int32),
            vmem((128, 2 * FF_ATOM), BF16),
            vmem((FF_ATOM, 128), BF16),
            vmem((128, 128), BF16),
            dma((7,)),
        ],
        compiler_params=pltpu.CompilerParams(vmem_limit_bytes=limit),
        name="atoms",
    )(done, atom_single, ids, atom_swiglu, atom_down)


def solution(mesh):
    split = P(("row", "col"), None)
    placed = (
        split,
        P(("row", "col")),
        P(),
        P(),
        P("row", "col", None),
    ) + (P(),) * 13
    return jax.shard_map(
        local_step,
        mesh=mesh,
        in_specs=placed,
        out_specs=(P("row", None), split),
        check_vma=False,
    )
```

```python
import jax
import jax.numpy as jnp
from jax import lax
from jax.experimental import pallas as pl
from jax.experimental.pallas import tpu as pltpu
from jax.sharding import PartitionSpec as P

MESH = pl.DeviceIdType.MESH
F32 = jnp.float32
BF16 = jnp.bfloat16

D = 768
HEADS = 16
HEAD = 48
FF_TOK = 1536
FF_ATOM = 256
ROWS = 64
KEYS = 128
COLS = 8
HALF = ROWS // 2
PAIR_STEP = 8
WIDE = D + 128
TILES = D // 128
PAIR_CHUNKS = 4

NT = (((1,), (1,)), ((), ()))


def norm(values):
    mean = jnp.mean(values, axis=-1, keepdims=True)
    centered = values - mean
    var = jnp.mean(centered * centered, axis=-1, keepdims=True)
    return centered * lax.rsqrt(var + 1e-05)


def row_mean(values):
    return jnp.mean(values, axis=-1, keepdims=True)


def norm_about(values, shift):
    moved = values - shift
    mean = row_mean(moved)
    var = jnp.maximum(row_mean(moved * moved) - mean * mean, 0.0)
    return (moved - mean) * lax.rsqrt(var + 1e-05)


def dot(a, b):
    return jnp.dot(a, b, preferred_element_type=F32)


def heads_of(tile):
    return [
        h for h in range(HEADS) if h * HEAD < (tile + 1) * 128 and (h + 1) * HEAD > tile * 128
    ]


FIRST_OF = [sum(len(heads_of(before)) for before in range(tile)) for tile in range(TILES)]
PLACES = FIRST_OF[-1] + len(heads_of(TILES - 1))


def lane_ids():
    return lax.broadcasted_iota(jnp.int32, (1, 128), 1)


def in_head(tile, h):
    lanes = lane_ids()
    return (lanes >= h * HEAD - tile * 128) & (lanes < (h + 1) * HEAD - tile * 128)


def coded(stats):
    lanes = lane_ids()
    piece0 = stats.astype(BF16).astype(F32)
    rest = stats - piece0
    piece1 = rest.astype(BF16).astype(F32)
    piece2 = (rest - piece1).astype(BF16).astype(F32)
    use0 = (lanes < 16) | ((lanes >= 48) & (lanes < 64))
    use1 = ((lanes >= 16) & (lanes < 32)) | (lanes >= 64)
    return jnp.where(use0, piece0, jnp.where(use1, piece1, piece2)).astype(BF16)


def decoded(line):
    line = line.astype(F32)
    top = line + pltpu.roll(line, 112, 1) + pltpu.roll(line, 96, 1)
    total = pltpu.roll(line, 80, 1) + pltpu.roll(line, 64, 1)
    return top, total


def spread(scales, expand):
    lanes = lane_ids()
    pieces = []
    for scale in scales:
        scale = jnp.where(lanes < HEADS, scale, 0.0)
        upper = scale.astype(BF16).astype(F32)
        pieces.append(upper + pltpu.roll(scale - upper, 16, 1))
    wide = dot(jnp.concatenate(pieces, axis=0).astype(BF16), expand)
    rows = scales[0].shape[0]
    return [wide[i * rows : (i + 1) * rows] for i in range(len(scales))]


def kernel(
    atom_hbm,
    ids_hbm,
    single_hbm,
    mask_hbm,
    pair_hbm,
    aproj_hbm,
    gain_hbm,
    wq_hbm,
    wk_hbm,
    wv_hbm,
    wg_hbm,
    wo_hbm,
    pproj_hbm,
    wsw_hbm,
    wdn_hbm,
    cproj_hbm,
    tok_hbm,
    cond_hbm,
    packed,
    ids,
    single,
    mask,
    pair,
    aproj,
    gain,
    wq,
    wk,
    wv,
    wg,
    wo,
    pproj,
    wsw,
    wdn,
    cproj,
    bias,
    projs,
    expand,
    abuf,
    ones,
    act_ref,
    qmask,
    nsend,
    kbuf,
    psend,
    sbuf,
    zsend,
    zbuf,
    obuf,
    cbuf,
    lsem,
    psem,
    send1,
    recv1,
    relay,
    send2,
    recv2,
    sems3,
    send4,
    recv4,
):
    r = lax.axis_index("row")
    c = lax.axis_index("col")
    x, y = lax.div(r, 4), lax.rem(r, 4)
    z, core = lax.div(c, 2), lax.rem(c, 2)
    turn = lax.rem(z - x + 4, 4)

    home = lax.div(y, 2)
    sender = core == home
    targets = []
    for dx in range(4):
        tx, ty = lax.rem(x + dx, 4), lax.rem(y + dx + turn, 4)
        targets.append((tx * 4 + ty, lax.div(r, 2)))
    own_keys = jnp.logical_and(sender, turn == 0)

    sibling = (r, c + 1 - 2 * core)
    around = [None] + [(r, lax.rem(c + 2 * k, COLS)) for k in range(1, 4)]
    along_x = [(lax.rem(x + k, 4) * 4 + y, c) for k in range(1, 4)]
    along_y = [(x * 4 + lax.rem(y + k, 4), c) for k in range(1, 4)]

    barrier = pltpu.get_barrier_semaphore()
    for peer in around[1:] + [sibling] + along_x + along_y:
        pl.semaphore_signal(barrier, inc=1, device_id=peer, device_id_type=MESH)

    local = {}

    def fetch(name, index, src, dst):
        copy = pltpu.make_async_copy(src, dst, lsem.at[index])
        copy.start()
        local[name] = copy

    fetch("atom", 0, atom_hbm, packed.at[pl.ds(0, 128), :])
    fetch("ids", 1, ids_hbm, ids)
    fetch("aproj", 2, aproj_hbm, aproj)
    fetch("pproj", 3, pproj_hbm, pproj)
    pair_copies = []
    span = ROWS // PAIR_CHUNKS
    for chunk in range(PAIR_CHUNKS):
        part = pl.ds(chunk * span, span)
        copy = pltpu.make_async_copy(pair_hbm.at[part], pair.at[part], psem.at[chunk])
        copy.start()
        pair_copies.append(copy)
    fetch("single", 4, single_hbm.at[pl.ds(pl.multiple_of(r * ROWS, ROWS), ROWS), :], single)
    fetch("gain", 5, gain_hbm, gain)
    fetch("mask", 6, mask_hbm, mask)
    fetch("wq", 7, wq_hbm, wq)
    fetch("wk", 8, wk_hbm, wk)
    fetch("wv", 9, wv_hbm, wv)
    fetch("wg", 10, wg_hbm, wg)
    fetch("wo", 11, wo_hbm, wo)
    fetch("wsw", 12, wsw_hbm, wsw)
    fetch("wdn", 13, wdn_hbm, wdn)
    fetch("cproj", 14, cproj_hbm, cproj)

    local["ids"].wait()
    own_ids = (ids[...] - r * ROWS).astype(F32)
    packed[pl.ds(128, 16), :] = jnp.broadcast_to(own_ids, (16, 128)).astype(BF16)
    local["atom"].wait()
    pl.semaphore_wait(barrier, 10)

    def remote(src, dst, send, recv, device):
        return pltpu.make_async_remote_copy(
            src_ref=src,
            dst_ref=dst,
            send_sem=send,
            recv_sem=recv,
            device_id=device,
            device_id_type=MESH,
        )

    sends1 = {}
    for k in (2, 1, 3):
        sends1[2 * k] = remote(packed, abuf.at[2 * k], send1.at[2 * k], recv1.at[2 * k], around[k])
    sends1[1] = remote(packed, abuf.at[1], send1.at[1], recv1.at[1], sibling)
    for copy in sends1.values():
        copy.start()
    for peer in along_x:
        pl.semaphore_signal(relay.at[0], inc=1, device_id=peer, device_id_type=MESH)

    token_iota = lax.broadcasted_iota(jnp.int32, (ROWS, 128), 0).astype(F32)

    def pooled_of(atoms, id_row):
        hidden = jnp.maximum(dot(atoms, aproj[...]), 0.0).astype(BF16)
        onehot = jnp.where(token_iota == id_row, 1.0, 0.0).astype(BF16)
        return dot(onehot, hidden)

    local["pproj"].wait()
    proj_t = pproj[...]
    high = proj_t.astype(BF16)
    projs[pl.ds(0, 16), :] = high
    projs[pl.ds(16, 16), :] = (proj_t - high.astype(F32)).astype(BF16)
    lane = lax.broadcasted_iota(jnp.int32, (128, D), 1)
    line = lax.broadcasted_iota(jnp.int32, (128, D), 0)
    line = jnp.where(line >= HEADS, line - HEADS, line) * HEAD
    inside = jnp.logical_and(lane >= line, lane < line + HEAD)
    expand[...] = jnp.where(inside, 1.0, 0.0).astype(BF16)
    lane = lax.broadcasted_iota(jnp.int32, (KEYS, 128), 1)
    for h in range(HEADS):
        ones[pl.ds(h * KEYS, KEYS), :] = jnp.where(
            (lane == h + 48) | (lane == h + 64), 1.0, 0.0
        ).astype(BF16)

    def pair_bias(group, carry):
        tile = pair[pl.ds(group * PAIR_STEP, PAIR_STEP)]
        rows = norm(tile.astype(F32).reshape(PAIR_STEP * KEYS, 128)).astype(BF16)
        both = lax.dot_general(projs[...], rows, NT, preferred_element_type=F32)
        summed = both[:HEADS] + both[HEADS:]
        for i in range(PAIR_STEP):
            bias[pl.ds(group * PAIR_STEP + i, HEADS, stride=ROWS), :] = summed[
                :, i * KEYS : (i + 1) * KEYS
            ]
        return carry

    groups = ROWS // PAIR_STEP
    first = groups // 2
    for copy in pair_copies[: PAIR_CHUNKS // 2]:
        copy.wait()
    lax.fori_loop(0, first, pair_bias, 0)
    pl.semaphore_wait(relay.at[0], 3)
    for peer in around[1:]:
        pl.semaphore_signal(relay.at[1], inc=1, device_id=peer, device_id_type=MESH)

    local["single"].wait()
    local["gain"].wait()
    given = single[...].astype(F32)
    gains = jnp.concatenate([gain[t : t + 1, :] for t in range(D // 128)], axis=1)
    local["aproj"].wait()
    pooled = pooled_of(packed[pl.ds(0, 128), :], own_ids)
    def pooled_slot(index):
        return pooled_of(abuf[index, :128, :], abuf[index, 128:144, :].astype(F32)[:1, :])

    sends1[1].wait_recv()
    pooled += pooled_slot(1)
    for k in (1, 3, 2):
        sends1[2 * k].wait_recv()
        index = 2 * k + 1
        sends1[index] = remote(
            abuf.at[2 * k], abuf.at[index], send1.at[index], recv1.at[index], sibling
        )
        sends1[index].start()
        pooled += pooled_slot(2 * k)
    for k in (1, 3, 2):
        sends1[2 * k + 1].wait_recv()
        pooled += pooled_slot(2 * k + 1)

    act = (norm(pooled) * gains + given).astype(BF16).astype(F32)
    normed = norm_about(act, row_mean(given)).astype(BF16)
    nsend[...] = normed

    slot = lax.rem(r, 2)
    sends2 = [
        remote(nsend, kbuf.at[slot], send2.at[dx], recv2.at[slot], targets[dx])
        for dx in range(4)
    ]
    pl.semaphore_wait(relay.at[1], 3)

    @pl.when(sender)
    def _():
        for copy in (sends2[2], sends2[1], sends2[3]):
            copy.start()

    @pl.when(jnp.logical_and(sender, turn != 0))
    def _():
        sends2[0].start()

    @pl.when(own_keys)
    def _():
        kbuf[slot] = nsend[...]

    act_ref[...] = act
    local["wq"].wait()
    query = dot(normed, wq[...]).astype(BF16)
    for t in range(TILES):
        for n, h in enumerate(heads_of(t)):
            qmask[pl.ds((FIRST_OF[t] + n) * ROWS, ROWS), :] = jnp.where(
                in_head(t, h), query[:, t * 128 : t * 128 + 128], 0.0
            ).astype(BF16)
    own_rows = pl.ds(pl.multiple_of(core * HALF, HALF), HALF)
    other_rows = pl.ds(pl.multiple_of(HALF - core * HALF, HALF), HALF)
    local["wg"].wait()
    gate = jax.nn.sigmoid(dot(nsend[own_rows, :], wg[...]))
    for copy in pair_copies[PAIR_CHUNKS // 2 :]:
        copy.wait()
    lax.fori_loop(first, groups, pair_bias, 0)
    local["mask"].wait()
    masking = jnp.where(mask[pl.ds(c, 1), :] == 1, 0.0, -1000000000.0).astype(F32)
    local["wk"].wait()
    local["wv"].wait()

    for block in range(2):
        own_block = jnp.logical_and(own_keys, slot == block)

        @pl.when(jnp.logical_not(own_block))
        def _():
            remote(
                nsend, kbuf.at[block], send2.at[0], recv2.at[block], targets[1]
            ).wait_recv()

    keys_in = kbuf[...].reshape(KEYS, D)
    key = dot(keys_in, wk[...]).astype(BF16)
    value = dot(keys_in, wv[...]).astype(BF16)

    scores = [None] * HEADS
    for t in range(TILES):
        heads = heads_of(t)
        terms = lax.dot_general(
            qmask[pl.ds(FIRST_OF[t] * ROWS, len(heads) * ROWS), :],
            key[:, t * 128 : t * 128 + 128],
            NT,
            preferred_element_type=F32,
        )
        for n, h in enumerate(heads):
            term = terms[n * ROWS : (n + 1) * ROWS]
            scores[h] = term if scores[h] is None else scores[h] + term
    scores = [
        score * (1.0 / HEAD**0.5) + bias[pl.ds(h * ROWS, ROWS), :] + masking
        for h, score in enumerate(scores)
    ]
    tops = [jnp.max(score, axis=-1, keepdims=True) for score in scores]
    expos = [jnp.exp(score - top).astype(BF16) for score, top in zip(scores, tops)]
    for t in range(TILES):
        heads = heads_of(t)
        v_tile = value[:, t * 128 : t * 128 + 128]
        part = dot(
            jnp.concatenate([expos[h] for h in heads], axis=1),
            jnp.concatenate(
                [jnp.where(in_head(t, h), v_tile, 0.0).astype(BF16) for h in heads], axis=0
            ),
        )
        psend[:, pl.ds(t * 128, 128)] = part.astype(BF16)
    stats = dot(jnp.concatenate(expos, axis=1), ones[...])
    lanes = lane_ids()
    for h, top in enumerate(tops):
        stats = jnp.where((lanes == h) | (lanes == h + 16) | (lanes == h + 32), top, stats)
    psend[:, pl.ds(D, 128)] = coded(stats)

    send3 = remote(psend.at[other_rows, :], sbuf, sems3.at[0], sems3.at[1], sibling)
    send3.start()
    own_act = act_ref[own_rows, :]
    own_mean = row_mean(own_act)
    for name in ("wo", "wsw", "wdn", "cproj"):
        local[name].wait()
    mine = psend[own_rows, :]
    send3.wait_recv()
    theirs = sbuf[...]
    top_a, total_a = decoded(mine[:, D:])
    top_b, total_b = decoded(theirs[:, D:])
    top = jnp.maximum(top_a, top_b)
    scale_a, scale_b = jnp.exp(top_a - top), jnp.exp(top_b - top)
    total = scale_a * total_a + scale_b * total_b
    wide_a, wide_b = spread([scale_a, scale_b], expand[...])
    merged = wide_a * mine[:, :D].astype(F32) + wide_b * theirs[:, :D].astype(F32)
    top = jnp.where(lanes < HEADS, top, 0.0)
    total = jnp.where(lanes < HEADS, total, 0.0)
    stats = (
        top
        + pltpu.roll(top, 16, 1)
        + pltpu.roll(top, 32, 1)
        + pltpu.roll(total, 48, 1)
        + pltpu.roll(total, 64, 1)
    )
    zsend[:, pl.ds(0, D)] = merged.astype(BF16)
    zsend[:, pl.ds(D, 128)] = coded(stats)
    sends4 = {}
    for k in (2, 1, 3):
        sends4[k] = remote(zsend, zbuf.at[k], send4.at[k], recv4.at[k], around[k])
        sends4[k].start()
    parts, tops, totals = [merged], [top], [total]
    for k in (1, 3, 2):
        sends4[k].wait_recv()
        got = zbuf[k]
        parts.append(got[:, :D].astype(F32))
        other_top, other_total = decoded(got[:, D:])
        tops.append(other_top)
        totals.append(other_total)
    peak = tops[0]
    for top in tops[1:]:
        peak = jnp.maximum(peak, top)
    scales = [jnp.exp(top - peak) for top in tops]
    whole = scales[0] * totals[0]
    for scale, total in zip(scales[1:], totals[1:]):
        whole += scale * total
    wides = spread([scale / whole for scale in scales], expand[...])
    attended = wides[0] * parts[0]
    for wide, part in zip(wides[1:], parts[1:]):
        attended += wide * part

    gated = (gate * attended).astype(BF16)
    updated = (own_act + dot(gated, wo[...])).astype(BF16).astype(F32)
    updated_norm = norm_about(updated, own_mean).astype(BF16)
    updated_mean = row_mean(updated)
    finished = updated
    width = 512
    down = jnp.zeros((HALF, D), F32)
    for step in range(FF_TOK // width):
        g = dot(updated_norm, wsw[:, step * width : (step + 1) * width])
        u = dot(updated_norm, wsw[:, FF_TOK + step * width : FF_TOK + (step + 1) * width])
        mid = (jax.nn.silu(g) * u).astype(BF16)
        down += dot(mid, wdn[step * width : (step + 1) * width, :])
    finished = (updated + down).astype(BF16).astype(F32)
    obuf[own_rows, :] = finished.astype(BF16)

    send5 = remote(
        obuf.at[own_rows, :], tok_hbm.at[own_rows, :], sems3.at[2], sems3.at[3], sibling
    )
    send5.start()
    cond = dot(norm_about(finished, updated_mean).astype(BF16), cproj[...])
    cbuf[own_rows, :] = cond.astype(BF16)
    send6 = remote(
        cbuf.at[own_rows, :], cond_hbm.at[own_rows, :], sems3.at[4], sems3.at[5], sibling
    )
    send6.start()
    store_tok = pltpu.make_async_copy(
        obuf.at[own_rows, :], tok_hbm.at[own_rows, :], lsem.at[15]
    )
    store_tok.start()
    store_cond = pltpu.make_async_copy(
        cbuf.at[own_rows, :], cond_hbm.at[own_rows, :], lsem.at[16]
    )
    store_cond.start()
    remote(
        obuf.at[other_rows, :], tok_hbm.at[other_rows, :], sems3.at[2], sems3.at[3], sibling
    ).wait_recv()
    remote(
        cbuf.at[other_rows, :], cond_hbm.at[other_rows, :], sems3.at[4], sems3.at[5], sibling
    ).wait_recv()

    for copy in sends1.values():
        copy.wait_send()

    @pl.when(sender)
    def _():
        for copy in sends2[1:]:
            copy.wait_send()

    @pl.when(jnp.logical_and(sender, turn != 0))
    def _():
        sends2[0].wait_send()

    send3.wait_send()
    for copy in sends4.values():
        copy.wait_send()
    send5.wait_send()
    send6.wait_send()
    store_tok.wait()
    store_cond.wait()


def atoms_kernel(
    tok_hbm,
    cond_hbm,
    atom_hbm,
    ids_hbm,
    asw_hbm,
    adn_hbm,
    out_tok,
    out_atom,
    tok,
    cond,
    atom,
    ids,
    asw,
    adn,
    result,
    sems,
):
    pairs = (
        (ids_hbm, ids),
        (tok_hbm, tok),
        (cond_hbm, cond),
        (atom_hbm, atom),
        (asw_hbm, asw),
        (adn_hbm, adn),
    )
    copies = [
        pltpu.make_async_copy(src, dst, sems.at[n]) for n, (src, dst) in enumerate(pairs)
    ]
    for copy in copies:
        copy.start()
    row_start = lax.axis_index("row") * ROWS
    copies[0].wait()
    token_iota = lax.broadcasted_iota(jnp.int32, (ROWS, 128), 0) + row_start
    onehot_t = jnp.transpose(jnp.where(token_iota == ids[...], 1.0, 0.0)).astype(BF16)
    copies[1].wait()
    store_tok = pltpu.make_async_copy(tok, out_tok, sems.at[6])
    store_tok.start()
    for copy in copies[2:]:
        copy.wait()
    atoms = atom[...].astype(F32)
    resid = atoms + dot(onehot_t, cond[...])
    both = dot(norm_about(resid, row_mean(atoms)).astype(BF16), asw[...])
    mid = (jax.nn.silu(both[:, :FF_ATOM]) * both[:, FF_ATOM:]).astype(BF16)
    result[...] = (resid + dot(mid, adn[...])).astype(BF16)
    store_atom = pltpu.make_async_copy(result, out_atom, sems.at[7])
    store_atom.start()
    store_tok.wait()
    store_atom.wait()


def local_step(
    atom_single,
    atom_token,
    token_single,
    token_mask,
    pair,
    atom_proj,
    pool_gain,
    w_query,
    w_key,
    w_value,
    w_gate,
    w_out,
    pair_proj,
    w_swiglu,
    w_down,
    cond_proj,
    atom_swiglu,
    atom_down,
):
    ids = atom_token.reshape(1, 128)
    args = (
        atom_single,
        ids,
        token_single,
        token_mask.reshape(COLS, KEYS),
        pair,
        atom_proj,
        pool_gain.reshape(D // 128, 128),
        w_query,
        w_key,
        w_value,
        w_gate,
        w_out,
        pair_proj.T,
        w_swiglu,
        w_down,
        cond_proj,
    )
    vmem = pltpu.VMEM
    dma = pltpu.SemaphoreType.DMA
    scratch = [
        vmem((144, 128), BF16),
        vmem((1, 128), jnp.int32),
        vmem((ROWS, D), BF16),
        vmem((COLS, KEYS), jnp.int32),
        vmem((ROWS, KEYS, 128), BF16),
        vmem((128, D), BF16),
        vmem((D // 128, 128), F32),
        vmem((D, D), BF16),
        vmem((D, D), BF16),
        vmem((D, D), BF16),
        vmem((D, D), BF16),
        vmem((D, D), BF16),
        vmem((HEADS, 128), F32),
        vmem((D, 2 * FF_TOK), BF16),
        vmem((FF_TOK, D), BF16),
        vmem((D, 128), BF16),
        vmem((HEADS * ROWS + ROWS, KEYS), F32),
        vmem((2 * HEADS, 128), BF16),
        vmem((128, D), BF16),
        vmem((COLS, 144, 128), BF16),
        vmem((HEADS * KEYS, 128), BF16),
        vmem((ROWS, D), F32),
        vmem((PLACES * ROWS, 128), BF16),
        vmem((ROWS, D), BF16),
        vmem((2, ROWS, D), BF16),
        vmem((ROWS, WIDE), BF16),
        vmem((HALF, WIDE), BF16),
        vmem((HALF, WIDE), BF16),
        vmem((4, HALF, WIDE), BF16),
        vmem((ROWS, D), BF16),
        vmem((ROWS, 128), BF16),
        dma((17,)),
        dma((PAIR_CHUNKS,)),
        dma((COLS,)),
        dma((COLS,)),
        pltpu.SemaphoreType.REGULAR((2,)),
        dma((4,)),
        dma((2,)),
        dma((6,)),
        dma((4,)),
        dma((4,)),
    ]
    anywhere = pl.BlockSpec(memory_space=pl.ANY)
    limit = 60 * 1024 * 1024
    tok, cond = pl.pallas_call(
        kernel,
        out_shape=(
            jax.ShapeDtypeStruct((ROWS, D), BF16),
            jax.ShapeDtypeStruct((ROWS, 128), BF16),
        ),
        in_specs=[anywhere] * len(args),
        out_specs=(anywhere, anywhere),
        scratch_shapes=scratch,
        compiler_params=pltpu.CompilerParams(
            collective_id=0, has_side_effects=True, vmem_limit_bytes=limit
        ),
        name="step",
    )(*args)
    return pl.pallas_call(
        atoms_kernel,
        out_shape=(
            jax.ShapeDtypeStruct((ROWS, D), BF16),
            jax.ShapeDtypeStruct((128, 128), BF16),
        ),
        in_specs=[anywhere] * 6,
        out_specs=(anywhere, anywhere),
        scratch_shapes=[
            vmem((ROWS, D), BF16),
            vmem((ROWS, 128), BF16),
            vmem((128, 128), BF16),
            vmem((1, 128), jnp.int32),
            vmem((128, 2 * FF_ATOM), BF16),
            vmem((FF_ATOM, 128), BF16),
            vmem((128, 128), BF16),
            dma((8,)),
        ],
        compiler_params=pltpu.CompilerParams(vmem_limit_bytes=limit),
        name="atoms",
    )(tok, cond, atom_single, ids, atom_swiglu, atom_down)


def solution(mesh):
    split = P(("row", "col"), None)
    placed = (
        split,
        P(("row", "col")),
        P(),
        P(),
        P("row", "col", None),
    ) + (P(),) * 13
    return jax.shard_map(
        local_step,
        mesh=mesh,
        in_specs=placed,
        out_specs=(P("row", None), split),
        check_vma=False,
    )
```
